32 devices in a mesh: wide: 4 (over y, core), narrow: 8 (over z, x).
Axes of the slice: x: 2, y: 2, z: 4, core: 2. Of those that a mesh axis runs over, the one named last changes fastest.
Arguments:
- tokens_in: bfloat16 [4096, 2048], P(('wide', 'narrow')), may hold values from -9 to 9
- query_weight: bfloat16 [2048, 2048], P(None, 'narrow'), may hold values from -0.125 to 0.125
- key_weight: bfloat16 [2048, 2048], P(None, 'narrow'), may hold values from -0.125 to 0.125
- value_weight: bfloat16 [2048, 2048], P(None, 'narrow'), may hold values from -0.125 to 0.125
- gate_weight: bfloat16 [2048, 2048], P(None, 'narrow'), may hold values from -0.125 to 0.125
- mixer_weight: bfloat16 [2048, 2048], P('narrow'), may hold values from -0.125 to 0.125
- first_weight: bfloat16 [2048, 5632], P(None, 'narrow'), may hold values from -0.125 to 0.125
- second_weight: bfloat16 [2048, 5632], P(None, 'narrow'), may hold values from -0.125 to 0.125
- down_weight: bfloat16 [5632, 2048], P('narrow'), may hold values from -0.078125 to 0.078125
- doc_lengths: int32 [4, 4], P('wide'), may hold values from 1 to 512, 1024 in all within a row
- head_decay: float32 [16], P('narrow'), may hold values from 0.00024414062 to 0.04
- out_grad: bfloat16 [4096, 2048], P(('wide', 'narrow')), may hold values from -6 to 6
Outputs:
- output: bfloat16 [4096, 2048], P(('wide', 'narrow'))
- input_grad: float32 [4096, 2048], P(('wide', 'narrow'))
- query_grad: float32 [2048, 2048], P(None, 'narrow')
- key_grad: float32 [2048, 2048], P(None, 'narrow')
- value_grad: float32 [2048, 2048], P(None, 'narrow')
- gate_grad: float32 [2048, 2048], P(None, 'narrow')
- mixer_grad: float32 [2048, 2048], P('narrow')
- first_grad: float32 [2048, 5632], P(None, 'narrow')
- second_grad: float32 [2048, 5632], P(None, 'narrow')
- down_grad: float32 [5632, 2048], P('narrow')
- stream_rms: float32 [3], replicated
The draws below stay inside these ranges and needn't reach their ends.
All inputs are finite; a program needn't handle non-finite values.
Results may differ from the reference program's by a relative error of at most 0.014.
Values may be sent and summed in bfloat16 or wider, within the bound.
No kernel may reach another device: no remote copies, remote signals or barrier semaphores. Data moves between devices by JAX's collectives and lax.ppermute only.
A program may use at most 256 MiB of HBM per device.

```python
import math
import jax
import jax.numpy as jnp
import numpy as np
from jax import lax

D = 2048
HEADS = 16
HEAD_DIM = 128
FF = 5632
NDOC = 4
LEN = 1024
ROWS = 4
TOKENS = 4096


def draw_tokens_in(key, part):
    places = jnp.arange(TOKENS, dtype=jnp.float32) / TOKENS
    base = jnp.clip(jax.random.normal(key, (TOKENS, D), jnp.float32), -5.0, 5.0)
    scale = 0.6 + 1.2 * places
    return (base * scale[:, None]).astype(jnp.bfloat16)


def block_scale(stream_key, shape, shards, smallest, top_value):
    def one(position, blocks):
        steps = jax.random.uniform(jax.random.fold_in(jax.random.fold_in(stream_key, 6), position), (blocks,), jnp.float32, smallest / len(shards), top_value / len(shards))
        return jnp.repeat(jnp.exp(steps), shape[position] // blocks).reshape((-1,) + (1,) * (len(shape) - position - 1))

    gain = one(*shards[0])
    for cut in shards[1:]:
        gain = gain * one(*cut)
    return gain


def length_profile(count, total, reach, slope):
    loads = [(1 << 20) // math.isqrt(rank ** slope) + 1 for rank in range(2, count + 1)]
    surplus, given = total - reach - (count - 1), [1] * (count - 1)
    while surplus > 0:
        movable = [i for i in range(count - 1) if given[i] < reach]
        pool, budget = sum([loads[i] for i in movable]), surplus
        for i in movable:
            extra = min(reach - given[i], max(1, budget * loads[i] // pool), surplus)
            given[i] = given[i] + extra
            surplus = surplus - extra
    return np.array([reach] + given)


def ragged_sizes(key, count, total, most, slope):
    if count == 2:
        one = jax.random.randint(key, (), max(1, total - most), min(most, total - 1) + 1)
        return jnp.stack([one, total - one])
    tallies = jnp.asarray(length_profile(count, total, most, slope), jnp.int32)
    pairs = (count - 1) // 2
    donor, sink = tallies[1:1 + 2 * pairs:2], tallies[2:2 + 2 * pairs:2]
    room = jnp.minimum(donor - 1, most - sink)
    passed = jax.random.randint(jax.random.fold_in(key, 1), (pairs,), 0, 1 << 20) % (room + 1)
    tallies = tallies.at[1:1 + 2 * pairs:2].set(donor - passed).at[2:2 + 2 * pairs:2].set(sink + passed)
    return tallies[jax.random.permutation(jax.random.fold_in(key, 2), count)]


def bell_draw(key, shape, width, most, shards=(), held_as=jnp.bfloat16):
    array = width * jax.random.normal(key, shape, jnp.float32)
    if shards:
        array = array * block_scale(key, shape, shards, -0.22, 0.18)
    return jnp.clip(array, -most, most).astype(held_as)


def setup_inputs(seed: int = 0) -> dict:
    key_list = jax.random.split(jax.random.key(seed), 13)
    return {
        "tokens_in": draw_tokens_in(jax.random.fold_in(key_list[12], 71), 0),
        "query_weight": bell_draw(key_list[1], (D, D), D ** -0.5, 0.125, ((1, 8),)),
        "key_weight": bell_draw(key_list[2], (D, D), D ** -0.5, 0.125, ((1, 8),)),
        "value_weight": bell_draw(key_list[3], (D, D), D ** -0.5, 0.125, ((1, 8),)),
        "gate_weight": bell_draw(key_list[4], (D, D), D ** -0.5, 0.125, ((1, 8),)),
        "mixer_weight": bell_draw(key_list[5], (D, D), D ** -0.5, 0.125, ((0, 8),)),
        "first_weight": bell_draw(key_list[6], (D, FF), D ** -0.5, 0.125, ((1, 8),)),
        "second_weight": bell_draw(key_list[7], (D, FF), D ** -0.5, 0.125, ((1, 8),)),
        "down_weight": bell_draw(key_list[8], (FF, D), FF ** -0.5, 0.078125, ((0, 8),)),
        "doc_lengths": jax.vmap(lambda own: ragged_sizes(own, NDOC, LEN, LEN // 2, 1))(jax.random.split(key_list[9], ROWS)).reshape((ROWS, NDOC)).astype(jnp.int32),
        "head_decay": jnp.clip(jnp.exp(math.log(0.04) - 5.0988903 * jax.random.uniform(key_list[10], (HEADS,), jnp.float32) ** block_scale(key_list[10], (HEADS,), ((0, 8),), -0.2, 0.2)), 0.00024414062, 0.04),
        "out_grad": bell_draw(key_list[11], (TOKENS, D), 1.0, 6.0, ((0, 32),)),
    }


EPS = 1e-06
HIGH = lax.Precision.HIGHEST

@jax.custom_vjp
def low(v):
    return lax.optimization_barrier(v.astype(jnp.bfloat16)).astype(jnp.float32)

@jax.custom_vjp
def low_back(v):
    return v

def low_keep(v):
    return (low(v), None)

def low_pass(kept, grad):
    return (grad,)

def back_keep(v):
    return (v, None)

def back_low(kept, grad):
    return (low(grad),)
low.defvjp(low_keep, low_pass)
low_back.defvjp(back_keep, back_low)

def normalize(values):
    return values * lax.rsqrt(lax.optimization_barrier(jnp.mean(values * values, axis=-1, keepdims=True)) + EPS)

def segment_ids(lengths_row, total):
    ends = jnp.cumsum(lengths_row)[:-1]
    positions = jnp.arange(total, dtype=jnp.int32)
    return lax.optimization_barrier(jnp.sum((positions[:, None] >= ends[None, :]).astype(jnp.int32), axis=1)).astype(jnp.int32)

def block_factors(segment_block, earlier_segment, rate):
    size = segment_block.shape[0]
    places = jnp.arange(size, dtype=jnp.float32)
    offset = places[:, None] - places[None, :]
    same = jnp.logical_and(segment_block[:, None] == segment_block[None, :], offset >= 0)
    decay = jnp.exp(-rate[:, None, None] * jnp.maximum(offset, 0.0)[None]) * same[None].astype(jnp.float32)
    inner = jnp.exp(-rate[None, :] * (places[:, None] + 1.0)) * (segment_block == earlier_segment)[:, None].astype(jnp.float32)
    carried = jnp.exp(-rate[None, :] * (size - 1.0 - places)[:, None]) * (segment_block == segment_block[-1])[:, None].astype(jnp.float32)
    keeping = jnp.exp(-rate * size) * (segment_block[-1] == earlier_segment).astype(jnp.float32)
    return (decay, inner, carried, keeping)

def row_attention(query_act, key_act, value_act, segments, rate):
    size = min(512, LEN)
    count = LEN // size
    shaped = (count, size, HEADS, HEAD_DIM)
    segment_blocks = segments.reshape(count, size)
    earlier = jnp.concatenate([jnp.full((1,), -1, dtype=jnp.int32), segment_blocks[:-1, -1].astype(jnp.int32)])

    def advance(state, inputs):
        query_block, key_block, value_block, segment_block, earlier_segment = inputs
        decay, inner, carried, keeping = block_factors(segment_block, earlier_segment, rate)
        scores = low_back(jnp.einsum('ihd,jhd->hij', query_block, key_block, precision=HIGH))
        weights = low(scores * decay)
        intra = jnp.einsum('hij,jhd->ihd', weights, value_block, precision=HIGH)
        inter = inner[:, :, None] * jnp.einsum('ihd,hde->ihe', query_block, state, precision=HIGH)
        state_next = keeping[:, None, None] * state + jnp.einsum('jhd,jhe->hde', key_block * carried[:, :, None], value_block, precision=HIGH)
        return (state_next, intra + inter)
    start_state = jnp.zeros((HEADS, HEAD_DIM, HEAD_DIM), jnp.float32)
    final_state, outputs = lax.scan(jax.checkpoint(advance), start_state, (query_act.reshape(shaped), key_act.reshape(shaped), value_act.reshape(shaped), segment_blocks, earlier))
    return outputs.reshape(LEN, HEADS, HEAD_DIM)

def reference(tokens_in, query_weight, key_weight, value_weight, gate_weight, mixer_weight, first_weight, second_weight, down_weight, doc_lengths, head_decay, out_grad):
    segments = jax.vmap(lambda lengths_row: segment_ids(lengths_row, LEN))(doc_lengths)

    def forward(tokens, wquery, wkey, wvalue, wgate, wmixer, wfirst, wsecond, wdown):
        normed = low(normalize(tokens))
        query_act = low(jax.nn.silu(low_back(jnp.dot(normed, wquery, precision=HIGH))))
        key_act = low(jax.nn.silu(low_back(jnp.dot(normed, wkey, precision=HIGH))))
        value_act = low(low_back(jnp.dot(normed, wvalue, precision=HIGH)))
        gate_act = low_back(jnp.dot(normed, wgate, precision=HIGH))
        shaped = (ROWS, LEN, HEADS, HEAD_DIM)
        mixed = lax.map(lambda packed: row_attention(packed[0], packed[1], packed[2], packed[3], head_decay), (query_act.reshape(shaped), key_act.reshape(shaped), value_act.reshape(shaped), segments))
        mixed = low_back(mixed.reshape(TOKENS, D))
        scaled = low(normalize(mixed) * gate_act)
        attn = low_back(jnp.dot(scaled, wmixer, precision=HIGH))
        hidden = tokens + attn
        normed2 = low(normalize(hidden))
        first_act = low_back(jnp.dot(normed2, wfirst, precision=HIGH))
        second_act = low_back(jnp.dot(normed2, wsecond, precision=HIGH))
        product = low(first_act * second_act)
        ffn = low_back(jnp.dot(product, wdown, precision=HIGH))
        return (hidden + ffn, (attn, ffn))
    primals = tuple((a.astype(jnp.float32) for a in (tokens_in, query_weight, key_weight, value_weight, gate_weight, mixer_weight, first_weight, second_weight, down_weight)))
    result, pullback, extras = jax.vjp(forward, *primals, has_aux=True)
    grads = pullback(out_grad.astype(jnp.float32))
    valid = (segments < NDOC - 1).reshape(TOKENS).astype(jnp.float32)
    counted = jnp.sum(valid)
    tokens = primals[0]
    sums = jnp.stack([jnp.sum(valid * lax.optimization_barrier(jnp.sum(tokens * tokens, axis=1))), jnp.sum(valid * lax.optimization_barrier(jnp.sum(extras[0] * extras[0], axis=1))), jnp.sum(valid * lax.optimization_barrier(jnp.sum(extras[1] * extras[1], axis=1)))])
    stream_rms = jnp.sqrt(sums / (counted * D))
    return (result.astype(jnp.bfloat16), grads[0], grads[1], grads[2], grads[3], grads[4], grads[5], grads[6], grads[7], grads[8], stream_rms)
```

```python
import functools

import jax
import jax.numpy as jnp
import numpy as np
from jax import lax
from jax.experimental import pallas as pl
from jax.experimental.pallas import tpu as pltpu
from jax.sharding import PartitionSpec as P

D = 2048
HEAD_DIM = 128
NDOC = 4
EPS = 1e-06
BLOCK = 256
MIB = 1 << 20

F32 = jnp.float32
BF16 = jnp.bfloat16
NN = (((1,), (0,)), ((), ()))
NT = (((1,), (1,)), ((), ()))
TN = (((0,), (0,)), ((), ()))
VMEM = pl.BlockSpec(memory_space=pltpu.VMEM)
SMEM = pl.BlockSpec(memory_space=pltpu.SMEM)


def dot(a, b, dims=NN):
    return lax.dot_general(a, b, dims, preferred_element_type=F32)


def split(values):
    high = values.astype(BF16)
    return high, (values - high.astype(F32)).astype(BF16)


def normalize(values):
    return values * lax.rsqrt(jnp.mean(values * values, axis=-1, keepdims=True) + EPS)


def norm_grad(values, grad_in):
    inverse = lax.rsqrt(jnp.mean(values * values, axis=-1, keepdims=True) + EPS)
    normed = values * inverse
    return inverse * (grad_in - normed * jnp.mean(grad_in * normed, axis=-1, keepdims=True))


def ring_order(n):
    if n == 16:
        return [r * 4 + (c if r % 2 == 0 else 3 - c) for r in range(4) for c in range(4)]
    return list(range(0, n, 2)) + list(range(n - 1, 0, -2))


def distances(n):
    out = [0]
    for k in range(1, n // 2):
        out += [-k, k]
    return out + [n // 2]


def order_table(n):
    ring = ring_order(n)
    place = {device: i for i, device in enumerate(ring)}
    return np.array(
        [[ring[(place[me] + d) % n] for d in distances(n)] for me in range(n)], np.int32
    )


def onward(values, n):
    ring = ring_order(n)
    return lax.ppermute(values, "narrow", [(ring[i], ring[(i + 1) % n]) for i in range(n)])


def backward(values, n):
    ring = ring_order(n)
    return lax.ppermute(values, "narrow", [(ring[(i + 1) % n], ring[i]) for i in range(n)])


def ring_gather(own, n):
    left = right = own
    pieces = [own]
    for _ in range(n // 2 - 1):
        left, right = onward(left, n), backward(right, n)
        pieces += [left, right]
    half = own.shape[0] // 2
    return pieces + [onward(left[:half], n), backward(right[half:], n)]


def add16(a, b):
    return (a.astype(F32) + b.astype(F32)).astype(BF16)


def ring_scatter(parts, n):
    near = {d: parts[i] for i, d in enumerate(distances(n)[:-1])}
    half = parts[-1].shape[0]
    far = n // 2 - 1
    left, right = onward(parts[-2], n), backward(parts[-1], n)
    left = jnp.concatenate([add16(near[far][:half], left), near[far][half:]], 0)
    right = jnp.concatenate([near[-far][:half], add16(near[-far][half:], right)], 0)
    for k in range(far - 1, 0, -1):
        left, right = onward(left, n), backward(right, n)
        left, right = add16(near[k], left), add16(near[-k], right)
    left, right = onward(left, n), backward(right, n)
    return near[0].astype(F32) + left.astype(F32) + right.astype(F32)


def swap(values, axis, bit):
    size = lax.axis_size(axis)
    return lax.ppermute(values, axis, [(i, i ^ bit) for i in range(size)])


def butterfly(values, axis, first=1):
    bit = first
    while bit < lax.axis_size(axis):
        values = values + swap(values, axis, bit)
        bit *= 2
    return values


def wide_sum(send, keep):
    total = keep + swap(send, "wide", 1).astype(F32)
    bit = 2
    while bit < lax.axis_size("wide"):
        own = total.astype(BF16)
        total = own.astype(F32) + swap(own, "wide", bit).astype(F32)
        bit *= 2
    own = total.astype(BF16)
    return own, swap(own, "wide", 1)


def call(kernel, outs, in_specs, flops, limit, scratch=()):
    return pl.pallas_call(
        kernel,
        out_shape=[jax.ShapeDtypeStruct(s, d) for s, d in outs],
        in_specs=in_specs,
        out_specs=[VMEM] * len(outs),
        scratch_shapes=list(scratch),
        compiler_params=pltpu.CompilerParams(vmem_limit_bytes=limit),
        cost_estimate=pl.CostEstimate(
            flops=flops, bytes_accessed=2 * flops // 1000, transcendentals=0
        ),
    )


def part_shapes(n, rows):
    return [((rows, D), BF16)] * (n - 1) + [((rows // 2, D), BF16)] * 2


def store_part(parts, r, values):
    n = len(parts) - 1
    if r < n - 1:
        parts[r][...] = values
    else:
        half = values.shape[0] // 2
        parts[n - 1][...] = values[:half]
        parts[n][...] = values[half:]


def assemble(pieces, target, start_of):
    n = len(pieces) - 1
    rows = pieces[0].shape[0]
    half = rows // 2
    for r in range(n - 1):
        target[pl.ds(start_of(r), rows), :] = pieces[r][...]
    start = start_of(n - 1)
    target[pl.ds(start, half), :] = pieces[n - 1][...]
    target[pl.ds(start + half, half), :] = pieces[n][...]


def segment_of(positions, ends):
    return sum((positions >= e).astype(jnp.int32) for e in ends)


def row_ends(lengths):
    first = lengths[0, 0]
    second = first + lengths[0, 1]
    return (first, second, second + lengths[0, 2])


class Block:
    def __init__(self, b, ends):
        start = b * BLOCK
        rows = lax.broadcasted_iota(jnp.int32, (BLOCK, BLOCK), 0)
        columns = lax.broadcasted_iota(jnp.int32, (BLOCK, BLOCK), 1)
        seg_rows = segment_of(rows + start, ends)
        seg_columns = segment_of(columns + start, ends)
        self.mask = jnp.logical_and(seg_rows == seg_columns, rows >= columns)
        self.last = segment_of(start + BLOCK - 1, ends)
        self.earlier = segment_of(start - 1, ends) if b > 0 else -1
        wide_rows = lax.broadcasted_iota(jnp.int32, (BLOCK, HEAD_DIM), 0)
        segments = segment_of(wide_rows + start, ends)
        self.from_state = segments == self.earlier
        self.to_state = segments == self.last

    def decay(self, full):
        return jnp.where(self.mask, full, 0.0)

    def keeping(self, rate):
        factor = jnp.exp(jnp.full((HEAD_DIM, HEAD_DIM), -rate * BLOCK, F32))
        return jnp.where(self.last == self.earlier, factor, 0.0)


def full_decay(rate):
    rows = lax.broadcasted_iota(jnp.int32, (BLOCK, BLOCK), 0)
    columns = lax.broadcasted_iota(jnp.int32, (BLOCK, BLOCK), 1)
    return jnp.exp(-rate * jnp.maximum(rows - columns, 0).astype(F32))


def edge_factors(rate):
    rows = lax.broadcasted_iota(jnp.int32, (BLOCK, HEAD_DIM), 0).astype(F32)
    return jnp.exp(-rate * (rows + 1.0)), jnp.exp(-rate * (BLOCK - 1.0 - rows))


def silu16(values):
    return (values * jax.nn.sigmoid(values)).astype(BF16)


def silu_grad(before):
    sigmoid = jax.nn.sigmoid(before)
    return sigmoid * (1.0 + before * (1.0 - sigmoid))


def entry_kernel(n, heads, order, lengths, rates, *refs):
    pieces, refs = refs[: n + 1], refs[n + 1 :]
    weights, mixer, refs = refs[:4], refs[4], refs[5:]
    normed, proj, mixed, squares, states, refs = *refs[:5], refs[5:]
    parts, pre = refs[: n + 1], refs[n + 1]
    rows = pieces[0].shape[0]
    total = n * rows
    width = heads * HEAD_DIM
    assemble(pieces, normed, lambda r: pl.multiple_of(order[0, r] * rows, rows))
    for b in range(total // BLOCK):
        here = pl.ds(b * BLOCK, BLOCK)
        tokens = normed[here, :]
        for i, weight in enumerate(weights):
            proj[here, i * width : (i + 1) * width] = dot(tokens, weight[...])
    ends = row_ends(lengths)
    fulls = [full_decay(rates[h]) for h in range(heads)]
    edges = [edge_factors(rates[h]) for h in range(heads)]
    state = [jnp.zeros((HEAD_DIM, HEAD_DIM), F32) for _ in range(heads)]
    ones = jnp.ones((8, HEAD_DIM), BF16)
    for b in range(total // BLOCK):
        here = pl.ds(b * BLOCK, BLOCK)
        block = Block(b, ends)
        square = jnp.zeros((8, BLOCK), F32)
        for h in range(heads):
            at = [slice(i * width + h * HEAD_DIM, i * width + (h + 1) * HEAD_DIM) for i in range(4)]
            query, key = silu16(proj[here, at[0]]), silu16(proj[here, at[1]])
            value = proj[here, at[2]].astype(BF16)
            inner, carried = edges[h]
            inner = jnp.where(block.from_state, inner, 0.0)
            carried = jnp.where(block.to_state, carried, 0.0)
            states[b, h] = state[h]
            weight = (dot(query, key, NT) * block.decay(fulls[h])).astype(BF16)
            high, low = split(state[h])
            out = dot(weight, value) + inner * (dot(query, high) + dot(query, low))
            high, low = split(key.astype(F32) * carried)
            state[h] = block.keeping(rates[h]) * state[h] + (
                dot(high, value, TN) + dot(low, value, TN)
            )
            mixed[here, at[0]] = out
            pre[here, at[0]] = (out * proj[here, at[3]]).astype(BF16)
            high, low = split(out * out)
            square += dot(ones, high, NT) + dot(ones, low, NT)
        squares[:, here] = square[0:1]
    for r in range(0, n, 2):
        both = jnp.concatenate(
            [pre[pl.ds(pl.multiple_of(order[0, q] * rows, rows), rows), :] for q in (r, r + 1)], 0
        )
        result = dot(both, mixer[...]).astype(BF16)
        store_part(parts, r, result[:rows])
        store_part(parts, r + 1, result[rows:])


def column(row):
    return jnp.transpose(jnp.broadcast_to(row, (HEAD_DIM, row.shape[1])))


def exit_kernel(n, heads, order, lengths, rates, *refs):
    pieces, refs = refs[: n + 1], refs[n + 1 :]
    weights, mixer, refs = refs[:4], refs[4], refs[5:]
    proj, mixed, states, inverses, inners, refs = *refs[:5], refs[5:]
    resid, scaled, entry_g, refs = *refs[:3], refs[3:]
    parts, scaled_g = refs[: n + 1], refs[n + 1]
    rows = pieces[0].shape[0]
    total = n * rows
    width = heads * HEAD_DIM
    assemble(pieces, resid, lambda r: pl.multiple_of(order[0, r] * rows, rows))
    for b in range(total // BLOCK):
        here = pl.ds(b * BLOCK, BLOCK)
        scaled_g[here, :] = dot(resid[here, :], mixer[...], NT)
    ends = row_ends(lengths)
    fulls = [full_decay(rates[h]) for h in range(heads)]
    edges = [edge_factors(rates[h]) for h in range(heads)]
    later = [jnp.zeros((HEAD_DIM, HEAD_DIM), F32) for _ in range(heads)]
    for b in reversed(range(total // BLOCK)):
        here = pl.ds(b * BLOCK, BLOCK)
        block = Block(b, ends)
        inverse = column(inverses[:, here])
        mean = column(inners[:, here]) * (1.0 / D)
        for h in range(heads):
            at = [slice(i * width + h * HEAD_DIM, i * width + (h + 1) * HEAD_DIM) for i in range(4)]
            query_pre, key_pre = proj[here, at[0]], proj[here, at[1]]
            query, key = silu16(query_pre), silu16(key_pre)
            value = proj[here, at[2]].astype(BF16)
            gate = proj[here, at[3]]
            grad_s = scaled_g[here, at[0]]
            unit = mixed[here, at[0]] * inverse
            scaled[here, at[0]] = (unit * gate).astype(BF16)
            entry_g[here, at[3]] = (grad_s * unit).astype(BF16)
            grad = (inverse * (grad_s * gate - unit * mean)).astype(BF16)
            inner, carried = edges[h]
            inner = jnp.where(block.from_state, inner, 0.0)
            carried = jnp.where(block.to_state, carried, 0.0)
            decay = block.decay(fulls[h])
            weight = (dot(query, key, NT) * decay).astype(BF16)
            score = (dot(grad, value, NT) * decay).astype(BF16)
            high, low = split(states[b, h])
            query_g = dot(score, key) + inner * (dot(grad, high, NT) + dot(grad, low, NT))
            high, low = split(later[h])
            key_g = dot(score, query, TN) + carried * (dot(value, high, NT) + dot(value, low, NT))
            value_g = dot(weight, grad, TN) + carried * (dot(key, high) + dot(key, low))
            high, low = split(query.astype(F32) * inner)
            later[h] = (
                dot(high, grad, TN) + dot(low, grad, TN) + block.keeping(rates[h]) * later[h]
            )
            entry_g[here, at[0]] = (query_g * silu_grad(query_pre)).astype(BF16)
            entry_g[here, at[1]] = (key_g * silu_grad(key_pre)).astype(BF16)
            entry_g[here, at[2]] = value_g.astype(BF16)
    for r in range(0, n, 2):
        both = jnp.concatenate(
            [entry_g[pl.ds(pl.multiple_of(order[0, q] * rows, rows), rows), :] for q in (r, r + 1)],
            0,
        )
        result = sum(
            dot(both[:, i * width : (i + 1) * width], weight[...], NT)
            for i, weight in enumerate(weights)
        ).astype(BF16)
        store_part(parts, r, result[:rows])
        store_part(parts, r + 1, result[rows:])


def cotangent_kernel(n, *refs):
    pieces, down, grad, product_g = refs[: n + 1], *refs[n + 1 :]
    rows = pieces[0].shape[0]
    assemble(pieces, grad, lambda r: r * rows)
    for b in range(n * rows // BLOCK):
        here = pl.ds(b * BLOCK, BLOCK)
        product_g[here, :] = dot(grad[here, :], down[...], NT)


def hidden_kernel(n, *refs):
    pieces, refs = refs[: n + 1], refs[n + 1 :]
    first, second, product_g, refs = *refs[:3], refs[3:]
    normed, product, first_g, second_g, parts = *refs[:4], refs[4:]
    rows = pieces[0].shape[0]
    assemble(pieces, normed, lambda r: r * rows)
    for r in range(0, n, 2):
        here = pl.ds(r * rows, 2 * rows)
        tokens = normed[here, :]
        first_act, second_act = dot(tokens, first[...]), dot(tokens, second[...])
        product[here, :] = (first_act * second_act).astype(BF16)
        grad = product_g[here, :]
        one, two = (grad * second_act).astype(BF16), (grad * first_act).astype(BF16)
        first_g[here, :] = one
        second_g[here, :] = two
        result = (dot(one, first[...], NT) + dot(two, second[...], NT)).astype(BF16)
        store_part(parts, r, result[:rows])
        store_part(parts, r + 1, result[rows:])


def down_kernel(n, product, down, *parts):
    rows = parts[0].shape[0]
    for r in range(0, n, 2):
        result = dot(product[pl.ds(r * rows, 2 * rows), :], down[...]).astype(BF16)
        store_part(parts, r, result[:rows])
        store_part(parts, r + 1, result[rows:])


def local(
    tokens_in,
    query_weight,
    key_weight,
    value_weight,
    gate_weight,
    mixer_weight,
    first_weight,
    second_weight,
    down_weight,
    doc_lengths,
    head_decay,
    out_grad,
):
    n = lax.axis_size("narrow")
    rows = tokens_in.shape[0]
    total = rows * n
    heads = head_decay.shape[0]
    width = heads * HEAD_DIM
    units = first_weight.shape[1]
    me = lax.axis_index("narrow")
    core = lax.axis_index("wide") % 2
    start_row = me * rows
    order = lax.dynamic_slice(jnp.asarray(order_table(n)), (me, 0), (1, n))
    entry_weights = (query_weight, key_weight, value_weight, gate_weight)
    tokens_wide = tokens_in.astype(F32)
    rates = head_decay

    pieces = ring_gather(normalize(tokens_wide).astype(BF16), n)
    blocks = total // BLOCK
    normed, proj, mixed, squares, states, *parts = call(
        functools.partial(entry_kernel, n, heads),
        [
            ((total, D), BF16),
            ((total, 4 * width), F32),
            ((total, width), F32),
            ((1, total), F32),
            ((blocks, heads, HEAD_DIM, HEAD_DIM), F32),
        ]
        + part_shapes(n, rows),
        [SMEM] * 3 + [VMEM] * (n + 6),
        12 * total * D * width,
        50 * MIB,
        [pltpu.VMEM((total, width), BF16)],
    )(order, doc_lengths, rates, *pieces, *entry_weights, mixer_weight)

    grad_own, _ = lax.optimization_barrier((out_grad, pieces[-1]))
    grad_pieces = ring_gather(grad_own, n)
    grad_all, product_g = call(
        functools.partial(cotangent_kernel, n),
        [((total, D), BF16), ((total, units), F32)],
        [VMEM] * (n + 2),
        2 * total * D * units,
        32 * MIB,
    )(*grad_pieces, down_weight)

    inverses = lax.rsqrt(butterfly(squares, "narrow") / D + EPS)
    inverse_own = lax.dynamic_slice(inverses, (0, start_row), (1, rows)).reshape(rows, 1)
    attn_own = ring_scatter(parts, n) * inverse_own
    hidden_own = tokens_wide + attn_own

    pieces = ring_gather(normalize(hidden_own).astype(BF16), n)
    normed2, product, first_g, second_g, *parts = call(
        functools.partial(hidden_kernel, n),
        [((total, D), BF16)] + [((total, units), BF16)] * 3 + part_shapes(n, rows),
        [VMEM] * (n + 4),
        8 * total * D * units,
        56 * MIB,
    )(*pieces, first_weight, second_weight, product_g)
    normed2_g = ring_scatter(parts, n)
    hidden_g = out_grad.astype(F32) + norm_grad(hidden_own, normed2_g)
    resid_own = hidden_g.astype(BF16)
    inner_own = jnp.sum(resid_own.astype(F32) * attn_own, axis=1).reshape(1, rows)
    inners = butterfly(
        lax.dynamic_update_slice(jnp.zeros((1, total), F32), inner_own, (0, start_row)), "narrow"
    )
    resid_pieces = ring_gather(resid_own, n)

    product_late, _ = lax.optimization_barrier((product, resid_pieces[-1]))
    parts = call(
        functools.partial(down_kernel, n),
        part_shapes(n, rows),
        [VMEM] * 2,
        2 * total * D * units,
        24 * MIB,
    )(product_late, down_weight)
    ffn_own = ring_scatter(parts, n)
    output = (hidden_own + ffn_own).astype(BF16)
    counted = jnp.sum(doc_lengths[0, : NDOC - 1])
    valid = (start_row + jnp.arange(rows, dtype=jnp.int32) < counted).astype(F32)
    sums = jnp.stack(
        [
            jnp.sum(valid * jnp.sum(tokens_wide * tokens_wide, axis=1)),
            jnp.sum(valid * jnp.sum(attn_own * attn_own, axis=1)),
            jnp.sum(valid * jnp.sum(ffn_own * ffn_own, axis=1)),
            jnp.sum(valid),
        ]
    )
    sums = butterfly(butterfly(sums, "narrow"), "wide")
    stream_rms = jnp.sqrt(sums[:3] / (sums[3] * D))

    resid, scaled, entry_g, *parts = call(
        functools.partial(exit_kernel, n, heads),
        [((total, D), BF16), ((total, width), BF16), ((total, 4 * width), BF16)]
        + part_shapes(n, rows),
        [SMEM] * 3 + [VMEM] * (n + 11),
        12 * total * D * width,
        50 * MIB,
        [pltpu.VMEM((total, width), F32)],
    )(
        order,
        doc_lengths,
        rates,
        *resid_pieces,
        *entry_weights,
        mixer_weight,
        proj,
        mixed,
        states,
        inverses,
        inners,
    )
    normed_g = ring_scatter(parts, n)
    input_grad = hidden_g + norm_grad(tokens_wide, normed_g)

    def halves(values):
        return [
            lax.dynamic_slice_in_dim(values, place * (D // 2), D // 2, axis=1)
            for place in (1 - core, core)
        ]

    def by_rows(tokens, grads):
        send, keep = halves(tokens)
        own, other = wide_sum(dot(send, grads, TN).astype(BF16), dot(keep, grads, TN))
        return jnp.concatenate(
            [jnp.where(core == 0, own, other), jnp.where(core == 0, other, own)], 0
        )

    def by_columns(tokens, grads):
        send, keep = halves(grads)
        own, other = wide_sum(dot(tokens, send, TN).astype(BF16), dot(tokens, keep, TN))
        return jnp.concatenate(
            [jnp.where(core == 0, own, other), jnp.where(core == 0, other, own)], 1
        ).astype(F32)

    first_w = by_rows(normed2, first_g).astype(F32)
    second_w = by_rows(normed2, second_g).astype(F32)
    down_w = by_columns(product, grad_all)
    mixer_w = by_columns(scaled, resid)
    entry_w = by_rows(normed, entry_g)
    entry_ws = [entry_w[:, i * width : (i + 1) * width].astype(F32) for i in range(4)]
    return (output, input_grad, *entry_ws, mixer_w, first_w, second_w, down_w, stream_rms)


def solution(mesh):
    split_tokens = P(("wide", "narrow"), None)
    columns, rows = P(None, "narrow"), P("narrow", None)
    return jax.shard_map(
        local,
        mesh=mesh,
        in_specs=(split_tokens,)
        + (columns,) * 4
        + (rows, columns, columns, rows, P("wide", None), P("narrow"), split_tokens),
        out_specs=(split_tokens,) * 2 + (columns,) * 4 + (rows, columns, columns, rows, P()),
        check_vma=False,
    )
```

```python
import functools

import jax
import jax.numpy as jnp
import numpy as np
from jax import lax
from jax.experimental import pallas as pl
from jax.experimental.pallas import tpu as pltpu
from jax.sharding import PartitionSpec as P

D = 2048
HEAD_DIM = 128
NDOC = 4
EPS = 1e-06
BLOCK = 256
MIB = 1 << 20

F32 = jnp.float32
BF16 = jnp.bfloat16
NN = (((1,), (0,)), ((), ()))
NT = (((1,), (1,)), ((), ()))
TN = (((0,), (0,)), ((), ()))
VMEM = pl.BlockSpec(memory_space=pltpu.VMEM)
SMEM = pl.BlockSpec(memory_space=pltpu.SMEM)
ANY = pl.BlockSpec(memory_space=pl.ANY)


def dot(a, b, dims=NN):
    return lax.dot_general(a, b, dims, preferred_element_type=F32)


def split(values):
    high = values.astype(BF16)
    return high, (values - high.astype(F32)).astype(BF16)


def normalize(values):
    return values * lax.rsqrt(jnp.mean(values * values, axis=-1, keepdims=True) + EPS)


def norm_grad(values, grad_in):
    inverse = lax.rsqrt(jnp.mean(values * values, axis=-1, keepdims=True) + EPS)
    normed = values * inverse
    return inverse * (grad_in - normed * jnp.mean(grad_in * normed, axis=-1, keepdims=True))


def ring_order(n):
    if n == 16:
        return [r * 4 + (c if r % 2 == 0 else 3 - c) for r in range(4) for c in range(4)]
    return list(range(0, n, 2)) + list(range(n - 1, 0, -2))


def distances(n):
    out = [0]
    for k in range(1, n // 2):
        out += [-k, k]
    return out + [n // 2]


def order_table(n):
    ring = ring_order(n)
    place = {device: i for i, device in enumerate(ring)}
    return np.array(
        [[ring[(place[me] + d) % n] for d in distances(n)] for me in range(n)], np.int32
    )


def onward(values, n):
    ring = ring_order(n)
    return lax.ppermute(values, "narrow", [(ring[i], ring[(i + 1) % n]) for i in range(n)])


def backward(values, n):
    ring = ring_order(n)
    return lax.ppermute(values, "narrow", [(ring[(i + 1) % n], ring[i]) for i in range(n)])


def barrier(*values):
    return lax.optimization_barrier(values)


def add16(a, b):
    return (a.astype(F32) + b.astype(F32)).astype(BF16)


class Gather:
    def __init__(self, own, n):
        self.n, self.left_steps = n, n // 2
        self.left = self.right = own
        self.pieces = [own]

    def outgoing(self):
        if self.left_steps == 1:
            half = self.left.shape[0] // 2
            return self.left[:half], self.right[half:]
        return self.left, self.right

    def incoming(self, left, right):
        self.left_steps -= 1
        self.left, self.right = left, right
        self.pieces += [left, right]

    def step(self, count=1):
        for _ in range(count):
            left, right = self.outgoing()
            self.incoming(onward(left, self.n), backward(right, self.n))
        return self

    def finish(self):
        return self.step(self.left_steps).pieces


def merge_kernel(layout, *refs):
    outs, refs = refs[-2:], list(refs[:-2])
    at = 0
    for rows, half, offset in layout:
        if offset is None:
            for out in outs:
                out[at : at + rows] = refs.pop(0)[...]
        else:
            nears, parts, refs = refs[:2], refs[2:4], refs[4:]
            for i in range(2):
                low = half * i if half < rows else 0
                outs[i][at : at + rows] = nears[i][...]
                outs[i][at + low : at + low + half] = add16(
                    nears[i][low : low + half], parts[i][offset : offset + half]
                )
        at += rows


def join_one(low, near, part, out):
    rows = part.shape[0]
    out[...] = near[...]
    out[low : low + rows] = add16(near[low : low + rows], part[...])


class Scatter:
    def __init__(self, parts, n):
        self.n, self.left_steps = n, n // 2
        self.near = {d: parts[i] for i, d in enumerate(distances(n)[:-1])}
        self.left, self.right = parts[-2], parts[-1]
        self.received = None

    def operands(self):
        if self.received is None:
            return [self.left, self.right], (self.left.shape[0], 0, None)
        left, right, offset, half = self.received
        near = [self.near[self.left_steps], self.near[-self.left_steps]]
        return near + [left, right], (near[0].shape[0], half, offset)

    def take(self, left, right, offset, rows):
        self.left_steps -= 1
        if self.left_steps == 0:
            at = slice(offset, offset + rows)
            self.result = self.near[0].astype(F32) + left[at].astype(F32) + right[at].astype(F32)
        self.received = (left, right, offset, rows)

    def step(self, count=1):
        for _ in range(count):
            self.left_steps -= 1
            left, right = onward(self.left, self.n), backward(self.right, self.n)
            k = self.left_steps
            shape = self.near[k].shape
            if k == 0:
                self.result = self.near[0].astype(F32) + left.astype(F32) + right.astype(F32)
            elif shape == left.shape:
                self.left, self.right = add16(self.near[k], left), add16(self.near[-k], right)
            else:
                half = shape[0] // 2
                self.left, self.right = [
                    call(
                        functools.partial(join_one, low),
                        [(shape, BF16)],
                        [VMEM] * 2,
                        shape[0] * shape[1],
                        4 * MIB,
                    )(near, part)[0]
                    for low, near, part in ((0, self.near[k], left), (half, self.near[-k], right))
                ]
        return self

    def finish(self):
        return self.step(self.left_steps).result


class Together:
    def __init__(self, *scatters):
        self.scatters, self.n = scatters, scatters[0].n

    def outgoing(self):
        operands, self.layout = [], []
        for s in self.scatters:
            values, layout = s.operands()
            operands += values
            self.layout.append(layout)
        if len(self.layout) == 1 and self.layout[0][2] is None:
            return operands
        rows = sum(entry[0] for entry in self.layout)
        return call(
            functools.partial(merge_kernel, tuple(self.layout)),
            [((rows, D), BF16)] * 2,
            [VMEM] * len(operands),
            2 * rows * D,
            10 * MIB,
        )(*operands)

    def incoming(self, left, right):
        offset = 0
        for s, (rows, _, _) in zip(self.scatters, self.layout):
            s.take(left, right, offset, rows)
            offset += rows


def region(streams=(), swaps=(), work=None, inputs=()):
    out = [v for s in streams for v in s.outgoing()]
    count = len(out)
    values, inputs = lax.optimization_barrier((out + [s[0] for s in swaps], list(inputs)))
    moved = [
        onward(v, streams[0].n) if i % 2 == 0 else backward(v, streams[0].n)
        for i, v in enumerate(values[:count])
    ]
    moved += [swap(v, s[1], s[2]) for v, s in zip(values[count:], swaps)]
    results = work(*inputs) if work else ()
    moved, results = lax.optimization_barrier((moved, results))
    for i, s in enumerate(streams):
        s.incoming(*moved[2 * i : 2 * i + 2])
    return moved[count:], results


def meet(*streams):
    values = barrier(*[v for s in streams for v in (s.left, s.right)])
    for i, s in enumerate(streams):
        s.left, s.right = values[2 * i : 2 * i + 2]


def swap(values, axis, bit):
    size = lax.axis_size(axis)
    return lax.ppermute(values, axis, [(i, i ^ bit) for i in range(size)])


class Butterfly:
    def __init__(self, values, axis):
        self.left, self.right, self.axis, self.bit = values, jnp.zeros((1, 128), F32), axis, 1

    def step(self):
        if self.bit < lax.axis_size(self.axis):
            self.left = self.left + swap(self.left, self.axis, self.bit)
            self.bit *= 2
        return self

    def finish(self):
        while self.bit < lax.axis_size(self.axis):
            self.step()
        return self.left


def ladder(values, bit=4):
    while bit < lax.axis_size("wide"):
        values = add16(values, swap(values, "wide", bit))
        bit *= 2
    return values


def own_half(core):
    return pl.ds(pl.multiple_of(core[0] * (D // 2), D // 2), D // 2)


def columns_kernel(cuts, width, right_low, core, left, left_other, right_hbm, right_other, *refs):
    outs, right, semaphores = refs[:-2], refs[-2], refs[-1]
    copies = Copies(semaphores)
    coming = copies.start(right_hbm.at[:, own_half(core)], right)
    other = right_other[:, right_low : right_low + D // 2]
    part = dot(left_other[:, :width], other, TN)
    coming.wait()
    part += dot(left[:, :width], right[...], TN)
    for out, (low, high) in zip(outs, cuts):
        out[...] = part[:, low:high].astype(BF16)


def own_columns(core, cuts, width, left, left_other, right, right_other):
    total = left.shape[0]
    return call(
        functools.partial(columns_kernel, cuts, width, right_other.shape[1] - D // 2),
        [((width, high - low), BF16) for low, high in cuts],
        [SMEM, VMEM, VMEM, ANY, VMEM],
        2 * total * D * width,
        40 * MIB,
        [pltpu.VMEM((total, D // 2), BF16), pltpu.SemaphoreType.DMA((1,))],
    )(core.reshape(1), left, left_other, right, right_other)


def entry_sums_kernel(
    core, bundle, bundle_other, resid_hbm, normed_hbm, normed_other, mixer_out, *refs
):
    outs, (resid, normed, semaphores) = refs[:4], refs[4:]
    width = mixer_out.shape[0]
    copies = Copies(semaphores)
    first = copies.start(normed_hbm.at[:, own_half(core)], normed)
    second = copies.start(resid_hbm.at[:, own_half(core)], resid)
    for i in (3, 2, 1, 0):
        at = slice(i * width, (i + 1) * width)
        part = dot(normed_other[...], bundle_other[:, at], TN)
        if i == 3:
            first.wait()
        outs[i][...] = (part + dot(normed[...], bundle[:, at], TN)).astype(BF16)
    at, half = slice(4 * width, 5 * width), slice(5 * width, 5 * width + D // 2)
    part = dot(bundle_other[:, at], bundle_other[:, half], TN)
    second.wait()
    mixer_out[...] = (part + dot(bundle[:, at], resid[...], TN)).astype(BF16)


def sum_kernel(*refs):
    out, low = refs[-1], 0
    for i in range(len(refs) // 2):
        width = refs[2 * i].shape[1]
        out[:, low : low + width] = add16(refs[2 * i][...], refs[2 * i + 1][...])
        low += width


def summed(*values):
    rows = values[0].shape[0]
    columns = sum(v.shape[1] for v in values[::2])
    return ladder(
        call(
            sum_kernel,
            [((rows, columns), BF16)],
            [VMEM] * len(values),
            rows * columns,
            12 * MIB,
        )(*values)[0]
    )


def place(core, own, other, row_halves):
    rows, columns = own.shape
    return call(
        functools.partial(place_kernel, row_halves),
        [((2 * rows, columns) if row_halves else (rows, 2 * columns), F32)],
        [SMEM] + [VMEM] * 2,
        rows * columns,
        14 * MIB,
    )(core.reshape(1), own, other)[0]


def place_kernel(row_halves, core, own, other, out):
    rows, columns = own.shape
    for where, ref in ((core[0], own), (1 - core[0], other)):
        if row_halves:
            out[pl.ds(pl.multiple_of(where * rows, 128), rows), :] = ref[...].astype(F32)
        else:
            out[:, pl.ds(pl.multiple_of(where * columns, 128), columns)] = ref[...].astype(F32)


def call(kernel, outs, in_specs, flops, limit, scratch=(), out_specs=None, aliases=None):
    return pl.pallas_call(
        kernel,
        out_shape=[jax.ShapeDtypeStruct(s, d) for s, d in outs],
        in_specs=in_specs,
        out_specs=out_specs or [VMEM] * len(outs),
        scratch_shapes=list(scratch),
        input_output_aliases=aliases or {},
        compiler_params=pltpu.CompilerParams(vmem_limit_bytes=limit),
        cost_estimate=pl.CostEstimate(
            flops=flops, bytes_accessed=2 * flops // 1000, transcendentals=0
        ),
    )


def part_shapes(n, rows):
    return [((rows, D), BF16)] * (n - 1) + [((rows // 2, D), BF16)] * 2


class Copies:
    def __init__(self, semaphores):
        self.semaphores, self.count, self.out = semaphores, 0, []

    def start(self, source, target):
        copy = pltpu.make_async_copy(source, target, self.semaphores.at[self.count])
        self.count += 1
        copy.start()
        return copy

    def write(self, source, target):
        self.out.append(self.start(source, target))

    def drain(self):
        for copy in self.out:
            copy.wait()


def other_half(core):
    return pl.ds(pl.multiple_of((1 - core[0]) * (D // 2), D // 2), D // 2)


def fetch_pieces(copies, pieces, target, start_of, halved=True):
    rows = pieces[0].shape[0]
    out = []
    for r, piece in enumerate(pieces):
        if halved and r == len(pieces) - 1:
            at = start_of(r - 1) + rows // 2
        else:
            at = start_of(r)
        out.append(copies.start(piece, target.at[pl.ds(at, piece.shape[0]), :]))
    return out


def write_part(copies, buffer, parts, r, halved=True):
    n = len(parts) - halved
    rows = parts[0].shape[0]
    start = r * rows
    if halved and r == n - 1:
        half = rows // 2
        copies.write(buffer.at[pl.ds(start, half), :], parts[n - 1])
        copies.write(buffer.at[pl.ds(start + half, half), :], parts[n])
    else:
        copies.write(buffer.at[pl.ds(start, rows), :], parts[r])


def store_part(parts, r, values):
    n = len(parts) - 1
    if r < n - 1:
        parts[r][...] = values
    else:
        half = values.shape[0] // 2
        parts[n - 1][...] = values[:half]
        parts[n][...] = values[half:]


def assemble(pieces, target, start_of):
    n = len(pieces) - 1
    rows = pieces[0].shape[0]
    half = rows // 2
    for r in range(n - 1):
        target[pl.ds(start_of(r), rows), :] = pieces[r][...]
    start = start_of(n - 1)
    target[pl.ds(start, half), :] = pieces[n - 1][...]
    target[pl.ds(start + half, half), :] = pieces[n][...]


def segment_of(positions, ends):
    return sum((positions >= e).astype(jnp.int32) for e in ends)


def row_ends(lengths):
    first = lengths[0, 0]
    second = first + lengths[0, 1]
    return (first, second, second + lengths[0, 2])


class Block:
    def __init__(self, b, ends):
        start = b * BLOCK
        rows = lax.broadcasted_iota(jnp.int32, (BLOCK, BLOCK), 0)
        columns = lax.broadcasted_iota(jnp.int32, (BLOCK, BLOCK), 1)
        seg_rows = segment_of(rows + start, ends)
        seg_columns = segment_of(columns + start, ends)
        self.mask = jnp.logical_and(seg_rows == seg_columns, rows >= columns)
        self.last = segment_of(start + BLOCK - 1, ends)
        self.earlier = segment_of(start - 1, ends) if b > 0 else -1
        wide_rows = lax.broadcasted_iota(jnp.int32, (BLOCK, HEAD_DIM), 0)
        segments = segment_of(wide_rows + start, ends)
        self.from_state = segments == self.earlier
        self.to_state = segments == self.last

    def decay(self, full):
        return jnp.where(self.mask, full, 0.0)

    def keeping(self, rate):
        factor = jnp.exp(jnp.full((HEAD_DIM, HEAD_DIM), -rate * BLOCK, F32))
        return jnp.where(self.last == self.earlier, factor, 0.0)


def full_decay(rate):
    rows = lax.broadcasted_iota(jnp.int32, (BLOCK, BLOCK), 0)
    columns = lax.broadcasted_iota(jnp.int32, (BLOCK, BLOCK), 1)
    return jnp.exp(-rate * jnp.maximum(rows - columns, 0).astype(F32))


def edge_factors(rate):
    rows = lax.broadcasted_iota(jnp.int32, (BLOCK, HEAD_DIM), 0).astype(F32)
    return jnp.exp(-rate * (rows + 1.0)), jnp.exp(-rate * (BLOCK - 1.0 - rows))


def silu16(values):
    return (values * jax.nn.sigmoid(values)).astype(BF16)


def silu_grad(before):
    sigmoid = jax.nn.sigmoid(before)
    return sigmoid * (1.0 + before * (1.0 - sigmoid))


def entry_kernel(n, heads, order, core, lengths, rates, *refs):
    pieces, refs = refs[: n + 1], refs[n + 1 :]
    weights, mixer, refs = refs[:4], refs[4], refs[5:]
    normed_out, normed_send, proj_out, mixed_out, squares, states_out, refs = *refs[:6], refs[6:]
    parts, refs = refs[: n + 1], refs[n + 1 :]
    normed, weight_in, mixer_in, proj, mixed, pre, states, buffer, semaphores = refs
    copies = Copies(semaphores)
    rows = pieces[0].shape[0]
    total = n * rows
    width = heads * HEAD_DIM
    coming = fetch_pieces(
        copies, pieces, normed, lambda r: pl.multiple_of(order[0, r] * rows, rows)
    )
    for copy in coming:
        copy.wait()
    fetched = [copies.start(w, weight_in.at[i]) for i, w in enumerate(weights)]
    mixer_copy = copies.start(mixer, mixer_in)
    copies.write(normed, normed_out)
    copies.write(normed.at[:, other_half(core)], normed_send)
    for i in range(4):
        fetched[i].wait()
        for b in range(total // BLOCK):
            here = pl.ds(b * BLOCK, BLOCK)
            proj[here, i * width : (i + 1) * width] = dot(normed[here, :], weight_in[i])
    copies.write(proj, proj_out)
    ends = row_ends(lengths)
    fulls = [full_decay(rates[h]) for h in range(heads)]
    edges = [edge_factors(rates[h]) for h in range(heads)]
    state = [jnp.zeros((HEAD_DIM, HEAD_DIM), F32) for _ in range(heads)]
    ones = jnp.ones((8, HEAD_DIM), BF16)
    for b in range(total // BLOCK):
        here = pl.ds(b * BLOCK, BLOCK)
        block = Block(b, ends)
        square = jnp.zeros((8, BLOCK), F32)
        for h in range(heads):
            at = [slice(i * width + h * HEAD_DIM, i * width + (h + 1) * HEAD_DIM) for i in range(4)]
            query, key = silu16(proj[here, at[0]]), silu16(proj[here, at[1]])
            value = proj[here, at[2]].astype(BF16)
            inner, carried = edges[h]
            inner = jnp.where(block.from_state, inner, 0.0)
            carried = jnp.where(block.to_state, carried, 0.0)
            states[b, h] = state[h]
            weight = (dot(query, key, NT) * block.decay(fulls[h])).astype(BF16)
            high, low = split(state[h])
            out = dot(weight, value) + inner * (dot(query, high) + dot(query, low))
            high, low = split(key.astype(F32) * carried)
            state[h] = block.keeping(rates[h]) * state[h] + (
                dot(high, value, TN) + dot(low, value, TN)
            )
            mixed[here, at[0]] = out
            pre[here, at[0]] = (out * proj[here, at[3]]).astype(BF16)
            high, low = split(out * out)
            square += dot(ones, high, NT) + dot(ones, low, NT)
        squares[:, here] = square[0:1]
    copies.write(mixed, mixed_out)
    copies.write(states, states_out)
    mixer_copy.wait()
    for r in reversed(range(0, n, 2)):
        both = jnp.concatenate(
            [pre[pl.ds(pl.multiple_of(order[0, q] * rows, rows), rows), :] for q in (r, r + 1)], 0
        )
        buffer[r * rows : (r + 2) * rows, :] = dot(both, mixer_in[...]).astype(BF16)
        write_part(copies, buffer, parts, r + 1)
        write_part(copies, buffer, parts, r)
    copies.drain()


def column(row):
    return jnp.transpose(jnp.broadcast_to(row, (HEAD_DIM, row.shape[1])))


def exit_kernel(n, heads, order, core, lengths, rates, *refs):
    pieces, refs = refs[: n + 1], refs[n + 1 :]
    weights, mixer_hbm, refs = refs[:4], refs[4], refs[5:]
    proj_hbm, mixed_hbm, states_hbm, inverses, inners, refs = *refs[:5], refs[5:]
    resid_out, bundle, refs = *refs[:2], refs[2:]
    parts, refs = refs[: n + 1], refs[n + 1 :]
    resid, weight_in, mixer, proj, mixed, states, scaled, entry_g, scaled_g, buffer, sems = refs
    copies = Copies(sems)
    rows = pieces[0].shape[0]
    total = n * rows
    width = heads * HEAD_DIM
    mixer_copy = copies.start(mixer_hbm, mixer)
    coming = fetch_pieces(
        copies, pieces, resid, lambda r: pl.multiple_of(order[0, r] * rows, rows)
    )
    mixer_copy.wait()
    for copy in coming:
        copy.wait()
    saved = [
        copies.start(a, b)
        for a, b in ((proj_hbm, proj), (mixed_hbm, mixed), (states_hbm, states))
    ]
    fetched = [copies.start(w, weight_in.at[i]) for i, w in enumerate(weights)]
    copies.write(resid, resid_out)
    copies.write(resid.at[:, other_half(core)], bundle.at[:, pl.ds(5 * width, D // 2)])
    for b in range(total // BLOCK):
        here = pl.ds(b * BLOCK, BLOCK)
        scaled_g[here, :] = dot(resid[here, :], mixer[...], NT)
    for copy in saved:
        copy.wait()
    ends = row_ends(lengths)
    fulls = [full_decay(rates[h]) for h in range(heads)]
    edges = [edge_factors(rates[h]) for h in range(heads)]
    later = [jnp.zeros((HEAD_DIM, HEAD_DIM), F32) for _ in range(heads)]
    for b in reversed(range(total // BLOCK)):
        here = pl.ds(b * BLOCK, BLOCK)
        block = Block(b, ends)
        inverse = column(inverses[:, here])
        mean = column(inners[:, here]) * (1.0 / D)
        for h in range(heads):
            at = [slice(i * width + h * HEAD_DIM, i * width + (h + 1) * HEAD_DIM) for i in range(4)]
            query_pre, key_pre = proj[here, at[0]], proj[here, at[1]]
            query, key = silu16(query_pre), silu16(key_pre)
            value = proj[here, at[2]].astype(BF16)
            gate = proj[here, at[3]]
            grad_s = scaled_g[here, at[0]]
            unit = mixed[here, at[0]] * inverse
            scaled[here, at[0]] = (unit * gate).astype(BF16)
            entry_g[here, at[3]] = (grad_s * unit).astype(BF16)
            grad = (inverse * (grad_s * gate - unit * mean)).astype(BF16)
            inner, carried = edges[h]
            inner = jnp.where(block.from_state, inner, 0.0)
            carried = jnp.where(block.to_state, carried, 0.0)
            decay = block.decay(fulls[h])
            weight = (dot(query, key, NT) * decay).astype(BF16)
            score = (dot(grad, value, NT) * decay).astype(BF16)
            high, low = split(states[b, h])
            query_g = dot(score, key) + inner * (dot(grad, high, NT) + dot(grad, low, NT))
            high, low = split(later[h])
            key_g = dot(score, query, TN) + carried * (dot(value, high, NT) + dot(value, low, NT))
            value_g = dot(weight, grad, TN) + carried * (dot(key, high) + dot(key, low))
            high, low = split(query.astype(F32) * inner)
            later[h] = (
                dot(high, grad, TN) + dot(low, grad, TN) + block.keeping(rates[h]) * later[h]
            )
            entry_g[here, at[0]] = (query_g * silu_grad(query_pre)).astype(BF16)
            entry_g[here, at[1]] = (key_g * silu_grad(key_pre)).astype(BF16)
            entry_g[here, at[2]] = value_g.astype(BF16)
    copies.write(scaled, bundle.at[:, pl.ds(4 * width, width)])
    copies.write(entry_g, bundle.at[:, pl.ds(0, 4 * width)])
    for copy in fetched:
        copy.wait()
    for r in reversed(range(0, n, 2)):
        both = jnp.concatenate(
            [entry_g[pl.ds(pl.multiple_of(order[0, q] * rows, rows), rows), :] for q in (r, r + 1)],
            0,
        )
        buffer[r * rows : (r + 2) * rows, :] = sum(
            dot(both[:, i * width : (i + 1) * width], weight_in[i], NT) for i in range(4)
        ).astype(BF16)
        write_part(copies, buffer, parts, r + 1)
        write_part(copies, buffer, parts, r)
    copies.drain()


def cotangent_kernel(n, core, *refs):
    pieces, down, grad, grad_send, *products = refs[: n + 1], *refs[n + 1 :]
    rows = pieces[0].shape[0]
    assemble(pieces, grad, lambda r: r * rows)
    grad_send[...] = grad[:, other_half(core)]
    for r, out in enumerate(products):
        out[...] = dot(grad[pl.ds(2 * r * rows, 2 * rows), :], down[...], NT)


def hidden_kernel(index, halved, core, *refs):
    count = 2 + halved
    pieces, refs = refs[:count], refs[count:]
    first, second, product_g, refs = *refs[:3], refs[3:]
    refs = refs if index == 0 else refs[4:]
    (normed_out, product_out, second_out, bundle), refs = refs[:4], refs[4:]
    parts, refs = refs[:count], refs[count:]
    normed, product, first_g, second_g, sems = refs
    copies = Copies(sems)
    low = 0
    for piece in pieces:
        normed[low : low + piece.shape[0], :] = piece[...]
        low += piece.shape[0]
    units, padded = first.shape[0], product.shape[1]
    if padded > units:
        for ref in (product, first_g, second_g):
            ref[:, units:] = jnp.zeros((low, padded - units), BF16)
    here = pl.ds(index * low, low)
    copies.write(normed, normed_out.at[here, :])
    copies.write(normed.at[:, other_half(core)], bundle.at[here, pl.ds(padded, D // 2)])
    tokens = normed[...]
    first_act, second_act = dot(tokens, first[...], NT), dot(tokens, second[...], NT)
    product[:, :units] = (first_act * second_act).astype(BF16)
    copies.write(product, product_out.at[here, :])
    grad = product_g[...]
    one, two = (grad * second_act).astype(BF16), (grad * first_act).astype(BF16)
    first_g[:, :units] = one
    copies.write(first_g, bundle.at[here, pl.ds(0, padded)])
    second_g[:, :units] = two
    copies.write(second_g, second_out.at[here, :])
    result = (dot(one, first[...]) + dot(two, second[...])).astype(BF16)
    low = 0
    for part in parts:
        part[...] = result[low : low + part.shape[0]]
        low += part.shape[0]
    copies.drain()


def down_kernel(n, product, down, *parts):
    rows, units = parts[0].shape[0], down.shape[0]
    for r in range(0, n, 2):
        result = dot(product[pl.ds(r * rows, 2 * rows), :units], down[...]).astype(BF16)
        store_part(parts, r, result[:rows])
        store_part(parts, r + 1, result[rows:])


def output_kernel(tokens, attn, ffn, valid_rows, output, sums):
    rows = tokens.shape[0]
    valid = lax.broadcasted_iota(jnp.int32, (rows, 1), 0) < valid_rows[0]
    tokens_wide = tokens[...].astype(F32)
    output[...] = (tokens_wide + attn[...] + ffn[...]).astype(BF16)
    lane = lax.broadcasted_iota(jnp.int32, (1, 128), 1)
    out = jnp.zeros((1, 128), F32)
    for i, values in enumerate((tokens_wide, attn[...], ffn[...])):
        per_row = jnp.sum(values * values, axis=1, keepdims=True)
        whole = jnp.sum(jnp.where(valid, per_row, 0.0), axis=0, keepdims=True)
        out += jnp.where(lane == i, whole, 0.0)
    counted = jnp.clip(valid_rows[0], 0, rows).astype(F32)
    sums[...] = out + jnp.where(lane == 3, counted, 0.0)


def local(
    tokens_in,
    query_weight,
    key_weight,
    value_weight,
    gate_weight,
    mixer_weight,
    first_weight,
    second_weight,
    down_weight,
    doc_lengths,
    head_decay,
    out_grad,
):
    n = lax.axis_size("narrow")
    rows = tokens_in.shape[0]
    total = rows * n
    heads = head_decay.shape[0]
    width = heads * HEAD_DIM
    units = first_weight.shape[1]
    me = lax.axis_index("narrow")
    core = lax.axis_index("wide") % 2
    start_row = me * rows
    order = lax.dynamic_slice(jnp.asarray(order_table(n)), (me, 0), (1, n))
    where = core.reshape(1)
    entry_weights = (query_weight, key_weight, value_weight, gate_weight)
    tokens_wide = tokens_in.astype(F32)
    rates = head_decay

    half_rows = total // 2
    blocks = total // BLOCK
    first_t, second_t = first_weight.T, second_weight.T
    valid_rows = (jnp.sum(doc_lengths[0, : NDOC - 1]) - start_row).reshape(1)

    pieces = Gather(normalize(tokens_wide).astype(BF16), n).finish()
    shapes = [
        ((total, D), BF16),
        ((total, D // 2), BF16),
        ((total, 4 * width), F32),
        ((total, width), F32),
        ((1, total), F32),
        ((blocks, heads, HEAD_DIM, HEAD_DIM), F32),
    ] + part_shapes(n, rows)
    *pieces, grad_own = barrier(*pieces, out_grad)
    cotangent = Gather(grad_own, n).step()
    normed, normed_send, proj, mixed, squares, states, *parts = call(
        functools.partial(entry_kernel, n, heads),
        shapes,
        [SMEM] * 4 + [ANY] * (n + 6),
        12 * total * D * width,
        48 * MIB,
        [
            pltpu.VMEM((total, D), BF16),
            pltpu.VMEM((4, D, width), BF16),
            pltpu.VMEM((width, D), BF16),
            pltpu.VMEM((total, 4 * width), F32),
            pltpu.VMEM((total, width), F32),
            pltpu.VMEM((total, width), BF16),
            pltpu.VMEM((blocks, heads, HEAD_DIM, HEAD_DIM), F32),
            pltpu.VMEM((total, D), BF16),
            pltpu.SemaphoreType.DMA((2 * n + 13,)),
        ],
        [VMEM if i == 4 else ANY for i in range(len(shapes))],
    )(order, where, doc_lengths, rates, *pieces, *entry_weights, mixer_weight)
    squares, cotangent.left, cotangent.right, *parts = barrier(
        squares, cotangent.left, cotangent.right, *parts
    )
    scatter = Scatter(parts, n)
    hop = Butterfly(squares, "narrow")
    while cotangent.left_steps:
        scatter.step()
        cotangent.step()
        hop.step()
        meet(scatter, cotangent, hop)
    squares = hop.finish()
    grad_pieces = cotangent.pieces
    attn_raw, normed_other = barrier(scatter.finish(), swap(normed_send, "wide", 1))
    inverses = lax.rsqrt(squares / D + EPS)
    inverse_own = lax.dynamic_slice(inverses, (0, start_row), (1, rows)).reshape(rows, 1)
    attn_own = attn_raw * inverse_own
    hidden_own = tokens_wide + attn_own

    padded = -(-units // 128) * 128

    def hidden(index, pieces):
        halved = len(pieces) == 3
        count = len(pieces)
        outs = call(
            functools.partial(hidden_kernel, index, halved),
            [((total, D), BF16)]
            + [((total, padded), BF16)] * 2
            + [((total, padded + D // 2), BF16)]
            + [(p.shape, BF16) for p in pieces],
            [SMEM] + [VMEM] * (count + 3) + [ANY] * len(whole),
            16 * rows * D * units,
            40 * MIB,
            [pltpu.VMEM((2 * rows, D), BF16)]
            + [pltpu.VMEM((2 * rows, padded), BF16)] * 3
            + [pltpu.SemaphoreType.DMA((5,))],
            [ANY] * 4 + [VMEM] * count,
            {count + 4 + i: i for i in range(len(whole))},
        )(where, *pieces, first_t, second_t, product_g[index], *whole)
        return outs[:4], list(outs[4:])

    gather = Gather(normalize(hidden_own).astype(BF16), n)
    *grad_pieces, gather.left = barrier(*grad_pieces, gather.left)
    gather.right = gather.left
    gather.step()
    grad_all, grad_send, *product_g = call(
        functools.partial(cotangent_kernel, n),
        [((total, D), BF16), ((total, D // 2), BF16)] + [((2 * rows, units), F32)] * (n // 2),
        [SMEM] + [VMEM] * (n + 2),
        2 * total * D * units,
        22 * MIB,
    )(where, *grad_pieces, down_weight)
    gather.left, gather.right, grad_send, *product_g = barrier(
        gather.left, gather.right, grad_send, *product_g
    )
    whole, parts = [], []
    for i in range(n // 2 - 1):
        pieces = gather.pieces[2 * i : 2 * i + 2]
        gather.step()
        whole, new_parts = hidden(i, pieces)
        if gather.left_steps:
            gather.left, gather.right, *new_parts = barrier(
                gather.left, gather.right, *new_parts
            )
        parts += new_parts
    grad_other = swap(grad_send, "wide", 1)
    pieces = barrier(*gather.pieces[n - 2 :], grad_other)
    grad_other = pieces[-1]
    whole, new_parts = hidden(n // 2 - 1, pieces[:-1])
    parts += new_parts
    normed2, product, second_g, bundle = whole

    scatter = Scatter(parts, n)
    stream = Together(scatter)
    half = D // 2
    step = 3 * half // 8
    cuts = tuple((low, min(half, low + step)) for low in range(0, half, step))

    def first_work(product, grad_all, grad_other):
        other = swap(product, "wide", 1)
        return own_columns(core, cuts, units, product, other, grad_all, grad_other)

    (bundle_other,), down_own = region(
        [stream], [(bundle, "wide", 1)], first_work, [product, grad_all, grad_other]
    )
    (received, second_other_g), first_own = region(
        [stream],
        [(down_own[0], "wide", 2), (second_g, "wide", 1)],
        lambda *v: own_columns(core, cuts, units, *v),
        [bundle, bundle_other, normed2, bundle_other],
    )
    down_in = [received]
    (received,), second_own = region(
        [stream],
        [(down_own[1], "wide", 2)],
        lambda *v: own_columns(core, cuts, units, *v),
        [second_g, second_other_g, normed2, bundle_other],
    )
    down_in.append(received)
    (received,), _ = region([stream], [(down_own[2], "wide", 2)])
    down_in.append(received)
    while scatter.left_steps:
        region([stream])
    normed2_g = scatter.result
    hidden_g = out_grad.astype(F32) + norm_grad(hidden_own, normed2_g)
    resid_own = hidden_g.astype(BF16)
    inner_own = jnp.sum(resid_own.astype(F32) * attn_own, axis=1).reshape(1, rows)
    inners = lax.dynamic_update_slice(jnp.zeros((1, total), F32), inner_own, (0, start_row))

    gather = Gather(resid_own, n)

    def mixed_pairs(owns, ins):
        return [v for pair in zip(owns, ins) for v in pair]

    def output_parts(product, *pairs):
        parts = call(
            functools.partial(down_kernel, n),
            part_shapes(n, rows),
            [VMEM] * 2,
            2 * total * D * units,
            40 * MIB,
        )(product, down_weight)
        return parts, summed(*pairs)

    (received, hop), (parts, down_total) = region(
        [gather],
        [(first_own[0], "wide", 2), (inners, "narrow", 1)],
        output_parts,
        [product, *mixed_pairs(down_own, down_in)],
    )
    first_in, inners = [received], inners + hop
    (received, hop, down_other), _ = region(
        [gather],
        [(first_own[1], "wide", 2), (inners, "narrow", 2), (down_total, "wide", 1)],
    )
    first_in.append(received)
    inners = inners + hop
    (received, hop), down_w = region(
        [gather],
        [(first_own[2], "wide", 2), (inners, "narrow", 4)],
        lambda own, other: place(core, own, other, False),
        [down_total, down_other],
    )
    first_in.append(received)
    inners = inners + hop
    bit = 8
    while gather.left_steps > 1:
        if bit < n:
            (hop,), _ = region([gather], [(inners, "narrow", bit)])
            inners = inners + hop
            bit *= 2
        else:
            region([gather])
    scatter2 = Scatter(parts, n)
    stream2 = Together(scatter2)
    (received,), first_total = region(
        [gather, stream2],
        [(second_own[0], "wide", 2)],
        summed,
        mixed_pairs(first_own, first_in),
    )
    second_in = [received]

    shapes = [
        ((total, D), BF16),
        ((total, 5 * width + D // 2), BF16),
    ] + part_shapes(n, rows)
    leave = call(
        functools.partial(exit_kernel, n, heads),
        shapes,
        [SMEM] * 4 + [ANY] * (n + 9) + [VMEM] * 2,
        12 * total * D * width,
        48 * MIB,
        [
            pltpu.VMEM((total, D), BF16),
            pltpu.VMEM((4, D, width), BF16),
            pltpu.VMEM((width, D), BF16),
            pltpu.VMEM((total, 4 * width), F32),
            pltpu.VMEM((total, width), F32),
            pltpu.VMEM((blocks, heads, HEAD_DIM, HEAD_DIM), F32),
            pltpu.VMEM((total, width), BF16),
            pltpu.VMEM((total, 4 * width), BF16),
            pltpu.VMEM((total, width), F32),
            pltpu.VMEM((total, D), BF16),
            pltpu.SemaphoreType.DMA((2 * n + 15,)),
        ],
        [ANY] * len(shapes),
    )
    (received, first_other), (resid, bundle, *parts) = region(
        [stream2],
        [(second_own[1], "wide", 2), (first_total, "wide", 1)],
        lambda inverses, inners, *pieces: leave(
            order,
            where,
            doc_lengths,
            rates,
            *pieces,
            *entry_weights,
            mixer_weight,
            proj,
            mixed,
            states,
            inverses,
            inners,
        ),
        [inverses, inners, *gather.pieces],
    )
    second_in.append(received)

    scatter = Scatter(parts, n)

    stream = Together(scatter2, scatter)

    def entry_work(bundle, resid, normed, normed_other, *first):
        owns = call(
            entry_sums_kernel,
            [((width, D // 2), BF16)] + [((D // 2, width), BF16)] * 4,
            [SMEM, VMEM, VMEM, ANY, ANY, VMEM],
            10 * total * D * width,
            40 * MIB,
            [pltpu.VMEM((total, D // 2), BF16)] * 2 + [pltpu.SemaphoreType.DMA((2,))],
        )(where, bundle, swap(bundle, "wide", 1), resid, normed, normed_other)
        return owns, place(core, *first, False)

    (received,), ((mixer_own, *owns), first_w) = region(
        [stream],
        [(second_own[2], "wide", 2)],
        entry_work,
        [bundle, resid, normed, normed_other, first_total, first_other],
    )
    second_in.append(received)
    query_own, key_own, value_own, gate_own = owns
    (mixer_in, gate_in), second_total = region(
        [stream],
        [(mixer_own, "wide", 2), (gate_own, "wide", 2)],
        summed,
        mixed_pairs(second_own, second_in),
    )
    while scatter2.left_steps:
        region([stream])
    ffn_own = scatter2.result
    stream = Together(scatter)

    def output_work(tokens_in, attn_own, ffn_own, a, b, c, d):
        output, stats = call(
            output_kernel,
            [((rows, D), BF16), ((1, 128), F32)],
            [VMEM] * 3 + [SMEM],
            6 * rows * D,
            8 * MIB,
        )(tokens_in, attn_own, ffn_own, valid_rows)
        return output, stats, summed(a, b), summed(c, d)

    (value_in, second_other), (output, stats, mixer_total, gate_total) = region(
        [stream],
        [(value_own, "wide", 2), (second_total, "wide", 1)],
        output_work,
        [tokens_in, attn_own, ffn_own, mixer_own, mixer_in, gate_own, gate_in],
    )
    (key_in, mixer_other, gate_other), (second_w, value_total) = region(
        [stream],
        [(key_own, "wide", 2), (mixer_total, "wide", 1), (gate_total, "wide", 1)],
        lambda own, other, *v: (place(core, own, other, False), summed(*v)),
        [second_total, second_other, value_own, value_in],
    )
    while scatter.left_steps:
        region([stream])
    normed_g = scatter.result

    def end_work(stats, normed_g, a, b, *v):
        key_total = summed(a, b)
        key_other = swap(key_total, "wide", 1)
        return (
            Butterfly(stats, "narrow").finish(),
            hidden_g + norm_grad(tokens_wide, normed_g),
            place(core, key_total, key_other, True),
            place(core, *v[:2], False),
            place(core, *v[2:], True),
        )

    (query_in, value_other), (stats, input_grad, key_w, mixer_w, gate_w) = region(
        [],
        [(query_own, "wide", 2), (value_total, "wide", 1)],
        end_work,
        [stats, normed_g, key_own, key_in, mixer_total, mixer_other, gate_total, gate_other],
    )
    query_total = summed(query_own, query_in)
    query_w = place(core, query_total, swap(query_total, "wide", 1), True)
    value_w = place(core, value_total, value_other, True)
    stats = Butterfly(stats, "wide").finish()
    stream_rms = jnp.sqrt(stats[0, :3] / (stats[0, 3] * D))
    return (
        output,
        input_grad,
        query_w,
        key_w,
        value_w,
        gate_w,
        mixer_w,
        first_w.T,
        second_w.T,
        down_w,
        stream_rms,
    )


def solution(mesh):
    split_tokens = P(("wide", "narrow"), None)
    columns, rows = P(None, "narrow"), P("narrow", None)
    return jax.shard_map(
        local,
        mesh=mesh,
        in_specs=(split_tokens,)
        + (columns,) * 4
        + (rows, columns, columns, rows, P("wide", None), P("narrow"), split_tokens),
        out_specs=(split_tokens,) * 2 + (columns,) * 4 + (rows, columns, columns, rows, P()),
        check_vma=False,
    )
```

```python
import functools

import jax
import jax.numpy as jnp
import numpy as np
from jax import lax
from jax.experimental import pallas as pl
from jax.experimental.pallas import tpu as pltpu
from jax.sharding import PartitionSpec as P

D = 2048
HEAD_DIM = 128
NDOC = 4
EPS = 1e-06
BLOCK = 256
MIB = 1 << 20

F32 = jnp.float32
BF16 = jnp.bfloat16
NN = (((1,), (0,)), ((), ()))
NT = (((1,), (1,)), ((), ()))
TN = (((0,), (0,)), ((), ()))
VMEM = pl.BlockSpec(memory_space=pltpu.VMEM)
SMEM = pl.BlockSpec(memory_space=pltpu.SMEM)
ANY = pl.BlockSpec(memory_space=pl.ANY)


def dot(a, b, dims=NN):
    return lax.dot_general(a, b, dims, preferred_element_type=F32)


def split(values):
    high = values.astype(BF16)
    return high, (values - high.astype(F32)).astype(BF16)


def normalize(values):
    return values * lax.rsqrt(jnp.mean(values * values, axis=-1, keepdims=True) + EPS)


def norm_grad(values, grad_in):
    inverse = lax.rsqrt(jnp.mean(values * values, axis=-1, keepdims=True) + EPS)
    normed = values * inverse
    return inverse * (grad_in - normed * jnp.mean(grad_in * normed, axis=-1, keepdims=True))


def ring_order(n):
    if n == 16:
        return [r * 4 + (c if r % 2 == 0 else 3 - c) for r in range(4) for c in range(4)]
    return list(range(0, n, 2)) + list(range(n - 1, 0, -2))


def distances(n):
    out = [0]
    for k in range(1, n // 2):
        out += [-k, k]
    return out + [n // 2]


def order_table(n):
    ring = ring_order(n)
    place = {device: i for i, device in enumerate(ring)}
    return np.array(
        [[ring[(place[me] + d) % n] for d in distances(n)] for me in range(n)], np.int32
    )


def onward(values, n):
    ring = ring_order(n)
    return lax.ppermute(values, "narrow", [(ring[i], ring[(i + 1) % n]) for i in range(n)])


def backward(values, n):
    ring = ring_order(n)
    return lax.ppermute(values, "narrow", [(ring[(i + 1) % n], ring[i]) for i in range(n)])


def barrier(*values):
    return lax.optimization_barrier(values)


def add16(a, b):
    return (a.astype(F32) + b.astype(F32)).astype(BF16)


class Gather:
    def __init__(self, own, n):
        self.n, self.left_steps = n, n // 2
        self.left = self.right = own
        self.pieces = [own]

    def outgoing(self):
        if self.left_steps == 1:
            half = self.left.shape[0] // 2
            return self.left[:half], self.right[half:]
        return self.left, self.right

    def incoming(self, left, right):
        self.left_steps -= 1
        self.left, self.right = left, right
        self.pieces += [left, right]

    def step(self, count=1):
        for _ in range(count):
            left, right = self.outgoing()
            self.incoming(onward(left, self.n), backward(right, self.n))
        return self

    def finish(self):
        return self.step(self.left_steps).pieces


def merge_kernel(layout, *refs):
    outs, refs = refs[-2:], list(refs[:-2])
    at = 0
    for rows, half, offset in layout:
        if offset is None:
            for out in outs:
                out[at : at + rows] = refs.pop(0)[...]
        else:
            nears, parts, refs = refs[:2], refs[2:4], refs[4:]
            for i in range(2):
                low = half * i if half < rows else 0
                outs[i][at : at + rows] = nears[i][...]
                outs[i][at + low : at + low + half] = add16(
                    nears[i][low : low + half], parts[i][offset : offset + half]
                )
        at += rows


def join_one(low, near, part, out):
    rows = part.shape[0]
    out[...] = near[...]
    out[low : low + rows] = add16(near[low : low + rows], part[...])


class Scatter:
    def __init__(self, parts, n):
        self.n, self.left_steps = n, n // 2
        self.near = {d: parts[i] for i, d in enumerate(distances(n)[:-1])}
        self.left, self.right = parts[-2], parts[-1]
        self.received = None

    def operands(self):
        if self.received is None:
            return [self.left, self.right], (self.left.shape[0], 0, None)
        left, right, offset, half = self.received
        near = [self.near[self.left_steps], self.near[-self.left_steps]]
        return near + [left, right], (near[0].shape[0], half, offset)

    def take(self, left, right, offset, rows):
        self.left_steps -= 1
        if self.left_steps == 0:
            at = slice(offset, offset + rows)
            self.result = self.near[0].astype(F32) + left[at].astype(F32) + right[at].astype(F32)
        self.received = (left, right, offset, rows)

    def step(self, count=1):
        for _ in range(count):
            self.left_steps -= 1
            left, right = onward(self.left, self.n), backward(self.right, self.n)
            k = self.left_steps
            shape = self.near[k].shape
            if k == 0:
                self.result = self.near[0].astype(F32) + left.astype(F32) + right.astype(F32)
            elif shape == left.shape:
                self.left, self.right = add16(self.near[k], left), add16(self.near[-k], right)
            else:
                half = shape[0] // 2
                self.left, self.right = [
                    call(
                        functools.partial(join_one, low),
                        [(shape, BF16)],
                        [VMEM] * 2,
                        shape[0] * shape[1],
                        14 * MIB,
                    )(near, part)[0]
                    for low, near, part in ((0, self.near[k], left), (half, self.near[-k], right))
                ]
        return self

    def finish(self):
        return self.step(self.left_steps).result


class Together:
    def __init__(self, *scatters):
        self.scatters, self.n = scatters, scatters[0].n

    def outgoing(self):
        operands, self.layout = [], []
        for s in self.scatters:
            values, layout = s.operands()
            operands += values
            self.layout.append(layout)
        if len(self.layout) == 1 and self.layout[0][2] is None:
            return operands
        rows = sum(entry[0] for entry in self.layout)
        return call(
            functools.partial(merge_kernel, tuple(self.layout)),
            [((rows, D), BF16)] * 2,
            [VMEM] * len(operands),
            2 * rows * D,
            14 * MIB,
        )(*operands)

    def incoming(self, left, right):
        offset = 0
        for s, (rows, _, _) in zip(self.scatters, self.layout):
            s.take(left, right, offset, rows)
            offset += rows


def region(streams=(), swaps=(), work=None, inputs=()):
    out = [v for s in streams for v in s.outgoing()]
    count = len(out)
    values, inputs = lax.optimization_barrier((out + [s[0] for s in swaps], list(inputs)))
    moved = [
        onward(v, streams[0].n) if i % 2 == 0 else backward(v, streams[0].n)
        for i, v in enumerate(values[:count])
    ]
    moved += [swap(v, s[1], s[2]) for v, s in zip(values[count:], swaps)]
    results = work(*inputs) if work else ()
    moved, results = lax.optimization_barrier((moved, results))
    for i, s in enumerate(streams):
        s.incoming(*moved[2 * i : 2 * i + 2])
    return moved[count:], results


def meet(*streams):
    values = barrier(*[v for s in streams for v in (s.left, s.right)])
    for i, s in enumerate(streams):
        s.left, s.right = values[2 * i : 2 * i + 2]


def swap(values, axis, bit):
    size = lax.axis_size(axis)
    return lax.ppermute(values, axis, [(i, i ^ bit) for i in range(size)])


class Butterfly:
    def __init__(self, values, axis):
        self.left, self.right, self.axis, self.bit = values, jnp.zeros((1, 128), F32), axis, 1

    def step(self):
        if self.bit < lax.axis_size(self.axis):
            self.left = self.left + swap(self.left, self.axis, self.bit)
            self.bit *= 2
        return self

    def finish(self):
        while self.bit < lax.axis_size(self.axis):
            self.step()
        return self.left


def ladder(values, bit=4):
    while bit < lax.axis_size("wide"):
        values = add16(values, swap(values, "wide", bit))
        bit *= 2
    return values


def own_half(core):
    return pl.ds(pl.multiple_of(core[0] * (D // 2), D // 2), D // 2)


def columns_kernel(cuts, lefts, rights, core, *refs):
    sources, outs, refs = refs[:4], refs[4 : 4 + len(cuts)], refs[4 + len(cuts) :]
    left, left_other, right, right_other, semaphores = refs
    width = outs[0].shape[0]
    columns = right.shape[1]
    copies = Copies(semaphores)
    coming = [
        copies.start(sources[1].at[:, pl.ds(lefts[1], left.shape[1])], left_other),
        copies.start(sources[3].at[:, pl.ds(rights[1], columns)], right_other),
        copies.start(sources[0].at[:, pl.ds(lefts[0], left.shape[1])], left),
    ]
    if rights[0] is None:
        coming.append(copies.start(sources[2].at[:, own_half(core)], right))
    else:
        coming.append(copies.start(sources[2].at[:, pl.ds(rights[0], columns)], right))
    coming[0].wait()
    coming[1].wait()
    part = dot(left_other[:, :width], right_other[...], TN)
    coming[2].wait()
    coming[3].wait()
    part += dot(left[:, :width], right[...], TN)
    for out, (low, high) in zip(outs, cuts):
        out[...] = part[:, low:high].astype(BF16)


def own_columns(core, cuts, width, left, left_other, right, right_other, lefts=(0, 0), low=0):
    total = left.shape[0]
    padded = -(-width // 128) * 128
    return call(
        functools.partial(columns_kernel, cuts, lefts, (None, low)),
        [((width, high - low), BF16) for low, high in cuts],
        [SMEM] + [ANY] * 4,
        2 * total * D * width,
        54 * MIB,
        [pltpu.VMEM((total, padded), BF16)] * 2
        + [pltpu.VMEM((total, D // 2), BF16)] * 2
        + [pltpu.SemaphoreType.DMA((4,))],
    )(core.reshape(1), left, left_other, right, right_other)


def rows_kernel(first, core, *refs):
    sources, refs = refs[:4], refs[4:]
    outs, (normed, normed_other, grads, grads_other, semaphores) = refs[:-5], refs[-5:]
    width = outs[0].shape[1]
    columns = pl.ds(first * width, len(outs) * width)
    copies = Copies(semaphores)
    coming = [
        copies.start(sources[1], normed_other),
        copies.start(sources[3].at[:, columns], grads_other),
        copies.start(sources[0].at[:, own_half(core)], normed),
        copies.start(sources[2].at[:, columns], grads),
    ]
    coming[0].wait()
    coming[1].wait()
    part = dot(normed_other[...], grads_other[...], TN)
    coming[2].wait()
    coming[3].wait()
    part += dot(normed[...], grads[...], TN)
    for i, out in enumerate(outs):
        out[...] = part[:, i * width : (i + 1) * width].astype(BF16)


def own_rows(core, first, count, width, normed, normed_other, bundle, bundle_other):
    total = normed.shape[0]
    return call(
        functools.partial(rows_kernel, first),
        [((D // 2, width), BF16)] * count,
        [SMEM] + [ANY] * 4,
        2 * total * D * width * count,
        54 * MIB,
        [pltpu.VMEM((total, D // 2), BF16)] * 2
        + [pltpu.VMEM((total, count * width), BF16)] * 2
        + [pltpu.SemaphoreType.DMA((4,))],
    )(core.reshape(1), normed, normed_other, bundle, bundle_other)


def add_kernel(keep, crossed, out):
    out[...] = (keep[...] + crossed[...].astype(F32)).astype(BF16)


def sum_kernel(*refs):
    out, low = refs[-1], 0
    for i in range(len(refs) // 2):
        width = refs[2 * i].shape[1]
        out[:, low : low + width] = add16(refs[2 * i][...], refs[2 * i + 1][...])
        low += width


def summed(*values):
    rows = values[0].shape[0]
    columns = sum(v.shape[1] for v in values[::2])
    return ladder(
        call(
            sum_kernel,
            [((rows, columns), BF16)],
            [VMEM] * len(values),
            rows * columns,
            14 * MIB,
        )(*values)[0]
    )


def place(core, own, other, row_halves):
    rows, columns = own.shape
    return call(
        functools.partial(place_kernel, row_halves),
        [((2 * rows, columns) if row_halves else (rows, 2 * columns), F32)],
        [SMEM] + [VMEM] * 2,
        rows * columns,
        14 * MIB,
    )(core.reshape(1), own, other)[0]


def place_kernel(row_halves, core, own, other, out):
    rows, columns = own.shape
    for where, ref in ((core[0], own), (1 - core[0], other)):
        if row_halves:
            out[pl.ds(pl.multiple_of(where * rows, 128), rows), :] = ref[...].astype(F32)
        else:
            out[:, pl.ds(pl.multiple_of(where * columns, 128), columns)] = ref[...].astype(F32)


def call(kernel, outs, in_specs, flops, limit, scratch=(), out_specs=None, aliases=None):
    return pl.pallas_call(
        kernel,
        out_shape=[jax.ShapeDtypeStruct(s, d) for s, d in outs],
        in_specs=in_specs,
        out_specs=out_specs or [VMEM] * len(outs),
        scratch_shapes=list(scratch),
        input_output_aliases=aliases or {},
        compiler_params=pltpu.CompilerParams(vmem_limit_bytes=limit),
        cost_estimate=pl.CostEstimate(
            flops=flops, bytes_accessed=2 * flops // 1000, transcendentals=0
        ),
    )


def part_shapes(n, rows):
    return [((rows, D), BF16)] * (n - 1) + [((rows // 2, D), BF16)] * 2


class Copies:
    def __init__(self, semaphores):
        self.semaphores, self.count, self.out = semaphores, 0, []

    def start(self, source, target):
        copy = pltpu.make_async_copy(source, target, self.semaphores.at[self.count])
        self.count += 1
        copy.start()
        return copy

    def write(self, source, target):
        self.out.append(self.start(source, target))

    def drain(self):
        for copy in self.out:
            copy.wait()


def other_half(core):
    return pl.ds(pl.multiple_of((1 - core[0]) * (D // 2), D // 2), D // 2)


def fetch_pieces(copies, pieces, target, start_of, halved=True):
    rows = pieces[0].shape[0]
    out = []
    for r, piece in enumerate(pieces):
        if halved and r == len(pieces) - 1:
            at = start_of(r - 1) + rows // 2
        else:
            at = start_of(r)
        out.append(copies.start(piece, target.at[pl.ds(at, piece.shape[0]), :]))
    return out


def write_part(copies, buffer, parts, r, halved=True):
    n = len(parts) - halved
    rows = parts[0].shape[0]
    start = r * rows
    if halved and r == n - 1:
        half = rows // 2
        copies.write(buffer.at[pl.ds(start, half), :], parts[n - 1])
        copies.write(buffer.at[pl.ds(start + half, half), :], parts[n])
    else:
        copies.write(buffer.at[pl.ds(start, rows), :], parts[r])


def store_part(parts, r, values):
    n = len(parts) - 1
    if r < n - 1:
        parts[r][...] = values
    else:
        half = values.shape[0] // 2
        parts[n - 1][...] = values[:half]
        parts[n][...] = values[half:]


def assemble(pieces, target, start_of):
    n = len(pieces) - 1
    rows = pieces[0].shape[0]
    half = rows // 2
    for r in range(n - 1):
        target[pl.ds(start_of(r), rows), :] = pieces[r][...]
    start = start_of(n - 1)
    target[pl.ds(start, half), :] = pieces[n - 1][...]
    target[pl.ds(start + half, half), :] = pieces[n][...]


def segment_of(positions, ends):
    return sum((positions >= e).astype(jnp.int32) for e in ends)


def row_ends(lengths):
    first = lengths[0, 0]
    second = first + lengths[0, 1]
    return (first, second, second + lengths[0, 2])


class Block:
    def __init__(self, b, ends):
        start = b * BLOCK
        rows = lax.broadcasted_iota(jnp.int32, (BLOCK, BLOCK), 0)
        columns = lax.broadcasted_iota(jnp.int32, (BLOCK, BLOCK), 1)
        seg_rows = segment_of(rows + start, ends)
        seg_columns = segment_of(columns + start, ends)
        same = seg_rows == seg_columns
        self.mask = jnp.logical_and(same, rows >= columns)
        self.mask_t = jnp.logical_and(same, columns >= rows)
        self.last = segment_of(start + BLOCK - 1, ends)
        self.earlier = segment_of(start - 1, ends) if b > 0 else -1
        wide_rows = lax.broadcasted_iota(jnp.int32, (BLOCK, HEAD_DIM), 0)
        segments = segment_of(wide_rows + start, ends)
        self.from_state = segments == self.earlier
        self.to_state = segments == self.last

    def decay(self, full):
        return jnp.where(self.mask, full, 0.0)

    def keeping(self, rate):
        factor = jnp.exp(jnp.full((HEAD_DIM, HEAD_DIM), -rate * BLOCK, F32))
        return jnp.where(self.last == self.earlier, factor, 0.0)


def full_decay(rate, turned=False):
    rows = lax.broadcasted_iota(jnp.int32, (BLOCK, BLOCK), int(turned))
    columns = lax.broadcasted_iota(jnp.int32, (BLOCK, BLOCK), 1 - int(turned))
    return jnp.exp(-rate * jnp.maximum(rows - columns, 0).astype(F32))


def edge_factors(rate):
    rows = lax.broadcasted_iota(jnp.int32, (BLOCK, HEAD_DIM), 0).astype(F32)
    return jnp.exp(-rate * (rows + 1.0)), jnp.exp(-rate * (BLOCK - 1.0 - rows))


def silu16(values):
    return (values * jax.nn.sigmoid(values)).astype(BF16)


def silu_grad(before):
    sigmoid = jax.nn.sigmoid(before)
    return sigmoid * (1.0 + before * (1.0 - sigmoid))


def entry_kernel(n, heads, order, core, lengths, rates, *refs):
    pieces, refs = refs[: n + 1], refs[n + 1 :]
    weights, mixer, refs = refs[:4], refs[4], refs[5:]
    normed_out, normed_send, proj_out, mixed_out, squares, states_out, refs = *refs[:6], refs[6:]
    parts, refs = refs[: n + 1], refs[n + 1 :]
    normed, weight_in, mixer_in, proj, mixed, pre, states, buffer, semaphores = refs
    copies = Copies(semaphores)
    rows = pieces[0].shape[0]
    total = n * rows
    width = heads * HEAD_DIM
    coming = fetch_pieces(
        copies, pieces, normed, lambda r: pl.multiple_of(order[0, r] * rows, rows)
    )
    for copy in coming:
        copy.wait()
    fetched = [copies.start(w, weight_in.at[i]) for i, w in enumerate(weights)]
    mixer_copy = copies.start(mixer, mixer_in)
    copies.write(normed, normed_out)
    copies.write(normed.at[:, other_half(core)], normed_send)
    for i in range(4):
        fetched[i].wait()
        for b in range(total // BLOCK):
            here = pl.ds(b * BLOCK, BLOCK)
            proj[here, i * width : (i + 1) * width] = dot(normed[here, :], weight_in[i])
    copies.write(proj, proj_out)
    ends = row_ends(lengths)
    fulls = [full_decay(rates[h]) for h in range(heads)]
    edges = [edge_factors(rates[h]) for h in range(heads)]
    state = [jnp.zeros((HEAD_DIM, HEAD_DIM), F32) for _ in range(heads)]
    ones = jnp.ones((8, HEAD_DIM), BF16)
    for b in range(total // BLOCK):
        here = pl.ds(b * BLOCK, BLOCK)
        block = Block(b, ends)
        square = jnp.zeros((8, BLOCK), F32)
        for h in range(heads):
            at = [slice(i * width + h * HEAD_DIM, i * width + (h + 1) * HEAD_DIM) for i in range(4)]
            query, key = silu16(proj[here, at[0]]), silu16(proj[here, at[1]])
            value = proj[here, at[2]].astype(BF16)
            inner, carried = edges[h]
            inner = jnp.where(block.from_state, inner, 0.0)
            carried = jnp.where(block.to_state, carried, 0.0)
            states[b, h] = state[h]
            weight = (dot(query, key, NT) * block.decay(fulls[h])).astype(BF16)
            high, low = split(state[h])
            out = dot(weight, value) + inner * (dot(query, high) + dot(query, low))
            state[h] = block.keeping(rates[h]) * state[h] + dot(
                (key.astype(F32) * carried).astype(BF16), value, TN
            )
            mixed[here, at[0]] = out
            pre[here, at[0]] = (out * proj[here, at[3]]).astype(BF16)
            high, low = split(out * out)
            square += dot(ones, high, NT) + dot(ones, low, NT)
        squares[:, here] = square[0:1]
    copies.write(mixed, mixed_out)
    copies.write(states, states_out)
    mixer_copy.wait()
    for r in reversed(range(0, n, 2)):
        both = jnp.concatenate(
            [pre[pl.ds(pl.multiple_of(order[0, q] * rows, rows), rows), :] for q in (r, r + 1)], 0
        )
        buffer[r * rows : (r + 2) * rows, :] = dot(both, mixer_in[...]).astype(BF16)
        write_part(copies, buffer, parts, r + 1)
        write_part(copies, buffer, parts, r)
    copies.drain()


def column(row):
    return jnp.transpose(jnp.broadcast_to(row, (HEAD_DIM, row.shape[1])))


def exit_kernel(n, heads, order, core, lengths, rates, *refs):
    pieces, refs = refs[: n + 1], refs[n + 1 :]
    weights, mixer_hbm, refs = refs[:4], refs[4], refs[5:]
    proj_hbm, mixed_hbm, states_hbm, inverses, refs = *refs[:4], refs[4:]
    entry_out, send_out, keep_out, refs = *refs[:3], refs[3:]
    parts, refs = refs[: n + 1], refs[n + 1 :]
    resid, weight_in, mixer, proj, mixed, states, scaled, entry_g, scaled_g, buffer, send, keep, sems = refs
    copies = Copies(sems)
    rows = pieces[0].shape[0]
    total = n * rows
    width = heads * HEAD_DIM
    mixer_copy = copies.start(mixer_hbm, mixer)
    coming = fetch_pieces(
        copies, pieces, resid, lambda r: pl.multiple_of(order[0, r] * rows, rows)
    )
    mixer_copy.wait()
    for copy in coming:
        copy.wait()
    saved = [
        copies.start(a, b)
        for a, b in ((proj_hbm, proj), (mixed_hbm, mixed), (states_hbm, states))
    ]
    fetched = [
        copies.start(w, weight_in.at[:, i * width : (i + 1) * width]) for i, w in enumerate(weights)
    ]
    for b in range(total // BLOCK):
        here = pl.ds(b * BLOCK, BLOCK)
        scaled_g[here, :] = dot(resid[here, :D], mixer[...], NT)
    for copy in saved:
        copy.wait()
    ends = row_ends(lengths)
    fulls = [full_decay(rates[h]) for h in range(heads)]
    turned = [full_decay(rates[h], True) for h in range(heads)]
    edges = [edge_factors(rates[h]) for h in range(heads)]
    later = [jnp.zeros((HEAD_DIM, HEAD_DIM), F32) for _ in range(heads)]
    for b in reversed(range(total // BLOCK)):
        here = pl.ds(b * BLOCK, BLOCK)
        block = Block(b, ends)
        inverse = column(inverses[:, here])
        coded = resid[here, D : D + 128].astype(F32)
        mean = (coded[:, 0:1] + coded[:, 1:2] + coded[:, 2:3]) * (1.0 / D)
        for h in range(heads):
            at = [slice(i * width + h * HEAD_DIM, i * width + (h + 1) * HEAD_DIM) for i in range(4)]
            query_pre, key_pre = proj[here, at[0]], proj[here, at[1]]
            query, key = silu16(query_pre), silu16(key_pre)
            value = proj[here, at[2]].astype(BF16)
            gate = proj[here, at[3]]
            grad_s = scaled_g[here, at[0]]
            unit = mixed[here, at[0]] * inverse
            scaled[here, at[0]] = (unit * gate).astype(BF16)
            entry_g[here, at[3]] = (grad_s * unit).astype(BF16)
            grad = (inverse * (grad_s * gate - unit * mean)).astype(BF16)
            inner, carried = edges[h]
            inner = jnp.where(block.from_state, inner, 0.0)
            carried = jnp.where(block.to_state, carried, 0.0)
            decay = block.decay(fulls[h])
            decay_t = jnp.where(block.mask_t, turned[h], 0.0)
            weight_t = (dot(key, query, NT) * decay_t).astype(BF16)
            score = (dot(grad, value, NT) * decay).astype(BF16)
            score_t = (dot(value, grad, NT) * decay_t).astype(BF16)
            high, low = split(states[b, h])
            query_g = dot(score, key) + inner * (dot(grad, high, NT) + dot(grad, low, NT))
            high, low = split(later[h])
            key_g = dot(score_t, query) + carried * (dot(value, high, NT) + dot(value, low, NT))
            value_g = dot(weight_t, grad) + carried * (dot(key, high) + dot(key, low))
            later[h] = (
                dot((query.astype(F32) * inner).astype(BF16), grad, TN)
                + block.keeping(rates[h]) * later[h]
            )
            entry_g[here, at[0]] = (query_g * silu_grad(query_pre)).astype(BF16)
            entry_g[here, at[1]] = (key_g * silu_grad(key_pre)).astype(BF16)
            entry_g[here, at[2]] = value_g.astype(BF16)
    copies.write(entry_g, entry_out)
    send[...] = dot(scaled[...], resid[:, other_half(core)], TN).astype(BF16)
    copies.write(send, send_out)
    keep[...] = dot(scaled[...], resid[:, own_half(core)], TN)
    copies.write(keep, keep_out)
    for copy in fetched:
        copy.wait()
    for r in reversed(range(0, n, 2)):
        both = jnp.concatenate(
            [entry_g[pl.ds(pl.multiple_of(order[0, q] * rows, rows), rows), :] for q in (r, r + 1)],
            0,
        )
        buffer[r * rows : (r + 2) * rows, :] = dot(both, weight_in[...], NT).astype(BF16)
        write_part(copies, buffer, parts, r + 1)
        write_part(copies, buffer, parts, r)
    copies.drain()


def cotangent_kernel(n, core, *refs):
    pieces, down, grad, grad_send, *products = refs[: n + 1], *refs[n + 1 :]
    rows = pieces[0].shape[0]
    assemble(pieces, grad, lambda r: r * rows)
    grad_send[...] = grad[:, other_half(core)]
    for r, out in enumerate(products):
        out[...] = dot(grad[pl.ds(2 * r * rows, 2 * rows), :], down[...], NT)


def hidden_kernel(index, halved, core, *refs):
    count = 2 + halved
    pieces, refs = refs[:count], refs[count:]
    first, second, product_g, refs = *refs[:3], refs[3:]
    refs = refs if index == 0 else refs[4:]
    (normed_out, product_out, second_out, bundle), refs = refs[:4], refs[4:]
    parts, refs = refs[:count], refs[count:]
    normed, product, first_g, second_g, sems = refs
    copies = Copies(sems)
    low = 0
    for piece in pieces:
        normed[low : low + piece.shape[0], :] = piece[...]
        low += piece.shape[0]
    units, padded = first.shape[0], product.shape[1]
    if padded > units:
        for ref in (product, first_g, second_g):
            ref[:, units:] = jnp.zeros((low, padded - units), BF16)
    here = pl.ds(index * low, low)
    copies.write(normed, normed_out.at[here, :])
    copies.write(normed.at[:, other_half(core)], bundle.at[here, pl.ds(padded, D // 2)])
    tokens = normed[...]
    first_act, second_act = dot(tokens, first[...], NT), dot(tokens, second[...], NT)
    product[:, :units] = (first_act * second_act).astype(BF16)
    copies.write(product, product_out.at[here, :])
    grad = product_g[...]
    one, two = (grad * second_act).astype(BF16), (grad * first_act).astype(BF16)
    first_g[:, :units] = one
    copies.write(first_g, bundle.at[here, pl.ds(0, padded)])
    second_g[:, :units] = two
    copies.write(second_g, second_out.at[here, :])
    result = (dot(one, first[...]) + dot(two, second[...])).astype(BF16)
    low = 0
    for part in parts:
        part[...] = result[low : low + part.shape[0]]
        low += part.shape[0]
    copies.drain()


def down_kernel(n, product, down, *parts):
    rows, units = parts[0].shape[0], down.shape[0]
    for r in range(0, n, 2):
        result = dot(product[pl.ds(r * rows, 2 * rows), :units], down[...]).astype(BF16)
        store_part(parts, r, result[:rows])
        store_part(parts, r + 1, result[rows:])


def resid_kernel(low, grad, hidden, near, left, right, attn, hidden_g, coded):
    rows = grad.shape[0]
    here = slice(low, low + rows)
    normed_g = near[...].astype(F32) + left[here, :].astype(F32) + right[here, :].astype(F32)
    whole = grad[...].astype(F32) + norm_grad(hidden[...], normed_g)
    hidden_g[...] = whole
    resid = whole.astype(BF16)
    coded[:, :D] = resid
    inner = jnp.sum(resid.astype(F32) * attn[...], axis=1, keepdims=True)
    lane = lax.broadcasted_iota(jnp.int32, (1, 128), 1)
    out = jnp.zeros((rows, 128), F32)
    for i in range(3):
        high = inner.astype(BF16).astype(F32)
        out += jnp.where(lane == i, high, 0.0)
        inner -= high
    coded[:, D:] = out.astype(BF16)


def output_kernel(tokens, attn, ffn, valid_rows, output, sums):
    rows = tokens.shape[0]
    valid = lax.broadcasted_iota(jnp.int32, (rows, 1), 0) < valid_rows[0]
    tokens_wide = tokens[...].astype(F32)
    output[...] = (tokens_wide + attn[...] + ffn[...]).astype(BF16)
    lane = lax.broadcasted_iota(jnp.int32, (1, 128), 1)
    out = jnp.zeros((1, 128), F32)
    for i, values in enumerate((tokens_wide, attn[...], ffn[...])):
        per_row = jnp.sum(values * values, axis=1, keepdims=True)
        whole = jnp.sum(jnp.where(valid, per_row, 0.0), axis=0, keepdims=True)
        out += jnp.where(lane == i, whole, 0.0)
    counted = jnp.clip(valid_rows[0], 0, rows).astype(F32)
    sums[...] = out + jnp.where(lane == 3, counted, 0.0)


def local(
    tokens_in,
    query_weight,
    key_weight,
    value_weight,
    gate_weight,
    mixer_weight,
    first_weight,
    second_weight,
    down_weight,
    doc_lengths,
    head_decay,
    out_grad,
):
    n = lax.axis_size("narrow")
    rows = tokens_in.shape[0]
    total = rows * n
    heads = head_decay.shape[0]
    width = heads * HEAD_DIM
    units = first_weight.shape[1]
    me = lax.axis_index("narrow")
    core = lax.axis_index("wide") % 2
    start_row = me * rows
    order = lax.dynamic_slice(jnp.asarray(order_table(n)), (me, 0), (1, n))
    where = core.reshape(1)
    entry_weights = (query_weight, key_weight, value_weight, gate_weight)
    tokens_wide = tokens_in.astype(F32)
    rates = head_decay

    half_rows = total // 2
    blocks = total // BLOCK
    first_t, second_t = first_weight.T, second_weight.T
    valid_rows = (jnp.sum(doc_lengths[0, : NDOC - 1]) - start_row).reshape(1)

    pieces = Gather(normalize(tokens_wide).astype(BF16), n).finish()
    shapes = [
        ((total, D), BF16),
        ((total, D // 2), BF16),
        ((total, 4 * width), F32),
        ((total, width), F32),
        ((1, total), F32),
        ((blocks, heads, HEAD_DIM, HEAD_DIM), F32),
    ] + part_shapes(n, rows)
    *pieces, grad_own = barrier(*pieces, out_grad)
    cotangent = Gather(grad_own, n).step()
    normed, normed_send, proj, mixed, squares, states, *parts = call(
        functools.partial(entry_kernel, n, heads),
        shapes,
        [SMEM] * 4 + [ANY] * (n + 6),
        12 * total * D * width,
        48 * MIB,
        [
            pltpu.VMEM((total, D), BF16),
            pltpu.VMEM((4, D, width), BF16),
            pltpu.VMEM((width, D), BF16),
            pltpu.VMEM((total, 4 * width), F32),
            pltpu.VMEM((total, width), F32),
            pltpu.VMEM((total, width), BF16),
            pltpu.VMEM((blocks, heads, HEAD_DIM, HEAD_DIM), F32),
            pltpu.VMEM((total, D), BF16),
            pltpu.SemaphoreType.DMA((2 * n + 13,)),
        ],
        [VMEM if i == 4 else ANY for i in range(len(shapes))],
    )(order, where, doc_lengths, rates, *pieces, *entry_weights, mixer_weight)
    squares, cotangent.left, cotangent.right, *parts = barrier(
        squares, cotangent.left, cotangent.right, *parts
    )
    scatter = Scatter(parts, n)
    hop = Butterfly(squares, "narrow")
    while cotangent.left_steps:
        scatter.step()
        cotangent.step()
        hop.step()
        meet(scatter, cotangent, hop)
    squares = hop.finish()
    grad_pieces = cotangent.pieces
    attn_raw = scatter.finish()
    inverses = lax.rsqrt(squares / D + EPS)
    inverse_own = lax.dynamic_slice(inverses, (0, start_row), (1, rows)).reshape(rows, 1)
    attn_own = attn_raw * inverse_own
    hidden_own = tokens_wide + attn_own

    padded = -(-units // 128) * 128

    def hidden(index, pieces):
        halved = len(pieces) == 3
        count = len(pieces)
        outs = call(
            functools.partial(hidden_kernel, index, halved),
            [((total, D), BF16)]
            + [((total, padded), BF16)] * 2
            + [((total, padded + D // 2), BF16)]
            + [(p.shape, BF16) for p in pieces],
            [SMEM] + [VMEM] * (count + 3) + [ANY] * len(whole),
            16 * rows * D * units,
            40 * MIB,
            [pltpu.VMEM((2 * rows, D), BF16)]
            + [pltpu.VMEM((2 * rows, padded), BF16)] * 3
            + [pltpu.SemaphoreType.DMA((5,))],
            [ANY] * 4 + [VMEM] * count,
            {count + 4 + i: i for i in range(len(whole))},
        )(where, *pieces, first_t, second_t, product_g[index], *whole)
        return outs[:4], list(outs[4:])

    gather = Gather(normalize(hidden_own).astype(BF16), n)
    *grad_pieces, gather.left = barrier(*grad_pieces, gather.left)
    gather.right = gather.left
    gather.step()
    grad_all, grad_send, *product_g = call(
        functools.partial(cotangent_kernel, n),
        [((total, D), BF16), ((total, D // 2), BF16)] + [((2 * rows, units), F32)] * (n // 2),
        [SMEM] + [VMEM] * (n + 2),
        2 * total * D * units,
        22 * MIB,
    )(where, *grad_pieces, down_weight)
    gather.left, gather.right, grad_send, normed_send, *product_g = barrier(
        gather.left, gather.right, grad_send, normed_send, *product_g
    )
    normed_other = swap(normed_send, "wide", 1)
    whole, parts = [], []
    for i in range(n // 2 - 1):
        pieces = gather.pieces[2 * i : 2 * i + 2]
        gather.step()
        whole, new_parts = hidden(i, pieces)
        if gather.left_steps:
            gather.left, gather.right, normed_other, *new_parts = barrier(
                gather.left, gather.right, normed_other, *new_parts
            )
        parts += new_parts
    grad_other = swap(grad_send, "wide", 1)
    pieces = barrier(*gather.pieces[n - 2 :], grad_other)
    grad_other = pieces[-1]
    whole, new_parts = hidden(n // 2 - 1, pieces[:-1])
    parts += new_parts
    normed2, product, second_g, bundle = whole

    scatter = Scatter(parts, n)
    stream = Together(scatter)
    half = D // 2
    cut_at = [(0, 384, 768, half), (0, 256, 640, half), (0, 384, 896, half)]
    cuts = [tuple(zip(at[:-1], at[1:])) for at in cut_at]

    (product_other, bundle_other), _ = region(
        [stream], [(product, "wide", 1), (bundle, "wide", 1)]
    )
    (second_other_g,), down_own = region(
        [stream],
        [(second_g, "wide", 1)],
        lambda *v: own_columns(core, cuts[0], units, *v),
        [product, product_other, grad_all, grad_other],
    )
    down_in, first_in, second_in = [], [], []
    (received,), first_own = region(
        [stream],
        [(down_own[0], "wide", 2)],
        lambda *v: own_columns(core, cuts[1], units, *v, v[1], low=padded),
        [bundle, bundle_other, normed2],
    )
    down_in.append(received)
    (received,), second_own = region(
        [stream],
        [(down_own[1], "wide", 2)],
        lambda *v: own_columns(core, cuts[2], units, *v, low=padded),
        [second_g, second_other_g, normed2, bundle_other],
    )
    down_in.append(received)
    while scatter.left_steps:
        region([stream])
    left, right, low, _ = scatter.received
    hidden_g, resid_own = call(
        functools.partial(resid_kernel, low),
        [((rows, D), F32), ((rows, D + 128), BF16)],
        [VMEM] * 6,
        20 * rows * D,
        14 * MIB,
    )(out_grad, hidden_own, scatter.near[0], left, right, attn_own)

    gather = Gather(resid_own, n)

    def mixed_pairs(owns, ins):
        return [v for pair in zip(owns, ins) for v in pair]

    def output_parts(product):
        return call(
            functools.partial(down_kernel, n),
            part_shapes(n, rows),
            [VMEM] * 2,
            2 * total * D * units,
            14 * MIB,
        )(product, down_weight)

    (received, received2), parts = region(
        [gather],
        [(down_own[2], "wide", 2), (first_own[0], "wide", 2)],
        output_parts,
        [product],
    )
    down_in.append(received)
    first_in.append(received2)
    (received,), down_total = region(
        [gather], [(first_own[1], "wide", 2)], summed, mixed_pairs(down_own, down_in)
    )
    first_in.append(received)
    (received, down_other), _ = region(
        [gather], [(first_own[2], "wide", 2), (down_total, "wide", 1)]
    )
    first_in.append(received)
    while gather.left_steps > 1:
        region([gather])
    scatter2 = Scatter(parts, n)
    stream2 = Together(scatter2)
    (received,), first_total = region(
        [gather, stream2],
        [(second_own[0], "wide", 2)],
        summed,
        mixed_pairs(first_own, first_in),
    )
    second_in.append(received)

    shapes = [
        ((total, 4 * width), BF16),
        ((width, D // 2), BF16),
        ((width, D // 2), F32),
    ] + part_shapes(n, rows)
    leave = call(
        functools.partial(exit_kernel, n, heads),
        shapes,
        [SMEM] * 4 + [ANY] * (n + 9) + [VMEM],
        12 * total * D * width,
        56 * MIB,
        [
            pltpu.VMEM((total, D + 128), BF16),
            pltpu.VMEM((D, 4 * width), BF16),
            pltpu.VMEM((width, D), BF16),
            pltpu.VMEM((total, 4 * width), F32),
            pltpu.VMEM((total, width), F32),
            pltpu.VMEM((blocks, heads, HEAD_DIM, HEAD_DIM), F32),
            pltpu.VMEM((total, width), BF16),
            pltpu.VMEM((total, 4 * width), BF16),
            pltpu.VMEM((total, width), F32),
            pltpu.VMEM((total, D), BF16),
            pltpu.VMEM((width, D // 2), BF16),
            pltpu.VMEM((width, D // 2), F32),
            pltpu.SemaphoreType.DMA((2 * n + 15,)),
        ],
        [ANY] * len(shapes),
    )
    (received, first_other), (entry_g, mixer_send, mixer_keep, *parts) = region(
        [stream2],
        [(second_own[1], "wide", 2), (first_total, "wide", 1)],
        lambda inverses, *pieces: leave(
            order,
            where,
            doc_lengths,
            rates,
            *pieces,
            *entry_weights,
            mixer_weight,
            proj,
            mixed,
            states,
            inverses,
        ),
        [inverses, *gather.pieces],
    )
    second_in.append(received)

    scatter = Scatter(parts, n)
    stream = Together(scatter2, scatter)

    def mixer_work(keep, crossed_send, entry_g, normed, normed_other, *placed):
        (mixer_own,) = call(
            add_kernel, [(keep.shape, BF16)], [VMEM] * 2, keep.size, 14 * MIB
        )(keep, swap(crossed_send, "wide", 1))
        mixer_in = swap(mixer_own, "wide", 2)
        entry_other = swap(entry_g, "wide", 1)
        owns = own_rows(core, 2, 2, width, normed, normed_other, entry_g, entry_other)
        down_w = place(core, *placed[:2], False)
        first_w = place(core, *placed[2:], False)
        return mixer_own, mixer_in, owns, entry_other, down_w, first_w

    (received,), work_out = region(
        [stream],
        [(second_own[2], "wide", 2)],
        mixer_work,
        [mixer_keep, mixer_send, entry_g, normed, normed_other]
        + [down_total, down_other, first_total, first_other],
    )
    second_in.append(received)
    mixer_own, mixer_in, (value_own, gate_own), entry_other, down_w, first_w = work_out

    def entry_work(normed, normed_other, entry_g, entry_other, *pairs):
        owns = own_rows(core, 0, 2, width, normed, normed_other, entry_g, entry_other)
        return owns, summed(*pairs[:2]), summed(*pairs[2:])

    (gate_in, value_in), ((query_own, key_own), mixer_total, second_total) = region(
        [stream],
        [(gate_own, "wide", 2), (value_own, "wide", 2)],
        entry_work,
        [normed, normed_other, entry_g, entry_other, mixer_own, mixer_in]
        + mixed_pairs(second_own, second_in),
    )
    while scatter2.left_steps:
        region([stream])
    ffn_own = scatter2.result
    stream = Together(scatter)

    def output_work(tokens_in, attn_own, ffn_own, a, b, c, d):
        output, stats = call(
            output_kernel,
            [((rows, D), BF16), ((1, 128), F32)],
            [VMEM] * 3 + [SMEM],
            6 * rows * D,
            14 * MIB,
        )(tokens_in, attn_own, ffn_own, valid_rows)
        return output, stats + swap(stats, "narrow", 1), summed(a, b), summed(c, d)

    (key_in, second_other), (output, stats, gate_total, value_total) = region(
        [stream],
        [(key_own, "wide", 2), (second_total, "wide", 1)],
        output_work,
        [tokens_in, attn_own, ffn_own, gate_own, gate_in, value_own, value_in],
    )
    (query_in, mixer_other, hop), (second_w, key_total) = region(
        [stream],
        [(query_own, "wide", 2), (mixer_total, "wide", 1), (stats, "narrow", 2)],
        lambda own, other, *v: (place(core, own, other, False), summed(*v)),
        [second_total, second_other, key_own, key_in],
    )
    stats = stats + hop
    while scatter.left_steps:
        region([stream])
    normed_g = scatter.result

    (gate_other, value_other, key_other, hop), (query_total, mixer_w) = region(
        [],
        [(v, "wide", 1) for v in (gate_total, value_total, key_total)] + [(stats, "narrow", 4)],
        lambda a, b, *v: (summed(a, b), place(core, *v, False)),
        [query_own, query_in, mixer_total, mixer_other],
    )
    stats = stats + hop
    query_other = swap(query_total, "wide", 1)
    for axis, bit in (("narrow", 8), ("wide", 1)):
        while bit < lax.axis_size(axis):
            stats = stats + swap(stats, axis, bit)
            bit *= 2
    gate_w = place(core, gate_total, gate_other, True)
    input_grad = hidden_g + norm_grad(tokens_wide, normed_g)
    value_w = place(core, value_total, value_other, True)
    key_w = place(core, key_total, key_other, True)
    query_w = place(core, query_total, query_other, True)
    stream_rms = jnp.sqrt(stats[0, :3] / (stats[0, 3] * D))
    return (
        output,
        input_grad,
        query_w,
        key_w,
        value_w,
        gate_w,
        mixer_w,
        first_w.T,
        second_w.T,
        down_w,
        stream_rms,
    )


def solution(mesh):
    split_tokens = P(("wide", "narrow"), None)
    columns, rows = P(None, "narrow"), P("narrow", None)
    return jax.shard_map(
        local,
        mesh=mesh,
        in_specs=(split_tokens,)
        + (columns,) * 4
        + (rows, columns, columns, rows, P("wide", None), P("narrow"), split_tokens),
        out_specs=(split_tokens,) * 2 + (columns,) * 4 + (rows, columns, columns, rows, P()),
        check_vma=False,
    )
```

```python
import functools

import jax
import jax.numpy as jnp
import numpy as np
from jax import lax
from jax.experimental import pallas as pl
from jax.experimental.pallas import tpu as pltpu
from jax.sharding import PartitionSpec as P

D = 2048
HEAD_DIM = 128
NDOC = 4
EPS = 1e-06
BLOCK = 256
MIB = 1 << 20

F32 = jnp.float32
BF16 = jnp.bfloat16
NN = (((1,), (0,)), ((), ()))
NT = (((1,), (1,)), ((), ()))
TN = (((0,), (0,)), ((), ()))
VMEM = pl.BlockSpec(memory_space=pltpu.VMEM)
SMEM = pl.BlockSpec(memory_space=pltpu.SMEM)
ANY = pl.BlockSpec(memory_space=pl.ANY)


def dot(a, b, dims=NN):
    return lax.dot_general(a, b, dims, preferred_element_type=F32)


def split(values):
    high = values.astype(BF16)
    return high, (values - high.astype(F32)).astype(BF16)


def normalize(values):
    return values * lax.rsqrt(jnp.mean(values * values, axis=-1, keepdims=True) + EPS)


def norm_grad(values, grad_in):
    inverse = lax.rsqrt(jnp.mean(values * values, axis=-1, keepdims=True) + EPS)
    normed = values * inverse
    return inverse * (grad_in - normed * jnp.mean(grad_in * normed, axis=-1, keepdims=True))


def ring_order(n):
    if n == 16:
        return [r * 4 + (c if r % 2 == 0 else 3 - c) for r in range(4) for c in range(4)]
    return list(range(0, n, 2)) + list(range(n - 1, 0, -2))


def distances(n):
    out = [0]
    for k in range(1, n // 2):
        out += [-k, k]
    return out + [n // 2]


def order_table(n):
    ring = ring_order(n)
    place = {device: i for i, device in enumerate(ring)}
    return np.array(
        [[ring[(place[me] + d) % n] for d in distances(n)] for me in range(n)], np.int32
    )


def onward(values, n):
    ring = ring_order(n)
    return lax.ppermute(values, "narrow", [(ring[i], ring[(i + 1) % n]) for i in range(n)])


def backward(values, n):
    ring = ring_order(n)
    return lax.ppermute(values, "narrow", [(ring[(i + 1) % n], ring[i]) for i in range(n)])


def barrier(*values):
    return lax.optimization_barrier(values)


def add16(a, b):
    return (a.astype(F32) + b.astype(F32)).astype(BF16)


class Gather:
    def __init__(self, own, n):
        self.n, self.left_steps = n, n // 2
        self.left = self.right = own
        self.pieces = [own]

    def outgoing(self):
        if self.left_steps == 1:
            half = self.left.shape[0] // 2
            return self.left[:half], self.right[half:]
        return self.left, self.right

    def incoming(self, left, right):
        self.left_steps -= 1
        self.left, self.right = left, right
        self.pieces += [left, right]

    def step(self, count=1):
        for _ in range(count):
            left, right = self.outgoing()
            self.incoming(onward(left, self.n), backward(right, self.n))
        return self

    def finish(self):
        return self.step(self.left_steps).pieces


class Gather2:
    def __init__(self, halves, n):
        self.n, self.left_steps = n, n // 2
        self.left, self.right = list(halves), list(halves)
        self.pieces = [list(halves)]

    def step(self, count=1):
        for _ in range(count):
            self.left_steps -= 1
            if self.left_steps == 0:
                self.pieces.append([onward(self.left[0], self.n), backward(self.right[1], self.n)])
                return self
            for i in range(2):
                self.left[i] = onward(self.left[i], self.n)
                self.right[i] = backward(self.right[i], self.n)
            self.pieces += [list(self.left), list(self.right)]
        return self

    def finish(self):
        return self.step(self.left_steps).pieces


def merge_kernel(layout, *refs):
    outs, refs = refs[-2:], list(refs[:-2])
    at = 0
    for rows, half, offset in layout:
        if offset is None:
            for out in outs:
                out[at : at + rows] = refs.pop(0)[...]
        else:
            nears, parts, refs = refs[:2], refs[2:4], refs[4:]
            for i in range(2):
                low = half * i if half < rows else 0
                outs[i][at : at + rows] = nears[i][...]
                outs[i][at + low : at + low + half] = add16(
                    nears[i][low : low + half], parts[i][offset : offset + half]
                )
        at += rows


def join_one(low, near, part, out):
    rows = part.shape[0]
    out[...] = near[...]
    out[low : low + rows] = add16(near[low : low + rows], part[...])


class Scatter:
    def __init__(self, parts, n):
        self.n, self.left_steps = n, n // 2
        self.near = {d: parts[i] for i, d in enumerate(distances(n)[:-1])}
        self.left, self.right = parts[-2], parts[-1]
        self.received = None

    def operands(self):
        if self.received is None:
            return [self.left, self.right], (self.left.shape[0], 0, None)
        left, right, offset, half = self.received
        near = [self.near[self.left_steps], self.near[-self.left_steps]]
        return near + [left, right], (near[0].shape[0], half, offset)

    def take(self, left, right, offset, rows):
        self.left_steps -= 1
        if self.left_steps == 0:
            at = slice(offset, offset + rows)
            self.result = self.near[0].astype(F32) + left[at].astype(F32) + right[at].astype(F32)
        self.received = (left, right, offset, rows)

    def step(self, count=1):
        for _ in range(count):
            self.left_steps -= 1
            left, right = onward(self.left, self.n), backward(self.right, self.n)
            k = self.left_steps
            shape = self.near[k].shape
            if k == 0:
                self.result = (self.near[0], left, right)
            elif shape == left.shape:
                self.left, self.right = add16(self.near[k], left), add16(self.near[-k], right)
            else:
                half = shape[0] // 2
                self.left, self.right = [
                    call(
                        functools.partial(join_one, low),
                        [(shape, BF16)],
                        [VMEM] * 2,
                        shape[0] * shape[1],
                        14 * MIB,
                    )(near, part)[0]
                    for low, near, part in ((0, self.near[k], left), (half, self.near[-k], right))
                ]
        return self

    def finish(self):
        return self.step(self.left_steps).result


class Together:
    def __init__(self, *scatters):
        self.scatters, self.n = scatters, scatters[0].n

    def outgoing(self):
        operands, self.layout = [], []
        for s in self.scatters:
            values, layout = s.operands()
            operands += values
            self.layout.append(layout)
        if len(self.layout) == 1 and self.layout[0][2] is None:
            return operands
        rows = sum(entry[0] for entry in self.layout)
        return call(
            functools.partial(merge_kernel, tuple(self.layout)),
            [((rows, D), BF16)] * 2,
            [VMEM] * len(operands),
            2 * rows * D,
            14 * MIB,
        )(*operands)

    def incoming(self, left, right):
        offset = 0
        for s, (rows, _, _) in zip(self.scatters, self.layout):
            s.take(left, right, offset, rows)
            offset += rows


def region(streams=(), swaps=(), work=None, inputs=()):
    out = [v for s in streams for v in s.outgoing()]
    count = len(out)
    values, inputs = lax.optimization_barrier((out + [s[0] for s in swaps], list(inputs)))
    moved = [
        onward(v, streams[0].n) if i % 2 == 0 else backward(v, streams[0].n)
        for i, v in enumerate(values[:count])
    ]
    moved += [swap(v, s[1], s[2]) for v, s in zip(values[count:], swaps)]
    results = work(*inputs) if work else ()
    moved, results = lax.optimization_barrier((moved, results))
    for i, s in enumerate(streams):
        s.incoming(*moved[2 * i : 2 * i + 2])
    return moved[count:], results


def meet(*streams):
    values = barrier(*[v for s in streams for v in (s.left, s.right)])
    for i, s in enumerate(streams):
        s.left, s.right = values[2 * i : 2 * i + 2]


def swap(values, axis, bit):
    size = lax.axis_size(axis)
    return lax.ppermute(values, axis, [(i, i ^ bit) for i in range(size)])


class Butterfly:
    def __init__(self, values, axis):
        self.left, self.right, self.axis, self.bit = values, jnp.zeros((1, 128), F32), axis, 1

    def step(self):
        if self.bit < lax.axis_size(self.axis):
            self.left = self.left + swap(self.left, self.axis, self.bit)
            self.bit *= 2
        return self

    def finish(self):
        while self.bit < lax.axis_size(self.axis):
            self.step()
        return self.left


def ladder(values, bit=4):
    while bit < lax.axis_size("wide"):
        values = add16(values, swap(values, "wide", bit))
        bit *= 2
    return values


def own_half(core):
    return pl.ds(pl.multiple_of(core[0] * (D // 2), D // 2), D // 2)


def columns_kernel(cuts, lefts, rights, core, *refs):
    sources, outs, refs = refs[:4], refs[4 : 4 + len(cuts)], refs[4 + len(cuts) :]
    left, left_other, right, right_other, semaphores = refs
    width = outs[0].shape[0]
    columns = right.shape[1]
    copies = Copies(semaphores)
    coming = [
        copies.start(sources[1].at[:, pl.ds(lefts[1], left.shape[1])], left_other),
        copies.start(sources[3].at[:, pl.ds(rights[1], columns)], right_other),
        copies.start(sources[0].at[:, pl.ds(lefts[0], left.shape[1])], left),
    ]
    if rights[0] is None:
        coming.append(copies.start(sources[2].at[:, own_half(core)], right))
    else:
        coming.append(copies.start(sources[2].at[:, pl.ds(rights[0], columns)], right))
    coming[0].wait()
    coming[1].wait()
    part = dot(left_other[:, :width], right_other[...], TN)
    coming[2].wait()
    coming[3].wait()
    part += dot(left[:, :width], right[...], TN)
    for out, (low, high) in zip(outs, cuts):
        out[...] = part[:, low:high].astype(BF16)


def own_columns(core, cuts, width, left, left_other, right, right_other, lefts=(0, 0), low=0):
    total = left.shape[0]
    padded = -(-width // 128) * 128
    return call(
        functools.partial(columns_kernel, cuts, lefts, (None, low)),
        [((width, high - low), BF16) for low, high in cuts],
        [SMEM] + [ANY] * 4,
        2 * total * D * width,
        54 * MIB,
        [pltpu.VMEM((total, padded), BF16)] * 2
        + [pltpu.VMEM((total, D // 2), BF16)] * 2
        + [pltpu.SemaphoreType.DMA((4,))],
    )(core.reshape(1), left, left_other, right, right_other)


def rows_kernel(first, core, *refs):
    sources, refs = refs[:4], refs[4:]
    outs, (normed, normed_other, grads, grads_other, semaphores) = refs[:-5], refs[-5:]
    width = outs[0].shape[1]
    columns = pl.ds(first * width, len(outs) * width)
    copies = Copies(semaphores)
    coming = [
        copies.start(sources[1], normed_other),
        copies.start(sources[3].at[:, columns], grads_other),
        copies.start(sources[0].at[:, own_half(core)], normed),
        copies.start(sources[2].at[:, columns], grads),
    ]
    coming[0].wait()
    coming[1].wait()
    part = dot(normed_other[...], grads_other[...], TN)
    coming[2].wait()
    coming[3].wait()
    part += dot(normed[...], grads[...], TN)
    for i, out in enumerate(outs):
        out[...] = part[:, i * width : (i + 1) * width].astype(BF16)


def own_rows(core, first, count, width, normed, normed_other, bundle, bundle_other):
    total = normed.shape[0]
    return call(
        functools.partial(rows_kernel, first),
        [((D // 2, width), BF16)] * count,
        [SMEM] + [ANY] * 4,
        2 * total * D * width * count,
        54 * MIB,
        [pltpu.VMEM((total, D // 2), BF16)] * 2
        + [pltpu.VMEM((total, count * width), BF16)] * 2
        + [pltpu.SemaphoreType.DMA((4,))],
    )(core.reshape(1), normed, normed_other, bundle, bundle_other)


def add_kernel(keep, crossed, out):
    out[...] = (keep[...] + crossed[...].astype(F32)).astype(BF16)


def sum_kernel(*refs):
    out, low = refs[-1], 0
    for i in range(len(refs) // 2):
        width = refs[2 * i].shape[1]
        out[:, low : low + width] = add16(refs[2 * i][...], refs[2 * i + 1][...])
        low += width


def summed(*values):
    rows = values[0].shape[0]
    columns = sum(v.shape[1] for v in values[::2])
    return ladder(
        call(
            sum_kernel,
            [((rows, columns), BF16)],
            [VMEM] * len(values),
            rows * columns,
            14 * MIB,
        )(*values)[0]
    )


def place(core, own, other, row_halves):
    rows, columns = own.shape
    return call(
        functools.partial(place_kernel, row_halves),
        [((2 * rows, columns) if row_halves else (rows, 2 * columns), F32)],
        [SMEM] + [VMEM] * 2,
        rows * columns,
        14 * MIB,
    )(core.reshape(1), own, other)[0]


def place_two(core, own, other):
    rows, columns = own.shape
    return call(
        place_two_kernel,
        [((2 * rows, columns // 2), F32)] * 2,
        [SMEM] + [VMEM] * 2,
        rows * columns,
        14 * MIB,
    )(core.reshape(1), own, other)


def place_two_kernel(core, own, other, *outs):
    rows, columns = own.shape[0], outs[0].shape[1]
    for where, ref in ((core[0], own), (1 - core[0], other)):
        here = pl.ds(pl.multiple_of(where * rows, 128), rows)
        for i, out in enumerate(outs):
            out[here, :] = ref[:, i * columns : (i + 1) * columns].astype(F32)


def place_kernel(row_halves, core, own, other, out):
    rows, columns = own.shape
    for where, ref in ((core[0], own), (1 - core[0], other)):
        if row_halves:
            out[pl.ds(pl.multiple_of(where * rows, 128), rows), :] = ref[...].astype(F32)
        else:
            out[:, pl.ds(pl.multiple_of(where * columns, 128), columns)] = ref[...].astype(F32)


def call(kernel, outs, in_specs, flops, limit, scratch=(), out_specs=None, aliases=None):
    return pl.pallas_call(
        kernel,
        out_shape=[jax.ShapeDtypeStruct(s, d) for s, d in outs],
        in_specs=in_specs,
        out_specs=out_specs or [VMEM] * len(outs),
        scratch_shapes=list(scratch),
        input_output_aliases=aliases or {},
        compiler_params=pltpu.CompilerParams(vmem_limit_bytes=limit),
        cost_estimate=pl.CostEstimate(
            flops=flops, bytes_accessed=2 * flops // 1000, transcendentals=0
        ),
    )


def part_shapes(n, rows):
    return [((rows, D), BF16)] * (n - 1) + [((rows // 2, D), BF16)] * 2


class Copies:
    def __init__(self, semaphores):
        self.semaphores, self.count, self.out = semaphores, 0, []

    def start(self, source, target):
        copy = pltpu.make_async_copy(source, target, self.semaphores.at[self.count])
        self.count += 1
        copy.start()
        return copy

    def write(self, source, target):
        self.out.append(self.start(source, target))

    def drain(self):
        for copy in self.out:
            copy.wait()


def other_half(core):
    return pl.ds(pl.multiple_of((1 - core[0]) * (D // 2), D // 2), D // 2)


def fetch_halves(copies, pieces, target, start_of):
    half = pieces[0].shape[0]
    out = []
    for r, piece in enumerate(pieces):
        at = start_of(r // 2) + r % 2 * half
        out.append(copies.start(piece, target.at[pl.ds(at, half), :]))
    return out


def fetch_pieces(copies, pieces, target, start_of, halved=True):
    rows = pieces[0].shape[0]
    out = []
    for r, piece in enumerate(pieces):
        if halved and r == len(pieces) - 1:
            at = start_of(r - 1) + rows // 2
        else:
            at = start_of(r)
        out.append(copies.start(piece, target.at[pl.ds(at, piece.shape[0]), :]))
    return out


def write_part(copies, buffer, parts, r, halved=True):
    n = len(parts) - halved
    rows = parts[0].shape[0]
    start = r * rows
    if halved and r == n - 1:
        half = rows // 2
        copies.write(buffer.at[pl.ds(start, half), :], parts[n - 1])
        copies.write(buffer.at[pl.ds(start + half, half), :], parts[n])
    else:
        copies.write(buffer.at[pl.ds(start, rows), :], parts[r])


def store_part(parts, r, values):
    n = len(parts) - 1
    if r < n - 1:
        parts[r][...] = values
    else:
        half = values.shape[0] // 2
        parts[n - 1][...] = values[:half]
        parts[n][...] = values[half:]


def assemble(pieces, target, start_of):
    n = len(pieces) - 1
    rows = pieces[0].shape[0]
    half = rows // 2
    for r in range(n - 1):
        target[pl.ds(start_of(r), rows), :] = pieces[r][...]
    start = start_of(n - 1)
    target[pl.ds(start, half), :] = pieces[n - 1][...]
    target[pl.ds(start + half, half), :] = pieces[n][...]


def segment_of(positions, ends):
    return sum((positions >= e).astype(jnp.int32) for e in ends)


def row_ends(lengths):
    first = lengths[0, 0]
    second = first + lengths[0, 1]
    return (first, second, second + lengths[0, 2])


class Block:
    def __init__(self, b, ends):
        start = b * BLOCK
        rows = lax.broadcasted_iota(jnp.int32, (BLOCK, BLOCK), 0)
        columns = lax.broadcasted_iota(jnp.int32, (BLOCK, BLOCK), 1)
        seg_rows = segment_of(rows + start, ends)
        seg_columns = segment_of(columns + start, ends)
        same = seg_rows == seg_columns
        self.mask = jnp.logical_and(same, rows >= columns)
        self.mask_t = jnp.logical_and(same, columns >= rows)
        self.last = segment_of(start + BLOCK - 1, ends)
        self.earlier = segment_of(start - 1, ends) if b > 0 else -1
        wide_rows = lax.broadcasted_iota(jnp.int32, (BLOCK, HEAD_DIM), 0)
        segments = segment_of(wide_rows + start, ends)
        self.from_state = segments == self.earlier
        self.to_state = segments == self.last

    def decay(self, full):
        return jnp.where(self.mask, full, 0.0)

    def keeping(self, rate):
        factor = jnp.exp(jnp.full((HEAD_DIM, HEAD_DIM), -rate * BLOCK, F32))
        return jnp.where(self.last == self.earlier, factor, 0.0)


def full_decay(rate, turned=False):
    rows = lax.broadcasted_iota(jnp.int32, (BLOCK, BLOCK), int(turned))
    columns = lax.broadcasted_iota(jnp.int32, (BLOCK, BLOCK), 1 - int(turned))
    return jnp.exp(-rate * jnp.maximum(rows - columns, 0).astype(F32))


def edge_factors(rate):
    rows = lax.broadcasted_iota(jnp.int32, (BLOCK, HEAD_DIM), 0).astype(F32)
    return jnp.exp(-rate * (rows + 1.0)), jnp.exp(-rate * (BLOCK - 1.0 - rows))


def silu16(values):
    return (values * jax.nn.sigmoid(values)).astype(BF16)


def silu_grad(before):
    sigmoid = jax.nn.sigmoid(before)
    return sigmoid * (1.0 + before * (1.0 - sigmoid))


def entry_kernel(n, heads, order, core, lengths, rates, *refs):
    pieces, refs = refs[: 2 * n], refs[2 * n :]
    weights, mixer, refs = refs[:4], refs[4], refs[5:]
    normed_out, normed_send, proj_out, mixed_out, squares, states_out, refs = *refs[:6], refs[6:]
    parts, refs = refs[: n + 1], refs[n + 1 :]
    normed, weight_in, mixer_in, proj, mixed, pre, states, buffer, semaphores = refs
    copies = Copies(semaphores)
    rows = 2 * pieces[0].shape[0]
    total = n * rows
    width = heads * HEAD_DIM
    coming = fetch_halves(
        copies, pieces, normed, lambda r: pl.multiple_of(order[0, r] * rows, rows)
    )
    for copy in coming:
        copy.wait()
    fetched = [copies.start(w, weight_in.at[i]) for i, w in enumerate(weights)]
    mixer_copy = copies.start(mixer, mixer_in)
    copies.write(normed, normed_out)
    copies.write(normed.at[:, other_half(core)], normed_send)
    for i in range(4):
        fetched[i].wait()
        for b in range(total // BLOCK):
            here = pl.ds(b * BLOCK, BLOCK)
            proj[here, i * width : (i + 1) * width] = dot(normed[here, :], weight_in[i])
    copies.write(proj, proj_out)
    ends = row_ends(lengths)
    fulls = [full_decay(rates[h]) for h in range(heads)]
    edges = [edge_factors(rates[h]) for h in range(heads)]
    state = [jnp.zeros((HEAD_DIM, HEAD_DIM), F32) for _ in range(heads)]
    ones = jnp.ones((8, HEAD_DIM), BF16)
    for b in range(total // BLOCK):
        here = pl.ds(b * BLOCK, BLOCK)
        block = Block(b, ends)
        square = jnp.zeros((8, BLOCK), F32)
        for h in range(heads):
            at = [slice(i * width + h * HEAD_DIM, i * width + (h + 1) * HEAD_DIM) for i in range(4)]
            query, key = silu16(proj[here, at[0]]), silu16(proj[here, at[1]])
            value = proj[here, at[2]].astype(BF16)
            inner, carried = edges[h]
            inner = jnp.where(block.from_state, inner, 0.0)
            carried = jnp.where(block.to_state, carried, 0.0)
            states[b, h] = state[h]
            weight = (dot(query, key, NT) * block.decay(fulls[h])).astype(BF16)
            high, low = split(state[h])
            out = dot(weight, value) + inner * (dot(query, high) + dot(query, low))
            state[h] = block.keeping(rates[h]) * state[h] + dot(
                (key.astype(F32) * carried).astype(BF16), value, TN
            )
            mixed[here, at[0]] = out
            pre[here, at[0]] = (out * proj[here, at[3]]).astype(BF16)
            high, low = split(out * out)
            square += dot(ones, high, NT) + dot(ones, low, NT)
        squares[:, here] = square[0:1]
    copies.write(mixed, mixed_out)
    copies.write(states, states_out)
    mixer_copy.wait()
    for r in reversed(range(0, n, 2)):
        both = jnp.concatenate(
            [pre[pl.ds(pl.multiple_of(order[0, q] * rows, rows), rows), :] for q in (r, r + 1)], 0
        )
        buffer[r * rows : (r + 2) * rows, :] = dot(both, mixer_in[...]).astype(BF16)
        write_part(copies, buffer, parts, r + 1)
        write_part(copies, buffer, parts, r)
    copies.drain()


def column(row):
    return jnp.transpose(jnp.broadcast_to(row, (HEAD_DIM, row.shape[1])))


def exit_kernel(n, heads, order, core, lengths, rates, *refs):
    pieces, refs = refs[: n + 1], refs[n + 1 :]
    weights, mixer_hbm, refs = refs[:4], refs[4], refs[5:]
    proj_hbm, mixed_hbm, states_hbm, inverses, refs = *refs[:4], refs[4:]
    entry_out, send_out, keep_out, refs = *refs[:3], refs[3:]
    parts, refs = refs[:3], refs[3:]
    resid, weight_in, mixer, proj, mixed, states, scaled, entry_g, scaled_g, buffer, send, keep, sems = refs
    copies = Copies(sems)
    rows = pieces[0].shape[0]
    total = n * rows
    width = heads * HEAD_DIM
    mixer_copy = copies.start(mixer_hbm, mixer)
    coming = fetch_pieces(
        copies, pieces, resid, lambda r: pl.multiple_of(order[0, r] * rows, rows)
    )
    mixer_copy.wait()
    for copy in coming:
        copy.wait()
    saved = [
        copies.start(a, b)
        for a, b in ((proj_hbm, proj), (mixed_hbm, mixed), (states_hbm, states))
    ]
    fetched = [
        copies.start(w, weight_in.at[:, i * width : (i + 1) * width]) for i, w in enumerate(weights)
    ]
    for b in range(total // BLOCK):
        here = pl.ds(b * BLOCK, BLOCK)
        scaled_g[here, :] = dot(resid[here, :D], mixer[...], NT)
    for copy in saved:
        copy.wait()
    ends = row_ends(lengths)
    fulls = [full_decay(rates[h]) for h in range(heads)]
    turned = [full_decay(rates[h], True) for h in range(heads)]
    edges = [edge_factors(rates[h]) for h in range(heads)]
    later = [jnp.zeros((HEAD_DIM, HEAD_DIM), F32) for _ in range(heads)]
    for b in reversed(range(total // BLOCK)):
        here = pl.ds(b * BLOCK, BLOCK)
        block = Block(b, ends)
        inverse = column(inverses[:, here])
        coded = resid[here, D : D + 128].astype(F32)
        mean = (coded[:, 0:1] + coded[:, 1:2] + coded[:, 2:3]) * (1.0 / D)
        for h in range(heads):
            at = [slice(i * width + h * HEAD_DIM, i * width + (h + 1) * HEAD_DIM) for i in range(4)]
            query_pre, key_pre = proj[here, at[0]], proj[here, at[1]]
            query, key = silu16(query_pre), silu16(key_pre)
            value = proj[here, at[2]].astype(BF16)
            gate = proj[here, at[3]]
            grad_s = scaled_g[here, at[0]]
            unit = mixed[here, at[0]] * inverse
            scaled[here, at[0]] = (unit * gate).astype(BF16)
            entry_g[here, at[3]] = (grad_s * unit).astype(BF16)
            grad = (inverse * (grad_s * gate - unit * mean)).astype(BF16)
            inner, carried = edges[h]
            inner = jnp.where(block.from_state, inner, 0.0)
            carried = jnp.where(block.to_state, carried, 0.0)
            decay = block.decay(fulls[h])
            decay_t = jnp.where(block.mask_t, turned[h], 0.0)
            weight_t = (dot(key, query, NT) * decay_t).astype(BF16)
            score = (dot(grad, value, NT) * decay).astype(BF16)
            score_t = (dot(value, grad, NT) * decay_t).astype(BF16)
            high, low = split(states[b, h])
            query_g = dot(score, key) + inner * (dot(grad, high, NT) + dot(grad, low, NT))
            high, low = split(later[h])
            key_g = dot(score_t, query) + carried * (dot(value, high, NT) + dot(value, low, NT))
            value_g = dot(weight_t, grad) + carried * (dot(key, high) + dot(key, low))
            later[h] = (
                dot((query.astype(F32) * inner).astype(BF16), grad, TN)
                + block.keeping(rates[h]) * later[h]
            )
            entry_g[here, at[0]] = (query_g * silu_grad(query_pre)).astype(BF16)
            entry_g[here, at[1]] = (key_g * silu_grad(key_pre)).astype(BF16)
            entry_g[here, at[2]] = value_g.astype(BF16)
    copies.write(entry_g, entry_out)
    send[...] = dot(scaled[...], resid[:, other_half(core)], TN).astype(BF16)
    copies.write(send, send_out)
    keep[...] = dot(scaled[...], resid[:, own_half(core)], TN)
    copies.write(keep, keep_out)
    for copy in fetched:
        copy.wait()
    both = jnp.concatenate(
        [
            entry_g[pl.ds(pl.multiple_of(order[0, q] * rows, rows), rows), :]
            for q in (n - 2, n - 1)
        ],
        0,
    )
    buffer[...] = dot(both, weight_in[...], NT).astype(BF16)
    half = rows // 2
    for part, (low, high) in zip(parts, ((0, rows), (rows, rows + half), (rows + half, 2 * rows))):
        copies.write(buffer.at[pl.ds(low, high - low), :], part)
    copies.drain()


def project_kernel(n, order, *refs):
    entry_hbm, weights, refs = refs[0], refs[1:5], refs[5:]
    parts, refs = refs[: n - 2], refs[n - 2 :]
    entry_g, weight_in, buffer, sems = refs
    copies = Copies(sems)
    rows = parts[0].shape[0]
    width = weights[0].shape[1]
    coming = [
        copies.start(w, weight_in.at[:, i * width : (i + 1) * width]) for i, w in enumerate(weights)
    ] + [copies.start(entry_hbm, entry_g)]
    for copy in coming:
        copy.wait()
    for r in reversed(range(0, n - 2, 2)):
        both = jnp.concatenate(
            [entry_g[pl.ds(pl.multiple_of(order[0, q] * rows, rows), rows), :] for q in (r, r + 1)],
            0,
        )
        buffer[r * rows : (r + 2) * rows, :] = dot(both, weight_in[...], NT).astype(BF16)
        for q in (r + 1, r):
            copies.write(buffer.at[pl.ds(q * rows, rows), :], parts[q])
    copies.drain()


def cotangent_kernel(n, core, *refs):
    pieces, down, grad, grad_send, *products = refs[: n + 1], *refs[n + 1 :]
    rows = pieces[0].shape[0]
    assemble(pieces, grad, lambda r: r * rows)
    grad_send[...] = grad[:, other_half(core)]
    for r, out in enumerate(products):
        out[...] = dot(grad[pl.ds(2 * r * rows, 2 * rows), :], down[...], NT)


def hidden_kernel(index, halved, core, *refs):
    count = 2 + halved
    pieces, refs = refs[:count], refs[count:]
    first, second, product_g, refs = *refs[:3], refs[3:]
    refs = refs if index == 0 else refs[4:]
    (normed_out, product_out, second_out, bundle), refs = refs[:4], refs[4:]
    parts, refs = refs[:count], refs[count:]
    normed, product, first_g, second_g, sems = refs
    copies = Copies(sems)
    low = 0
    for piece in pieces:
        normed[low : low + piece.shape[0], :] = piece[...]
        low += piece.shape[0]
    units, padded = first.shape[0], product.shape[1]
    if padded > units:
        for ref in (product, first_g, second_g):
            ref[:, units:] = jnp.zeros((low, padded - units), BF16)
    here = pl.ds(index * low, low)
    copies.write(normed, normed_out.at[here, :])
    copies.write(normed.at[:, other_half(core)], bundle.at[here, pl.ds(padded, D // 2)])
    tokens = normed[...]
    first_act, second_act = dot(tokens, first[...], NT), dot(tokens, second[...], NT)
    product[:, :units] = (first_act * second_act).astype(BF16)
    copies.write(product, product_out.at[here, :])
    grad = product_g[...]
    one, two = (grad * second_act).astype(BF16), (grad * first_act).astype(BF16)
    first_g[:, :units] = one
    copies.write(first_g, bundle.at[here, pl.ds(0, padded)])
    second_g[:, :units] = two
    copies.write(second_g, second_out.at[here, :])
    result = (dot(one, first[...]) + dot(two, second[...])).astype(BF16)
    low = 0
    for part in parts:
        part[...] = result[low : low + part.shape[0]]
        low += part.shape[0]
    copies.drain()


def down_kernel(n, product, down, *parts):
    rows, units = parts[0].shape[0], down.shape[0]
    for r in range(0, n, 2):
        result = dot(product[pl.ds(r * rows, 2 * rows), :units], down[...]).astype(BF16)
        store_part(parts, r, result[:rows])
        store_part(parts, r + 1, result[rows:])


def norm_kernel(tokens, *halves):
    out = normalize(tokens[...].astype(F32)).astype(BF16)
    half = halves[0].shape[0]
    halves[0][...] = out[:half]
    halves[1][...] = out[half:]


def middle_kernel(tokens, near, left, right, inverse, attn, hidden, normed):
    whole = near[...].astype(F32) + left[...].astype(F32) + right[...].astype(F32)
    whole = whole * inverse[...]
    attn[...] = whole
    whole = tokens[...].astype(F32) + whole
    hidden[...] = whole
    normed[...] = normalize(whole).astype(BF16)


def resid_kernel(low, grad, hidden, near, left, right, attn, hidden_g, coded):
    rows = grad.shape[0]
    here = slice(low, low + rows)
    normed_g = near[...].astype(F32) + left[here, :].astype(F32) + right[here, :].astype(F32)
    whole = grad[...].astype(F32) + norm_grad(hidden[...], normed_g)
    hidden_g[...] = whole
    resid = whole.astype(BF16)
    coded[:, :D] = resid
    inner = jnp.sum(resid.astype(F32) * attn[...], axis=1, keepdims=True)
    lane = lax.broadcasted_iota(jnp.int32, (1, 128), 1)
    out = jnp.zeros((rows, 128), F32)
    for i in range(3):
        high = inner.astype(BF16).astype(F32)
        out += jnp.where(lane == i, high, 0.0)
        inner -= high
    coded[:, D:] = out.astype(BF16)


def output_kernel(tokens, attn, ffn, valid_rows, output, sums):
    rows = tokens.shape[0]
    valid = lax.broadcasted_iota(jnp.int32, (rows, 1), 0) < valid_rows[0]
    tokens_wide = tokens[...].astype(F32)
    output[...] = (tokens_wide + attn[...] + ffn[...]).astype(BF16)
    lane = lax.broadcasted_iota(jnp.int32, (1, 128), 1)
    out = jnp.zeros((1, 128), F32)
    for i, values in enumerate((tokens_wide, attn[...], ffn[...])):
        per_row = jnp.sum(values * values, axis=1, keepdims=True)
        whole = jnp.sum(jnp.where(valid, per_row, 0.0), axis=0, keepdims=True)
        out += jnp.where(lane == i, whole, 0.0)
    counted = jnp.clip(valid_rows[0], 0, rows).astype(F32)
    sums[...] = out + jnp.where(lane == 3, counted, 0.0)


def local(
    tokens_in,
    query_weight,
    key_weight,
    value_weight,
    gate_weight,
    mixer_weight,
    first_weight,
    second_weight,
    down_weight,
    doc_lengths,
    head_decay,
    out_grad,
):
    n = lax.axis_size("narrow")
    rows = tokens_in.shape[0]
    total = rows * n
    heads = head_decay.shape[0]
    width = heads * HEAD_DIM
    units = first_weight.shape[1]
    me = lax.axis_index("narrow")
    core = lax.axis_index("wide") % 2
    start_row = me * rows
    order = lax.dynamic_slice(jnp.asarray(order_table(n)), (me, 0), (1, n))
    where = core.reshape(1)
    entry_weights = (query_weight, key_weight, value_weight, gate_weight)
    tokens_wide = tokens_in.astype(F32)
    rates = head_decay

    half_rows = total // 2
    blocks = total // BLOCK
    first_t, second_t = first_weight.T, second_weight.T
    valid_rows = (jnp.sum(doc_lengths[0, : NDOC - 1]) - start_row).reshape(1)

    half_shapes = [((rows // 2, D), BF16)] * 2
    halves = call(norm_kernel, half_shapes, [VMEM], 6 * rows * D, 14 * MIB)(tokens_in)
    pieces = [v for pair in Gather2(halves, n).finish() for v in pair]
    shapes = [
        ((total, D), BF16),
        ((total, D // 2), BF16),
        ((total, 4 * width), F32),
        ((total, width), F32),
        ((1, total), F32),
        ((blocks, heads, HEAD_DIM, HEAD_DIM), F32),
    ] + part_shapes(n, rows)
    *pieces, grad_own = barrier(*pieces, out_grad)
    cotangent = Gather(grad_own, n).step()
    normed, normed_send, proj, mixed, squares, states, *parts = call(
        functools.partial(entry_kernel, n, heads),
        shapes,
        [SMEM] * 4 + [ANY] * (2 * n + 5),
        12 * total * D * width,
        48 * MIB,
        [
            pltpu.VMEM((total, D), BF16),
            pltpu.VMEM((4, D, width), BF16),
            pltpu.VMEM((width, D), BF16),
            pltpu.VMEM((total, 4 * width), F32),
            pltpu.VMEM((total, width), F32),
            pltpu.VMEM((total, width), BF16),
            pltpu.VMEM((blocks, heads, HEAD_DIM, HEAD_DIM), F32),
            pltpu.VMEM((total, D), BF16),
            pltpu.SemaphoreType.DMA((3 * n + 13,)),
        ],
        [VMEM if i == 4 else ANY for i in range(len(shapes))],
    )(order, where, doc_lengths, rates, *pieces, *entry_weights, mixer_weight)
    squares, cotangent.left, cotangent.right, *parts = barrier(
        squares, cotangent.left, cotangent.right, *parts
    )
    scatter = Scatter(parts, n)
    hop = Butterfly(squares, "narrow")
    while cotangent.left_steps:
        scatter.step()
        cotangent.step()
        hop.step()
        meet(scatter, cotangent, hop)
    squares = hop.finish()
    grad_pieces = cotangent.pieces
    inverses = lax.rsqrt(squares / D + EPS)
    inverse_own = lax.dynamic_slice(inverses, (0, start_row), (1, rows)).reshape(rows, 1)
    near, left, right = scatter.finish()
    attn_own, hidden_own, normed_own = call(
        middle_kernel,
        [((rows, D), F32)] * 2 + [((rows, D), BF16)],
        [VMEM] * 5,
        12 * rows * D,
        14 * MIB,
    )(tokens_in, near, left, right, inverse_own)

    padded = -(-units // 128) * 128

    def hidden(index, pieces):
        halved = index == n // 2 - 1
        half_row = rows // 2
        part_rows = [rows, half_row, half_row] if halved else [rows, rows]
        count = len(part_rows)
        outs = call(
            functools.partial(hidden_kernel, index, halved),
            [((total, D), BF16)]
            + [((total, padded), BF16)] * 2
            + [((total, padded + D // 2), BF16)]
            + [((p, D), BF16) for p in part_rows],
            [SMEM] + [VMEM] * (count + 3) + [ANY] * len(whole),
            16 * rows * D * units,
            40 * MIB,
            [pltpu.VMEM((2 * rows, D), BF16)]
            + [pltpu.VMEM((2 * rows, padded), BF16)] * 3
            + [pltpu.SemaphoreType.DMA((5,))],
            [ANY] * 4 + [VMEM] * count,
            {count + 4 + i: i for i in range(len(whole))},
        )(where, *pieces, first_t, second_t, product_g[index], *whole)
        return outs[:4], list(outs[4:])

    normed_own, grad_pieces = lax.optimization_barrier((normed_own, grad_pieces))
    gather = Gather(normed_own, n).step()
    grad_all, grad_send, *product_g = call(
        functools.partial(cotangent_kernel, n),
        [((total, D), BF16), ((total, D // 2), BF16)] + [((2 * rows, units), F32)] * (n // 2),
        [SMEM] + [VMEM] * (n + 2),
        2 * total * D * units,
        22 * MIB,
    )(where, *grad_pieces, down_weight)
    gather.left, gather.right, grad_send, normed_send, product_g = lax.optimization_barrier(
        (gather.left, gather.right, grad_send, normed_send, product_g)
    )
    whole, parts = [], []
    for i in range(n // 2 - 1):
        pieces = gather.pieces[2 * i : 2 * i + 2]
        gather.step()
        whole, new_parts = hidden(i, pieces)
        if i == 0:
            normed_other = swap(normed_send, "wide", 1)
            gather.left, gather.right, normed_other, new_parts = lax.optimization_barrier(
                (gather.left, gather.right, normed_other, new_parts)
            )
        parts += new_parts
    grad_other = swap(grad_send, "wide", 1)
    *pieces, grad_other = barrier(*gather.pieces[n - 2 :], grad_other)
    whole, new_parts = hidden(n // 2 - 1, pieces)
    parts += new_parts
    normed2, product, second_g, bundle = whole

    scatter = Scatter(parts, n)
    stream = Together(scatter)
    half = D // 2
    cut_at = [(0, 384, 768, half), (0, half), (0, 384, 768, half)]
    cuts = [tuple(zip(at[:-1], at[1:])) for at in cut_at]

    (product_other, bundle_other), _ = region(
        [stream], [(product, "wide", 1), (bundle, "wide", 1)]
    )
    (second_other_g,), down_own = region(
        [stream],
        [(second_g, "wide", 1)],
        lambda *v: own_columns(core, cuts[0], units, *v),
        [product, product_other, grad_all, grad_other],
    )
    down_in, first_in, second_in = [], [], []
    (received,), first_own = region(
        [stream],
        [(down_own[0], "wide", 2)],
        lambda *v: own_columns(core, cuts[1], units, *v, v[1], low=padded),
        [bundle, bundle_other, normed2],
    )
    down_in.append(received)
    (received,), second_own = region(
        [stream],
        [(down_own[1], "wide", 2)],
        lambda *v: own_columns(core, cuts[2], units, *v, low=padded),
        [second_g, second_other_g, normed2, bundle_other],
    )
    down_in.append(received)
    while scatter.left_steps:
        region([stream])
    left, right, low, _ = scatter.received
    hidden_g, resid_own = call(
        functools.partial(resid_kernel, low),
        [((rows, D), F32), ((rows, D + 128), BF16)],
        [VMEM] * 6,
        20 * rows * D,
        14 * MIB,
    )(out_grad, hidden_own, scatter.near[0], left, right, attn_own)

    gather = Gather(resid_own, n)

    def mixed_pairs(owns, ins):
        return [v for pair in zip(owns, ins) for v in pair]

    def output_parts(product):
        return call(
            functools.partial(down_kernel, n),
            part_shapes(n, rows),
            [VMEM] * 2,
            2 * total * D * units,
            14 * MIB,
        )(product, down_weight)

    down_own, first_own = list(down_own), list(first_own)
    resid_own, product, down_own[2], first_own[0] = barrier(
        resid_own, product, down_own[2], first_own[0]
    )
    gather = Gather(resid_own, n).step(n // 2 - 1)
    parts = output_parts(product)
    down_in.append(swap(down_own[2], "wide", 2))
    first_in = swap(first_own[0], "wide", 2)
    gather.left, gather.right, parts, down_in[2], first_in = lax.optimization_barrier(
        (gather.left, gather.right, parts, down_in[2], first_in)
    )
    scatter2 = Scatter(parts, n)
    stream2 = Together(scatter2)
    (received,), (first_total, down_total) = region(
        [gather, stream2],
        [(second_own[0], "wide", 2)],
        lambda own, other, *v: (summed(own, other), summed(*v)),
        [first_own[0], first_in, *mixed_pairs(down_own, down_in)],
    )
    second_in.append(received)

    shapes = [
        ((total, 4 * width), BF16),
        ((width, D // 2), BF16),
        ((width, D // 2), F32),
        ((rows, D), BF16),
        ((rows // 2, D), BF16),
        ((rows // 2, D), BF16),
    ]
    leave = call(
        functools.partial(exit_kernel, n, heads),
        shapes,
        [SMEM] * 4 + [ANY] * (n + 9) + [VMEM],
        12 * total * D * width,
        60 * MIB,
        [
            pltpu.VMEM((total, D + 128), BF16),
            pltpu.VMEM((D, 4 * width), BF16),
            pltpu.VMEM((width, D), BF16),
            pltpu.VMEM((total, 4 * width), F32),
            pltpu.VMEM((total, width), F32),
            pltpu.VMEM((blocks, heads, HEAD_DIM, HEAD_DIM), F32),
            pltpu.VMEM((total, width), BF16),
            pltpu.VMEM((total, 4 * width), BF16),
            pltpu.VMEM((total, width), F32),
            pltpu.VMEM((2 * rows, D), BF16),
            pltpu.VMEM((width, D // 2), BF16),
            pltpu.VMEM((width, D // 2), F32),
            pltpu.SemaphoreType.DMA((2 * n + 15,)),
        ],
        [ANY] * len(shapes),
    )
    (received, first_other, down_other), (entry_g, mixer_send, mixer_keep, *parts) = region(
        [stream2],
        [(second_own[1], "wide", 2), (first_total, "wide", 1), (down_total, "wide", 1)],
        lambda inverses, *pieces: leave(
            order,
            where,
            doc_lengths,
            rates,
            *pieces,
            *entry_weights,
            mixer_weight,
            proj,
            mixed,
            states,
            inverses,
        ),
        [inverses, *gather.pieces],
    )
    second_in.append(received)

    far = parts
    scatter = Scatter(part_shapes(n, rows)[: n - 2] + far, n)
    stream = Together(scatter2, scatter)

    def mixer_work(keep, crossed_send, entry_g, normed, normed_other):
        (mixer_own,) = call(
            add_kernel, [(keep.shape, BF16)], [VMEM] * 2, keep.size, 14 * MIB
        )(keep, swap(crossed_send, "wide", 1))
        mixer_in = swap(mixer_own, "wide", 2)
        entry_other = swap(entry_g, "wide", 1)
        parts = call(
            functools.partial(project_kernel, n),
            part_shapes(n, rows)[: n - 2],
            [SMEM] + [ANY] * 5,
            6 * total * D * width,
            48 * MIB,
            [
                pltpu.VMEM((total, 4 * width), BF16),
                pltpu.VMEM((D, 4 * width), BF16),
                pltpu.VMEM((total - 2 * rows, D), BF16),
                pltpu.SemaphoreType.DMA((n + 4,)),
            ],
            [ANY] * (n - 2),
        )(order, entry_g, *entry_weights)
        owns = own_rows(core, 2, 2, width, normed, normed_other, entry_g, entry_other)
        return mixer_own, mixer_in, owns, entry_other, parts

    (received,), (mixer_own, mixer_in, (value_own, gate_own), entry_other, parts) = region(
        [stream],
        [(second_own[2], "wide", 2)],
        mixer_work,
        [mixer_keep, mixer_send, entry_g, normed, normed_other],
    )
    second_in.append(received)
    scatter.near.update({d: parts[i] for i, d in enumerate(distances(n)[:-2])})

    def entry_work(normed, normed_other, entry_g, entry_other, *values):
        mixer_total = summed(*values[:2])
        mixer_other = swap(mixer_total, "wide", 1)
        owns = own_rows(core, 0, 2, width, normed, normed_other, entry_g, entry_other)
        first_w = place(core, *values[2:4], False)
        down_w = place(core, *values[4:6], False)
        return owns, mixer_total, mixer_other, first_w, down_w, summed(*values[6:])

    (gate_in, value_in), work_out = region(
        [stream],
        [(gate_own, "wide", 2), (value_own, "wide", 2)],
        entry_work,
        [normed, normed_other, entry_g, entry_other, mixer_own, mixer_in]
        + [first_total, first_other, down_total, down_other]
        + mixed_pairs(second_own, second_in),
    )
    (query_own, key_own), mixer_total, mixer_other, first_w, down_w, second_total = work_out
    while scatter2.left_steps:
        region([stream])
    ffn_own = scatter2.result
    stream = Together(scatter)

    def output_work(tokens_in, attn_own, ffn_own, a, b, *pairs):
        output, stats = call(
            output_kernel,
            [((rows, D), BF16), ((1, 128), F32)],
            [VMEM] * 3 + [SMEM],
            6 * rows * D,
            14 * MIB,
        )(tokens_in, attn_own, ffn_own, valid_rows)
        stats = stats + swap(stats, "narrow", 1)
        return output, stats, place(core, a, b, False), summed(*pairs)

    (key_in, second_other), (output, stats, mixer_w, pair_total) = region(
        [stream],
        [(key_own, "wide", 2), (second_total, "wide", 1)],
        output_work,
        [tokens_in, attn_own, ffn_own, mixer_total, mixer_other]
        + [gate_own, gate_in, value_own, value_in],
    )
    (query_in, pair_other, hop), (second_w, key_total) = region(
        [stream],
        [(query_own, "wide", 2), (pair_total, "wide", 1), (stats, "narrow", 2)],
        lambda own, other, *v: (place(core, own, other, False), summed(*v)),
        [second_total, second_other, key_own, key_in],
    )
    stats = stats + hop
    while scatter.left_steps:
        region([stream])
    normed_g = scatter.result

    (key_other, hop), (query_total, (gate_w, value_w)) = region(
        [],
        [(key_total, "wide", 1), (stats, "narrow", 4)],
        lambda a, b, *v: (summed(a, b), place_two(core, *v)),
        [query_own, query_in, pair_total, pair_other],
    )
    stats = stats + hop
    query_other = swap(query_total, "wide", 1)
    for axis, bit in (("narrow", 8), ("wide", 1)):
        while bit < lax.axis_size(axis):
            stats = stats + swap(stats, axis, bit)
            bit *= 2
    input_grad = hidden_g + norm_grad(tokens_wide, normed_g)
    key_w = place(core, key_total, key_other, True)
    query_w = place(core, query_total, query_other, True)
    stream_rms = jnp.sqrt(stats[0, :3] / (stats[0, 3] * D))
    return (
        output,
        input_grad,
        query_w,
        key_w,
        value_w,
        gate_w,
        mixer_w,
        first_w.T,
        second_w.T,
        down_w,
        stream_rms,
    )


def solution(mesh):
    split_tokens = P(("wide", "narrow"), None)
    columns, rows = P(None, "narrow"), P("narrow", None)
    return jax.shard_map(
        local,
        mesh=mesh,
        in_specs=(split_tokens,)
        + (columns,) * 4
        + (rows, columns, columns, rows, P("wide", None), P("narrow"), split_tokens),
        out_specs=(split_tokens,) * 2 + (columns,) * 4 + (rows, columns, columns, rows, P()),
        check_vma=False,
    )
```

```python
import functools

import jax
import jax.numpy as jnp
import numpy as np
from jax import lax
from jax.experimental import pallas as pl
from jax.experimental.pallas import tpu as pltpu
from jax.sharding import PartitionSpec as P

D = 2048
HEAD_DIM = 128
NDOC = 4
EPS = 1e-06
BLOCK = 256
MIB = 1 << 20

F32 = jnp.float32
BF16 = jnp.bfloat16
NN = (((1,), (0,)), ((), ()))
NT = (((1,), (1,)), ((), ()))
TN = (((0,), (0,)), ((), ()))
VMEM = pl.BlockSpec(memory_space=pltpu.VMEM)
SMEM = pl.BlockSpec(memory_space=pltpu.SMEM)
ANY = pl.BlockSpec(memory_space=pl.ANY)


def dot(a, b, dims=NN):
    return lax.dot_general(a, b, dims, preferred_element_type=F32)


def split(values):
    high = values.astype(BF16)
    return high, (values - high.astype(F32)).astype(BF16)


def normalize(values):
    return values * lax.rsqrt(jnp.mean(values * values, axis=-1, keepdims=True) + EPS)


def norm_grad(values, grad_in):
    inverse = lax.rsqrt(jnp.mean(values * values, axis=-1, keepdims=True) + EPS)
    normed = values * inverse
    return inverse * (grad_in - normed * jnp.mean(grad_in * normed, axis=-1, keepdims=True))


def ring_order(n):
    if n == 16:
        return [r * 4 + (c if r % 2 == 0 else 3 - c) for r in range(4) for c in range(4)]
    return list(range(0, n, 2)) + list(range(n - 1, 0, -2))


def distances(n):
    out = [0]
    for k in range(1, n // 2):
        out += [-k, k]
    return out + [n // 2]


def order_table(n):
    ring = ring_order(n)
    place = {device: i for i, device in enumerate(ring)}
    return np.array(
        [[ring[(place[me] + d) % n] for d in distances(n)] for me in range(n)], np.int32
    )


def onward(values, n):
    ring = ring_order(n)
    return lax.ppermute(values, "narrow", [(ring[i], ring[(i + 1) % n]) for i in range(n)])


def backward(values, n):
    ring = ring_order(n)
    return lax.ppermute(values, "narrow", [(ring[(i + 1) % n], ring[i]) for i in range(n)])


def barrier(*values):
    return lax.optimization_barrier(values)


def add16(a, b):
    return (a.astype(F32) + b.astype(F32)).astype(BF16)


class Gather:
    def __init__(self, own, n):
        self.n, self.left_steps = n, n // 2
        self.left = self.right = own
        self.pieces = [own]

    def outgoing(self):
        if self.left_steps == 1:
            half = self.left.shape[0] // 2
            return self.left[:half], self.right[half:]
        return self.left, self.right

    def incoming(self, left, right):
        self.left_steps -= 1
        self.left, self.right = left, right
        self.pieces += [left, right]

    def step(self, count=1):
        for _ in range(count):
            left, right = self.outgoing()
            self.incoming(onward(left, self.n), backward(right, self.n))
        return self

    def finish(self):
        return self.step(self.left_steps).pieces


class Gather2:
    def __init__(self, halves, n):
        self.n, self.left_steps = n, n // 2
        self.left, self.right = list(halves), list(halves)
        self.pieces = [list(halves)]

    def step(self, count=1):
        for _ in range(count):
            self.left_steps -= 1
            if self.left_steps == 0:
                self.pieces.append([onward(self.left[0], self.n), backward(self.right[1], self.n)])
                return self
            for i in range(2):
                self.left[i] = onward(self.left[i], self.n)
                self.right[i] = backward(self.right[i], self.n)
            self.pieces += [list(self.left), list(self.right)]
        return self

    def finish(self):
        return self.step(self.left_steps).pieces


def merge_kernel(layout, *refs):
    outs, refs = refs[-2:], list(refs[:-2])
    at = 0
    for rows, half, offset in layout:
        if offset is None:
            for out in outs:
                out[at : at + rows] = refs.pop(0)[...]
        else:
            nears, parts, refs = refs[:2], refs[2:4], refs[4:]
            for i in range(2):
                low = half * i if half < rows else 0
                outs[i][at : at + rows] = nears[i][...]
                outs[i][at + low : at + low + half] = add16(
                    nears[i][low : low + half], parts[i][offset : offset + half]
                )
        at += rows


def join_one(low, near, part, out):
    rows = part.shape[0]
    out[...] = near[...]
    out[low : low + rows] = add16(near[low : low + rows], part[...])


class Scatter:
    def __init__(self, parts, n):
        self.n, self.left_steps = n, n // 2
        self.near = {d: parts[i] for i, d in enumerate(distances(n)[:-1])}
        self.left, self.right = parts[-2], parts[-1]
        self.received = None

    def operands(self):
        if self.received is None:
            return [self.left, self.right], (self.left.shape[0], 0, None)
        left, right, offset, half = self.received
        near = [self.near[self.left_steps], self.near[-self.left_steps]]
        return near + [left, right], (near[0].shape[0], half, offset)

    def take(self, left, right, offset, rows):
        self.left_steps -= 1
        if self.left_steps == 0:
            at = slice(offset, offset + rows)
            self.result = self.near[0].astype(F32) + left[at].astype(F32) + right[at].astype(F32)
        self.received = (left, right, offset, rows)

    def step(self, count=1):
        for _ in range(count):
            self.left_steps -= 1
            left, right = onward(self.left, self.n), backward(self.right, self.n)
            k = self.left_steps
            shape = self.near[k].shape
            if k == 0:
                self.result = (self.near[0], left, right)
            elif shape == left.shape:
                self.left, self.right = add16(self.near[k], left), add16(self.near[-k], right)
            else:
                half = shape[0] // 2
                self.left, self.right = [
                    call(
                        functools.partial(join_one, low),
                        [(shape, BF16)],
                        [VMEM] * 2,
                        shape[0] * shape[1],
                        14 * MIB,
                    )(near, part)[0]
                    for low, near, part in ((0, self.near[k], left), (half, self.near[-k], right))
                ]
        return self

    def finish(self):
        return self.step(self.left_steps).result


class Together:
    def __init__(self, *scatters):
        self.scatters, self.n = scatters, scatters[0].n

    def outgoing(self):
        operands, self.layout = [], []
        for s in self.scatters:
            values, layout = s.operands()
            operands += values
            self.layout.append(layout)
        if len(self.layout) == 1 and self.layout[0][2] is None:
            return operands
        rows = sum(entry[0] for entry in self.layout)
        return call(
            functools.partial(merge_kernel, tuple(self.layout)),
            [((rows, D), BF16)] * 2,
            [VMEM] * len(operands),
            2 * rows * D,
            14 * MIB,
        )(*operands)

    def incoming(self, left, right):
        offset = 0
        for s, (rows, _, _) in zip(self.scatters, self.layout):
            s.take(left, right, offset, rows)
            offset += rows


def region(streams=(), swaps=(), work=None, inputs=()):
    out = [v for s in streams for v in s.outgoing()]
    count = len(out)
    values, inputs = lax.optimization_barrier((out + [s[0] for s in swaps], list(inputs)))
    moved = [
        onward(v, streams[0].n) if i % 2 == 0 else backward(v, streams[0].n)
        for i, v in enumerate(values[:count])
    ]
    moved += [swap(v, s[1], s[2]) for v, s in zip(values[count:], swaps)]
    results = work(*inputs) if work else ()
    moved, results = lax.optimization_barrier((moved, results))
    for i, s in enumerate(streams):
        s.incoming(*moved[2 * i : 2 * i + 2])
    return moved[count:], results


def meet(*streams):
    values = barrier(*[v for s in streams for v in (s.left, s.right)])
    for i, s in enumerate(streams):
        s.left, s.right = values[2 * i : 2 * i + 2]


def swap(values, axis, bit):
    size = lax.axis_size(axis)
    return lax.ppermute(values, axis, [(i, i ^ bit) for i in range(size)])


class Butterfly:
    def __init__(self, values, axis):
        self.left, self.right, self.axis, self.bit = values, jnp.zeros((1, 128), F32), axis, 1

    def step(self):
        if self.bit < lax.axis_size(self.axis):
            self.left = self.left + swap(self.left, self.axis, self.bit)
            self.bit *= 2
        return self

    def finish(self):
        while self.bit < lax.axis_size(self.axis):
            self.step()
        return self.left


def ladder(values, bit=4):
    while bit < lax.axis_size("wide"):
        values = add16(values, swap(values, "wide", bit))
        bit *= 2
    return values


def own_half(core):
    return pl.ds(pl.multiple_of(core[0] * (D // 2), D // 2), D // 2)


def columns_kernel(cuts, lefts, rights, core, *refs):
    sources, outs, refs = refs[:4], refs[4 : 4 + len(cuts)], refs[4 + len(cuts) :]
    left, left_other, right, right_other, semaphores = refs
    width = outs[0].shape[0]
    columns = right.shape[1]
    copies = Copies(semaphores)
    coming = [
        copies.start(sources[1].at[:, pl.ds(lefts[1], left.shape[1])], left_other),
        copies.start(sources[3].at[:, pl.ds(rights[1], columns)], right_other),
        copies.start(sources[0].at[:, pl.ds(lefts[0], left.shape[1])], left),
    ]
    if rights[0] is None:
        coming.append(copies.start(sources[2].at[:, own_half(core)], right))
    else:
        coming.append(copies.start(sources[2].at[:, pl.ds(rights[0], columns)], right))
    coming[0].wait()
    coming[1].wait()
    part = dot(left_other[:, :width], right_other[...], TN)
    coming[2].wait()
    coming[3].wait()
    part += dot(left[:, :width], right[...], TN)
    for out, (low, high) in zip(outs, cuts):
        out[...] = part[:, low:high].astype(BF16)


def own_columns(core, cuts, width, left, left_other, right, right_other, lefts=(0, 0), low=0):
    total = left.shape[0]
    padded = -(-width // 128) * 128
    return call(
        functools.partial(columns_kernel, cuts, lefts, (None, low)),
        [((width, high - low), BF16) for low, high in cuts],
        [SMEM] + [ANY] * 4,
        2 * total * D * width,
        50 * MIB,
        [pltpu.VMEM((total, padded), BF16)] * 2
        + [pltpu.VMEM((total, D // 2), BF16)] * 2
        + [pltpu.SemaphoreType.DMA((4,))],
    )(core.reshape(1), left, left_other, right, right_other)


def rows_kernel(first, core, *refs):
    sources, refs = refs[:4], refs[4:]
    outs, (normed, normed_other, grads, grads_other, semaphores) = refs[:-5], refs[-5:]
    width = outs[0].shape[1]
    columns = pl.ds(first * width, len(outs) * width)
    copies = Copies(semaphores)
    coming = [
        copies.start(sources[1], normed_other),
        copies.start(sources[3].at[:, columns], grads_other),
        copies.start(sources[0].at[:, own_half(core)], normed),
        copies.start(sources[2].at[:, columns], grads),
    ]
    coming[0].wait()
    coming[1].wait()
    part = dot(normed_other[...], grads_other[...], TN)
    coming[2].wait()
    coming[3].wait()
    part += dot(normed[...], grads[...], TN)
    for i, out in enumerate(outs):
        out[...] = part[:, i * width : (i + 1) * width].astype(BF16)


def own_rows(core, first, count, width, normed, normed_other, bundle, bundle_other):
    total = normed.shape[0]
    return call(
        functools.partial(rows_kernel, first),
        [((D // 2, width), BF16)] * count,
        [SMEM] + [ANY] * 4,
        2 * total * D * width * count,
        50 * MIB,
        [pltpu.VMEM((total, D // 2), BF16)] * 2
        + [pltpu.VMEM((total, count * width), BF16)] * 2
        + [pltpu.SemaphoreType.DMA((4,))],
    )(core.reshape(1), normed, normed_other, bundle, bundle_other)


def add_kernel(keep, crossed, out):
    out[...] = (keep[...] + crossed[...].astype(F32)).astype(BF16)


def sum_kernel(*refs):
    out, low = refs[-1], 0
    for i in range(len(refs) // 2):
        width = refs[2 * i].shape[1]
        out[:, low : low + width] = add16(refs[2 * i][...], refs[2 * i + 1][...])
        low += width


def summed(*values):
    rows = values[0].shape[0]
    columns = sum(v.shape[1] for v in values[::2])
    return ladder(
        call(
            sum_kernel,
            [((rows, columns), BF16)],
            [VMEM] * len(values),
            rows * columns,
            14 * MIB,
        )(*values)[0]
    )


def place(core, own, other, row_halves):
    rows, columns = own.shape
    return call(
        functools.partial(place_kernel, row_halves),
        [((2 * rows, columns) if row_halves else (rows, 2 * columns), F32)],
        [SMEM] + [VMEM] * 2,
        rows * columns,
        14 * MIB,
    )(core.reshape(1), own, other)[0]


def place_two(core, own, other):
    rows, columns = own.shape
    return call(
        place_two_kernel,
        [((2 * rows, columns // 2), F32)] * 2,
        [SMEM] + [VMEM] * 2,
        rows * columns,
        14 * MIB,
    )(core.reshape(1), own, other)


def place_two_kernel(core, own, other, *outs):
    rows, columns = own.shape[0], outs[0].shape[1]
    for where, ref in ((core[0], own), (1 - core[0], other)):
        here = pl.ds(pl.multiple_of(where * rows, 128), rows)
        for i, out in enumerate(outs):
            out[here, :] = ref[:, i * columns : (i + 1) * columns].astype(F32)


def place_kernel(row_halves, core, own, other, out):
    rows, columns = own.shape
    for where, ref in ((core[0], own), (1 - core[0], other)):
        if row_halves:
            out[pl.ds(pl.multiple_of(where * rows, 128), rows), :] = ref[...].astype(F32)
        else:
            out[:, pl.ds(pl.multiple_of(where * columns, 128), columns)] = ref[...].astype(F32)


def call(kernel, outs, in_specs, flops, limit, scratch=(), out_specs=None, aliases=None):
    return pl.pallas_call(
        kernel,
        out_shape=[jax.ShapeDtypeStruct(s, d) for s, d in outs],
        in_specs=in_specs,
        out_specs=out_specs or [VMEM] * len(outs),
        scratch_shapes=list(scratch),
        input_output_aliases=aliases or {},
        compiler_params=pltpu.CompilerParams(vmem_limit_bytes=limit),
        cost_estimate=pl.CostEstimate(
            flops=flops, bytes_accessed=2 * flops // 1000, transcendentals=0
        ),
    )


def part_shapes(n, rows):
    return [((rows, D), BF16)] * (n - 1) + [((rows // 2, D), BF16)] * 2


class Copies:
    def __init__(self, semaphores):
        self.semaphores, self.count, self.out = semaphores, 0, []

    def start(self, source, target):
        copy = pltpu.make_async_copy(source, target, self.semaphores.at[self.count])
        self.count += 1
        copy.start()
        return copy

    def write(self, source, target):
        self.out.append(self.start(source, target))

    def drain(self):
        for copy in self.out:
            copy.wait()


def other_half(core):
    return pl.ds(pl.multiple_of((1 - core[0]) * (D // 2), D // 2), D // 2)


def fetch_halves(copies, pieces, target, start_of):
    half = pieces[0].shape[0]
    out = []
    for r, piece in enumerate(pieces):
        at = start_of(r // 2) + r % 2 * half
        out.append(copies.start(piece, target.at[pl.ds(at, half), :]))
    return out


def fetch_pieces(copies, pieces, target, start_of, halved=True):
    rows = pieces[0].shape[0]
    out = []
    for r, piece in enumerate(pieces):
        if halved and r == len(pieces) - 1:
            at = start_of(r - 1) + rows // 2
        else:
            at = start_of(r)
        out.append(copies.start(piece, target.at[pl.ds(at, piece.shape[0]), :]))
    return out


def write_part(copies, buffer, parts, r, halved=True):
    n = len(parts) - halved
    rows = parts[0].shape[0]
    start = r * rows
    if halved and r == n - 1:
        half = rows // 2
        copies.write(buffer.at[pl.ds(start, half), :], parts[n - 1])
        copies.write(buffer.at[pl.ds(start + half, half), :], parts[n])
    else:
        copies.write(buffer.at[pl.ds(start, rows), :], parts[r])


def store_part(parts, r, values):
    n = len(parts) - 1
    if r < n - 1:
        parts[r][...] = values
    else:
        half = values.shape[0] // 2
        parts[n - 1][...] = values[:half]
        parts[n][...] = values[half:]


def assemble(pieces, target, start_of):
    n = len(pieces) - 1
    rows = pieces[0].shape[0]
    half = rows // 2
    for r in range(n - 1):
        target[pl.ds(start_of(r), rows), :] = pieces[r][...]
    start = start_of(n - 1)
    target[pl.ds(start, half), :] = pieces[n - 1][...]
    target[pl.ds(start + half, half), :] = pieces[n][...]


def segment_of(positions, ends):
    return sum((positions >= e).astype(jnp.int32) for e in ends)


def row_ends(lengths):
    first = lengths[0, 0]
    second = first + lengths[0, 1]
    return (first, second, second + lengths[0, 2])


class Block:
    def __init__(self, b, ends):
        start = b * BLOCK
        rows = lax.broadcasted_iota(jnp.int32, (BLOCK, BLOCK), 0)
        columns = lax.broadcasted_iota(jnp.int32, (BLOCK, BLOCK), 1)
        seg_rows = segment_of(rows + start, ends)
        seg_columns = segment_of(columns + start, ends)
        same = seg_rows == seg_columns
        self.mask = jnp.logical_and(same, rows >= columns)
        self.mask_t = jnp.logical_and(same, columns >= rows)
        self.last = segment_of(start + BLOCK - 1, ends)
        self.earlier = segment_of(start - 1, ends) if b > 0 else -1
        wide_rows = lax.broadcasted_iota(jnp.int32, (BLOCK, HEAD_DIM), 0)
        segments = segment_of(wide_rows + start, ends)
        self.from_state = segments == self.earlier
        self.to_state = segments == self.last

    def decay(self, full):
        return jnp.where(self.mask, full, 0.0)

    def keeping(self, rate):
        factor = jnp.exp(jnp.full((HEAD_DIM, HEAD_DIM), -rate * BLOCK, F32))
        return jnp.where(self.last == self.earlier, factor, 0.0)


def full_decay(rate, turned=False):
    rows = lax.broadcasted_iota(jnp.int32, (BLOCK, BLOCK), int(turned))
    columns = lax.broadcasted_iota(jnp.int32, (BLOCK, BLOCK), 1 - int(turned))
    return jnp.exp(-rate * jnp.maximum(rows - columns, 0).astype(F32))


def edge_factors(rate):
    rows = lax.broadcasted_iota(jnp.int32, (BLOCK, HEAD_DIM), 0).astype(F32)
    return jnp.exp(-rate * (rows + 1.0)), jnp.exp(-rate * (BLOCK - 1.0 - rows))


def silu16(values):
    return (values * jax.nn.sigmoid(values)).astype(BF16)


def silu_grad(before):
    sigmoid = jax.nn.sigmoid(before)
    return sigmoid * (1.0 + before * (1.0 - sigmoid))


def entry_kernel(n, heads, order, core, lengths, rates, *refs):
    pieces, refs = refs[: 2 * n], refs[2 * n :]
    weights, mixer, refs = refs[:4], refs[4], refs[5:]
    normed_out, normed_send, proj_out, mixed_out, squares, states_out, refs = *refs[:6], refs[6:]
    parts, refs = refs[: n + 1], refs[n + 1 :]
    normed, weight_in, mixer_in, proj, mixed, pre, states, buffer, semaphores = refs
    copies = Copies(semaphores)
    rows = 2 * pieces[0].shape[0]
    total = n * rows
    width = heads * HEAD_DIM
    coming = fetch_halves(
        copies, pieces, normed, lambda r: pl.multiple_of(order[0, r] * rows, rows)
    )
    for copy in coming:
        copy.wait()
    fetched = [copies.start(w, weight_in.at[i]) for i, w in enumerate(weights)]
    mixer_copy = copies.start(mixer, mixer_in)
    copies.write(normed, normed_out)
    copies.write(normed.at[:, other_half(core)], normed_send)
    for i in range(4):
        fetched[i].wait()
        for b in range(total // BLOCK):
            here = pl.ds(b * BLOCK, BLOCK)
            proj[here, i * width : (i + 1) * width] = dot(normed[here, :], weight_in[i])
    copies.write(proj, proj_out)
    ends = row_ends(lengths)
    fulls = [full_decay(rates[h]) for h in range(heads)]
    edges = [edge_factors(rates[h]) for h in range(heads)]
    state = [jnp.zeros((HEAD_DIM, HEAD_DIM), F32) for _ in range(heads)]
    ones = jnp.ones((8, HEAD_DIM), BF16)
    for b in range(total // BLOCK):
        here = pl.ds(b * BLOCK, BLOCK)
        block = Block(b, ends)
        square = jnp.zeros((8, BLOCK), F32)
        for h in range(heads):
            at = [slice(i * width + h * HEAD_DIM, i * width + (h + 1) * HEAD_DIM) for i in range(4)]
            query, key = silu16(proj[here, at[0]]), silu16(proj[here, at[1]])
            value = proj[here, at[2]].astype(BF16)
            inner, carried = edges[h]
            inner = jnp.where(block.from_state, inner, 0.0)
            carried = jnp.where(block.to_state, carried, 0.0)
            states[b, h] = state[h]
            weight = (dot(query, key, NT) * block.decay(fulls[h])).astype(BF16)
            high, low = split(state[h])
            out = dot(weight, value) + inner * (dot(query, high) + dot(query, low))
            state[h] = block.keeping(rates[h]) * state[h] + dot(
                (key.astype(F32) * carried).astype(BF16), value, TN
            )
            mixed[here, at[0]] = out
            pre[here, at[0]] = (out * proj[here, at[3]]).astype(BF16)
            high, low = split(out * out)
            square += dot(ones, high, NT) + dot(ones, low, NT)
        squares[:, here] = square[0:1]
    copies.write(mixed, mixed_out)
    copies.write(states, states_out)
    mixer_copy.wait()
    for r in reversed(range(0, n, 2)):
        both = jnp.concatenate(
            [pre[pl.ds(pl.multiple_of(order[0, q] * rows, rows), rows), :] for q in (r, r + 1)], 0
        )
        buffer[r * rows : (r + 2) * rows, :] = dot(both, mixer_in[...]).astype(BF16)
        write_part(copies, buffer, parts, r + 1)
        write_part(copies, buffer, parts, r)
    copies.drain()


def column(row):
    return jnp.transpose(jnp.broadcast_to(row, (HEAD_DIM, row.shape[1])))


def exit_kernel(n, heads, order, core, lengths, rates, *refs):
    pieces, refs = refs[: n + 1], refs[n + 1 :]
    weights, mixer_hbm, refs = refs[:4], refs[4], refs[5:]
    proj_hbm, mixed_hbm, states_hbm, inverses, refs = *refs[:4], refs[4:]
    entry_out, send_out, keep_out, refs = *refs[:3], refs[3:]
    parts, refs = refs[:3], refs[3:]
    resid, weight_in, mixer, proj, mixed, states, scaled, entry_g, scaled_g, buffer, send, keep, sems = refs
    copies = Copies(sems)
    rows = pieces[0].shape[0]
    total = n * rows
    width = heads * HEAD_DIM
    mixer_copy = copies.start(mixer_hbm, mixer)
    coming = fetch_pieces(
        copies, pieces, resid, lambda r: pl.multiple_of(order[0, r] * rows, rows)
    )
    mixer_copy.wait()
    for copy in coming:
        copy.wait()
    saved = [
        copies.start(a, b)
        for a, b in ((proj_hbm, proj), (mixed_hbm, mixed), (states_hbm, states))
    ]
    fetched = [
        copies.start(w, weight_in.at[:, i * width : (i + 1) * width]) for i, w in enumerate(weights)
    ]
    for b in range(total // BLOCK):
        here = pl.ds(b * BLOCK, BLOCK)
        scaled_g[here, :] = dot(resid[here, :D], mixer[...], NT)
    for copy in saved:
        copy.wait()
    ends = row_ends(lengths)
    fulls = [full_decay(rates[h]) for h in range(heads)]
    turned = [full_decay(rates[h], True) for h in range(heads)]
    edges = [edge_factors(rates[h]) for h in range(heads)]
    later = [jnp.zeros((HEAD_DIM, HEAD_DIM), F32) for _ in range(heads)]
    for b in reversed(range(total // BLOCK)):
        here = pl.ds(b * BLOCK, BLOCK)
        block = Block(b, ends)
        inverse = column(inverses[:, here])
        coded = resid[here, D : D + 128].astype(F32)
        mean = (coded[:, 0:1] + coded[:, 1:2] + coded[:, 2:3]) * (1.0 / D)
        for h in range(heads):
            at = [slice(i * width + h * HEAD_DIM, i * width + (h + 1) * HEAD_DIM) for i in range(4)]
            query_pre, key_pre = proj[here, at[0]], proj[here, at[1]]
            query, key = silu16(query_pre), silu16(key_pre)
            value = proj[here, at[2]].astype(BF16)
            gate = proj[here, at[3]]
            grad_s = scaled_g[here, at[0]]
            unit = mixed[here, at[0]] * inverse
            scaled[here, at[0]] = (unit * gate).astype(BF16)
            entry_g[here, at[3]] = (grad_s * unit).astype(BF16)
            grad = (inverse * (grad_s * gate - unit * mean)).astype(BF16)
            inner, carried = edges[h]
            inner = jnp.where(block.from_state, inner, 0.0)
            carried = jnp.where(block.to_state, carried, 0.0)
            decay = block.decay(fulls[h])
            decay_t = jnp.where(block.mask_t, turned[h], 0.0)
            weight_t = (dot(key, query, NT) * decay_t).astype(BF16)
            score = (dot(grad, value, NT) * decay).astype(BF16)
            score_t = (dot(value, grad, NT) * decay_t).astype(BF16)
            high, low = split(states[b, h])
            query_g = dot(score, key) + inner * (dot(grad, high, NT) + dot(grad, low, NT))
            high, low = split(later[h])
            key_g = dot(score_t, query) + carried * (dot(value, high, NT) + dot(value, low, NT))
            value_g = dot(weight_t, grad) + carried * (dot(key, high) + dot(key, low))
            later[h] = (
                dot((query.astype(F32) * inner).astype(BF16), grad, TN)
                + block.keeping(rates[h]) * later[h]
            )
            entry_g[here, at[0]] = (query_g * silu_grad(query_pre)).astype(BF16)
            entry_g[here, at[1]] = (key_g * silu_grad(key_pre)).astype(BF16)
            entry_g[here, at[2]] = value_g.astype(BF16)
    copies.write(entry_g, entry_out)
    send[...] = dot(scaled[...], resid[:, other_half(core)], TN).astype(BF16)
    copies.write(send, send_out)
    keep[...] = dot(scaled[...], resid[:, own_half(core)], TN)
    copies.write(keep, keep_out)
    for copy in fetched:
        copy.wait()
    both = jnp.concatenate(
        [
            entry_g[pl.ds(pl.multiple_of(order[0, q] * rows, rows), rows), :]
            for q in (n - 2, n - 1)
        ],
        0,
    )
    buffer[...] = dot(both, weight_in[...], NT).astype(BF16)
    half = rows // 2
    for part, (low, high) in zip(parts, ((0, rows), (rows, rows + half), (rows + half, 2 * rows))):
        copies.write(buffer.at[pl.ds(low, high - low), :], part)
    copies.drain()


def project_kernel(n, order, *refs):
    entry_hbm, weights, refs = refs[0], refs[1:5], refs[5:]
    parts, refs = refs[: n - 2], refs[n - 2 :]
    entry_g, weight_in, buffer, sems = refs
    copies = Copies(sems)
    rows = parts[0].shape[0]
    width = weights[0].shape[1]
    coming = [
        copies.start(w, weight_in.at[:, i * width : (i + 1) * width]) for i, w in enumerate(weights)
    ] + [copies.start(entry_hbm, entry_g)]
    for copy in coming:
        copy.wait()
    for r in reversed(range(0, n - 2, 2)):
        both = jnp.concatenate(
            [entry_g[pl.ds(pl.multiple_of(order[0, q] * rows, rows), rows), :] for q in (r, r + 1)],
            0,
        )
        buffer[r * rows : (r + 2) * rows, :] = dot(both, weight_in[...], NT).astype(BF16)
        for q in (r + 1, r):
            copies.write(buffer.at[pl.ds(q * rows, rows), :], parts[q])
    copies.drain()


def cotangent_kernel(n, core, *refs):
    pieces, down, grad, grad_send, *products = refs[: n + 1], *refs[n + 1 :]
    rows = pieces[0].shape[0]
    assemble(pieces, grad, lambda r: r * rows)
    grad_send[...] = grad[:, other_half(core)]
    for r, out in enumerate(products):
        out[...] = dot(grad[pl.ds(2 * r * rows, 2 * rows), :], down[...], NT)


def hidden_kernel(index, halved, core, *refs):
    count = 2 + halved
    pieces, refs = refs[:count], refs[count:]
    first, second, product_g, refs = *refs[:3], refs[3:]
    refs = refs if index == 0 else refs[4:]
    (normed_out, product_out, second_out, bundle), refs = refs[:4], refs[4:]
    parts, refs = refs[:count], refs[count:]
    normed, product, first_g, second_g, sems = refs
    copies = Copies(sems)
    low = 0
    for piece in pieces:
        normed[low : low + piece.shape[0], :] = piece[...]
        low += piece.shape[0]
    units, padded = first.shape[0], product.shape[1]
    if padded > units:
        for ref in (product, first_g, second_g):
            ref[:, units:] = jnp.zeros((low, padded - units), BF16)
    here = pl.ds(index * low, low)
    copies.write(normed, normed_out.at[here, :])
    copies.write(normed.at[:, other_half(core)], bundle.at[here, pl.ds(padded, D // 2)])
    tokens = normed[...]
    first_act, second_act = dot(tokens, first[...], NT), dot(tokens, second[...], NT)
    product[:, :units] = (first_act * second_act).astype(BF16)
    copies.write(product, product_out.at[here, :])
    grad = product_g[...]
    one, two = (grad * second_act).astype(BF16), (grad * first_act).astype(BF16)
    first_g[:, :units] = one
    copies.write(first_g, bundle.at[here, pl.ds(0, padded)])
    second_g[:, :units] = two
    copies.write(second_g, second_out.at[here, :])
    result = (dot(one, first[...]) + dot(two, second[...])).astype(BF16)
    low = 0
    for part in parts:
        part[...] = result[low : low + part.shape[0]]
        low += part.shape[0]
    copies.drain()


def down_kernel(n, product, down, *parts):
    rows, units = parts[0].shape[0], down.shape[0]
    for r in range(0, n, 2):
        result = dot(product[pl.ds(r * rows, 2 * rows), :units], down[...]).astype(BF16)
        store_part(parts, r, result[:rows])
        store_part(parts, r + 1, result[rows:])


def norm_kernel(tokens, *halves):
    out = normalize(tokens[...].astype(F32)).astype(BF16)
    half = halves[0].shape[0]
    halves[0][...] = out[:half]
    halves[1][...] = out[half:]


def middle_kernel(tokens, near, left, right, inverse, attn, hidden, normed):
    whole = near[...].astype(F32) + left[...].astype(F32) + right[...].astype(F32)
    whole = whole * inverse[...]
    attn[...] = whole
    whole = tokens[...].astype(F32) + whole
    hidden[...] = whole
    normed[...] = normalize(whole).astype(BF16)


def resid_kernel(low, grad, hidden, near, left, right, attn, hidden_g, coded):
    rows = grad.shape[0]
    here = slice(low, low + rows)
    normed_g = near[...].astype(F32) + left[here, :].astype(F32) + right[here, :].astype(F32)
    whole = grad[...].astype(F32) + norm_grad(hidden[...], normed_g)
    hidden_g[...] = whole
    resid = whole.astype(BF16)
    coded[:, :D] = resid
    inner = jnp.sum(resid.astype(F32) * attn[...], axis=1, keepdims=True)
    lane = lax.broadcasted_iota(jnp.int32, (1, 128), 1)
    out = jnp.zeros((rows, 128), F32)
    for i in range(3):
        high = inner.astype(BF16).astype(F32)
        out += jnp.where(lane == i, high, 0.0)
        inner -= high
    coded[:, D:] = out.astype(BF16)


def output_kernel(tokens, attn, ffn, valid_rows, output, sums):
    rows = tokens.shape[0]
    valid = lax.broadcasted_iota(jnp.int32, (rows, 1), 0) < valid_rows[0]
    tokens_wide = tokens[...].astype(F32)
    output[...] = (tokens_wide + attn[...] + ffn[...]).astype(BF16)
    lane = lax.broadcasted_iota(jnp.int32, (1, 128), 1)
    out = jnp.zeros((1, 128), F32)
    for i, values in enumerate((tokens_wide, attn[...], ffn[...])):
        per_row = jnp.sum(values * values, axis=1, keepdims=True)
        whole = jnp.sum(jnp.where(valid, per_row, 0.0), axis=0, keepdims=True)
        out += jnp.where(lane == i, whole, 0.0)
    counted = jnp.clip(valid_rows[0], 0, rows).astype(F32)
    sums[...] = out + jnp.where(lane == 3, counted, 0.0)


def local(
    tokens_in,
    query_weight,
    key_weight,
    value_weight,
    gate_weight,
    mixer_weight,
    first_weight,
    second_weight,
    down_weight,
    doc_lengths,
    head_decay,
    out_grad,
):
    n = lax.axis_size("narrow")
    rows = tokens_in.shape[0]
    total = rows * n
    heads = head_decay.shape[0]
    width = heads * HEAD_DIM
    units = first_weight.shape[1]
    me = lax.axis_index("narrow")
    core = lax.axis_index("wide") % 2
    start_row = me * rows
    order = lax.dynamic_slice(jnp.asarray(order_table(n)), (me, 0), (1, n))
    where = core.reshape(1)
    entry_weights = (query_weight, key_weight, value_weight, gate_weight)
    tokens_wide = tokens_in.astype(F32)
    rates = head_decay

    half_rows = total // 2
    blocks = total // BLOCK
    first_t, second_t = first_weight.T, second_weight.T
    valid_rows = (jnp.sum(doc_lengths[0, : NDOC - 1]) - start_row).reshape(1)

    half_shapes = [((rows // 2, D), BF16)] * 2
    halves = call(norm_kernel, half_shapes, [VMEM], 6 * rows * D, 14 * MIB)(tokens_in)
    pieces = [v for pair in Gather2(halves, n).finish() for v in pair]
    shapes = [
        ((total, D), BF16),
        ((total, D // 2), BF16),
        ((total, 4 * width), F32),
        ((total, width), F32),
        ((1, total), F32),
        ((blocks, heads, HEAD_DIM, HEAD_DIM), F32),
    ] + part_shapes(n, rows)
    *pieces, grad_own = barrier(*pieces, out_grad)
    cotangent = Gather(grad_own, n).step()
    normed, normed_send, proj, mixed, squares, states, *parts = call(
        functools.partial(entry_kernel, n, heads),
        shapes,
        [SMEM] * 4 + [ANY] * (2 * n + 5),
        12 * total * D * width,
        54 * MIB,
        [
            pltpu.VMEM((total, D), BF16),
            pltpu.VMEM((4, D, width), BF16),
            pltpu.VMEM((width, D), BF16),
            pltpu.VMEM((total, 4 * width), F32),
            pltpu.VMEM((total, width), F32),
            pltpu.VMEM((total, width), BF16),
            pltpu.VMEM((blocks, heads, HEAD_DIM, HEAD_DIM), F32),
            pltpu.VMEM((total, D), BF16),
            pltpu.SemaphoreType.DMA((3 * n + 13,)),
        ],
        [VMEM if i == 4 else ANY for i in range(len(shapes))],
    )(order, where, doc_lengths, rates, *pieces, *entry_weights, mixer_weight)
    squares, cotangent.left, cotangent.right, *parts = barrier(
        squares, cotangent.left, cotangent.right, *parts
    )
    scatter = Scatter(parts, n)
    hop = Butterfly(squares, "narrow")
    while cotangent.left_steps:
        scatter.step()
        cotangent.step()
        hop.step()
        meet(scatter, cotangent, hop)
    squares = hop.finish()
    grad_pieces = cotangent.pieces
    inverses = lax.rsqrt(squares / D + EPS)
    inverse_own = lax.dynamic_slice(inverses, (0, start_row), (1, rows)).reshape(rows, 1)
    near, left, right = scatter.finish()
    attn_own, hidden_own, normed_own = call(
        middle_kernel,
        [((rows, D), F32)] * 2 + [((rows, D), BF16)],
        [VMEM] * 5,
        12 * rows * D,
        14 * MIB,
    )(tokens_in, near, left, right, inverse_own)

    padded = -(-units // 128) * 128

    def hidden(index, pieces):
        halved = index == n // 2 - 1
        half_row = rows // 2
        part_rows = [rows, half_row, half_row] if halved else [rows, rows]
        count = len(part_rows)
        outs = call(
            functools.partial(hidden_kernel, index, halved),
            [((total, D), BF16)]
            + [((total, padded), BF16)] * 2
            + [((total, padded + D // 2), BF16)]
            + [((p, D), BF16) for p in part_rows],
            [SMEM] + [VMEM] * (count + 3) + [ANY] * len(whole),
            16 * rows * D * units,
            40 * MIB,
            [pltpu.VMEM((2 * rows, D), BF16)]
            + [pltpu.VMEM((2 * rows, padded), BF16)] * 3
            + [pltpu.SemaphoreType.DMA((5,))],
            [ANY] * 4 + [VMEM] * count,
            {count + 4 + i: i for i in range(len(whole))},
        )(where, *pieces, first_t, second_t, product_g[index], *whole)
        return outs[:4], list(outs[4:])

    normed_own, grad_pieces = lax.optimization_barrier((normed_own, grad_pieces))
    gather = Gather(normed_own, n).step()
    grad_all, grad_send, *product_g = call(
        functools.partial(cotangent_kernel, n),
        [((total, D), BF16), ((total, D // 2), BF16)] + [((2 * rows, units), F32)] * (n // 2),
        [SMEM] + [VMEM] * (n + 2),
        2 * total * D * units,
        22 * MIB,
    )(where, *grad_pieces, down_weight)
    gather.left, gather.right, grad_send, normed_send, product_g = lax.optimization_barrier(
        (gather.left, gather.right, grad_send, normed_send, product_g)
    )
    whole, parts = [], []
    for i in range(n // 2 - 1):
        pieces = gather.pieces[2 * i : 2 * i + 2]
        gather.step()
        whole, new_parts = hidden(i, pieces)
        if i == 0:
            normed_other = swap(normed_send, "wide", 1)
            gather.left, gather.right, normed_other, new_parts = lax.optimization_barrier(
                (gather.left, gather.right, normed_other, new_parts)
            )
        parts += new_parts
    grad_other = swap(grad_send, "wide", 1)
    *pieces, grad_other = barrier(*gather.pieces[n - 2 :], grad_other)
    whole, new_parts = hidden(n // 2 - 1, pieces)
    parts += new_parts
    normed2, product, second_g, bundle = whole

    scatter = Scatter(parts, n)
    stream = Together(scatter)
    half = D // 2
    cut_at = [(0, 384, 768, half), (0, half), (0, 512, half)]
    cuts = [tuple(zip(at[:-1], at[1:])) for at in cut_at]

    (product_other, bundle_other), _ = region(
        [stream], [(product, "wide", 1), (bundle, "wide", 1)]
    )
    (second_other_g,), down_own = region(
        [stream],
        [(second_g, "wide", 1)],
        lambda *v: own_columns(core, cuts[0], units, *v),
        [product, product_other, grad_all, grad_other],
    )
    down_in, first_in, second_in = [], [], []
    (received,), first_own = region(
        [stream],
        [(down_own[0], "wide", 2)],
        lambda *v: own_columns(core, cuts[1], units, *v, v[1], low=padded),
        [bundle, bundle_other, normed2],
    )
    down_in.append(received)
    (received,), second_own = region(
        [stream],
        [(down_own[1], "wide", 2)],
        lambda *v: own_columns(core, cuts[2], units, *v, low=padded),
        [second_g, second_other_g, normed2, bundle_other],
    )
    down_in.append(received)
    while scatter.left_steps:
        region([stream])
    left, right, low, _ = scatter.received
    hidden_g, resid_own = call(
        functools.partial(resid_kernel, low),
        [((rows, D), F32), ((rows, D + 128), BF16)],
        [VMEM] * 6,
        20 * rows * D,
        14 * MIB,
    )(out_grad, hidden_own, scatter.near[0], left, right, attn_own)

    gather = Gather(resid_own, n)

    def mixed_pairs(owns, ins):
        return [v for pair in zip(owns, ins) for v in pair]

    def output_parts(product):
        return call(
            functools.partial(down_kernel, n),
            part_shapes(n, rows),
            [VMEM] * 2,
            2 * total * D * units,
            14 * MIB,
        )(product, down_weight)

    down_own, first_own = list(down_own), list(first_own)
    resid_own, product, down_own[2], first_own[0] = barrier(
        resid_own, product, down_own[2], first_own[0]
    )
    gather = Gather(resid_own, n).step(n // 2 - 1)
    parts = output_parts(product)
    down_in.append(swap(down_own[2], "wide", 2))
    first_in = swap(first_own[0], "wide", 2)
    gather.left, gather.right, parts, down_in[2], first_in = lax.optimization_barrier(
        (gather.left, gather.right, parts, down_in[2], first_in)
    )
    scatter2 = Scatter(parts, n)
    stream2 = Together(scatter2)
    (received,), (first_total, down_total) = region(
        [gather, stream2],
        [(second_own[0], "wide", 2)],
        lambda own, other, *v: (summed(own, other), summed(*v)),
        [first_own[0], first_in, *mixed_pairs(down_own, down_in)],
    )
    second_in.append(received)

    shapes = [
        ((total, 4 * width), BF16),
        ((width, D // 2), BF16),
        ((width, D // 2), F32),
        ((rows, D), BF16),
        ((rows // 2, D), BF16),
        ((rows // 2, D), BF16),
    ]
    leave = call(
        functools.partial(exit_kernel, n, heads),
        shapes,
        [SMEM] * 4 + [ANY] * (n + 9) + [VMEM],
        12 * total * D * width,
        60 * MIB,
        [
            pltpu.VMEM((total, D + 128), BF16),
            pltpu.VMEM((D, 4 * width), BF16),
            pltpu.VMEM((width, D), BF16),
            pltpu.VMEM((total, 4 * width), F32),
            pltpu.VMEM((total, width), F32),
            pltpu.VMEM((blocks, heads, HEAD_DIM, HEAD_DIM), F32),
            pltpu.VMEM((total, width), BF16),
            pltpu.VMEM((total, 4 * width), BF16),
            pltpu.VMEM((total, width), F32),
            pltpu.VMEM((2 * rows, D), BF16),
            pltpu.VMEM((width, D // 2), BF16),
            pltpu.VMEM((width, D // 2), F32),
            pltpu.SemaphoreType.DMA((2 * n + 15,)),
        ],
        [ANY] * len(shapes),
    )
    (received, first_other, down_other), (entry_g, mixer_send, mixer_keep, *parts) = region(
        [stream2],
        [(second_own[1], "wide", 2), (first_total, "wide", 1), (down_total, "wide", 1)],
        lambda inverses, *pieces: leave(
            order,
            where,
            doc_lengths,
            rates,
            *pieces,
            *entry_weights,
            mixer_weight,
            proj,
            mixed,
            states,
            inverses,
        ),
        [inverses, *gather.pieces],
    )
    second_in.append(received)

    far = parts
    scatter = Scatter(part_shapes(n, rows)[: n - 2] + far, n)
    stream = Together(scatter2, scatter)

    def mixer_work(keep, crossed_send, entry_g, normed, normed_other):
        (mixer_own,) = call(
            add_kernel, [(keep.shape, BF16)], [VMEM] * 2, keep.size, 14 * MIB
        )(keep, swap(crossed_send, "wide", 1))
        mixer_in = swap(mixer_own, "wide", 2)
        entry_other = swap(entry_g, "wide", 1)
        parts = call(
            functools.partial(project_kernel, n),
            part_shapes(n, rows)[: n - 2],
            [SMEM] + [ANY] * 5,
            6 * total * D * width,
            48 * MIB,
            [
                pltpu.VMEM((total, 4 * width), BF16),
                pltpu.VMEM((D, 4 * width), BF16),
                pltpu.VMEM((total - 2 * rows, D), BF16),
                pltpu.SemaphoreType.DMA((n + 4,)),
            ],
            [ANY] * (n - 2),
        )(order, entry_g, *entry_weights)
        owns = own_rows(core, 2, 2, width, normed, normed_other, entry_g, entry_other)
        return mixer_own, mixer_in, owns, entry_other, parts

    _, (mixer_own, mixer_in, (value_own, gate_own), entry_other, parts) = region(
        [stream],
        [],
        mixer_work,
        [mixer_keep, mixer_send, entry_g, normed, normed_other],
    )
    scatter.near.update({d: parts[i] for i, d in enumerate(distances(n)[:-2])})

    def entry_work(normed, normed_other, entry_g, entry_other, *values):
        mixer_total = summed(*values[:2])
        mixer_other = swap(mixer_total, "wide", 1)
        owns = own_rows(core, 0, 2, width, normed, normed_other, entry_g, entry_other)
        first_w = place(core, *values[2:4], False)
        down_w = place(core, *values[4:6], False)
        return owns, mixer_total, mixer_other, first_w, down_w, summed(*values[6:])

    (gate_in, value_in), work_out = region(
        [stream],
        [(gate_own, "wide", 2), (value_own, "wide", 2)],
        entry_work,
        [normed, normed_other, entry_g, entry_other, mixer_own, mixer_in]
        + [first_total, first_other, down_total, down_other]
        + mixed_pairs(second_own, second_in),
    )
    (query_own, key_own), mixer_total, mixer_other, first_w, down_w, second_total = work_out
    while scatter2.left_steps:
        region([stream])
    ffn_own = scatter2.result
    stream = Together(scatter)

    def output_work(tokens_in, attn_own, ffn_own, a, b, *pairs):
        output, stats = call(
            output_kernel,
            [((rows, D), BF16), ((1, 128), F32)],
            [VMEM] * 3 + [SMEM],
            6 * rows * D,
            14 * MIB,
        )(tokens_in, attn_own, ffn_own, valid_rows)
        stats = stats + swap(stats, "narrow", 1)
        return output, stats, place(core, a, b, False), summed(*pairs)

    (key_in, second_other), (output, stats, mixer_w, pair_total) = region(
        [stream],
        [(key_own, "wide", 2), (second_total, "wide", 1)],
        output_work,
        [tokens_in, attn_own, ffn_own, mixer_total, mixer_other]
        + [gate_own, gate_in, value_own, value_in],
    )
    (query_in, pair_other, hop), (second_w, key_total) = region(
        [stream],
        [(query_own, "wide", 2), (pair_total, "wide", 1), (stats, "narrow", 2)],
        lambda own, other, *v: (place(core, own, other, False), summed(*v)),
        [second_total, second_other, key_own, key_in],
    )
    stats = stats + hop
    while scatter.left_steps:
        region([stream])
    normed_g = scatter.result

    (key_other, hop), (query_total, (gate_w, value_w)) = region(
        [],
        [(key_total, "wide", 1), (stats, "narrow", 4)],
        lambda a, b, *v: (summed(a, b), place_two(core, *v)),
        [query_own, query_in, pair_total, pair_other],
    )
    stats = stats + hop
    query_other = swap(query_total, "wide", 1)
    for axis, bit in (("narrow", 8), ("wide", 1)):
        while bit < lax.axis_size(axis):
            stats = stats + swap(stats, axis, bit)
            bit *= 2
    input_grad = hidden_g + norm_grad(tokens_wide, normed_g)
    key_w = place(core, key_total, key_other, True)
    query_w = place(core, query_total, query_other, True)
    stream_rms = jnp.sqrt(stats[0, :3] / (stats[0, 3] * D))
    return (
        output,
        input_grad,
        query_w,
        key_w,
        value_w,
        gate_w,
        mixer_w,
        first_w.T,
        second_w.T,
        down_w,
        stream_rms,
    )


def solution(mesh):
    split_tokens = P(("wide", "narrow"), None)
    columns, rows = P(None, "narrow"), P("narrow", None)
    return jax.shard_map(
        local,
        mesh=mesh,
        in_specs=(split_tokens,)
        + (columns,) * 4
        + (rows, columns, columns, rows, P("wide", None), P("narrow"), split_tokens),
        out_specs=(split_tokens,) * 2 + (columns,) * 4 + (rows, columns, columns, rows, P()),
        check_vma=False,
    )
```

```python
import functools

import jax
import jax.numpy as jnp
import numpy as np
from jax import lax
from jax.experimental import pallas as pl
from jax.experimental.pallas import tpu as pltpu
from jax.sharding import PartitionSpec as P

D = 2048
HEAD_DIM = 128
NDOC = 4
EPS = 1e-06
BLOCK = 256
MIB = 1 << 20

F32 = jnp.float32
BF16 = jnp.bfloat16
NN = (((1,), (0,)), ((), ()))
NT = (((1,), (1,)), ((), ()))
TN = (((0,), (0,)), ((), ()))
VMEM = pl.BlockSpec(memory_space=pltpu.VMEM)
SMEM = pl.BlockSpec(memory_space=pltpu.SMEM)
ANY = pl.BlockSpec(memory_space=pl.ANY)


def dot(a, b, dims=NN):
    return lax.dot_general(a, b, dims, preferred_element_type=F32)


def split(values):
    high = values.astype(BF16)
    return high, (values - high.astype(F32)).astype(BF16)


def normalize(values):
    return values * lax.rsqrt(jnp.mean(values * values, axis=-1, keepdims=True) + EPS)


def norm_grad(values, grad_in):
    inverse = lax.rsqrt(jnp.mean(values * values, axis=-1, keepdims=True) + EPS)
    normed = values * inverse
    return inverse * (grad_in - normed * jnp.mean(grad_in * normed, axis=-1, keepdims=True))


def ring_order(n):
    if n == 16:
        return [r * 4 + (c if r % 2 == 0 else 3 - c) for r in range(4) for c in range(4)]
    return list(range(0, n, 2)) + list(range(n - 1, 0, -2))


def distances(n):
    out = [0]
    for k in range(1, n // 2):
        out += [-k, k]
    return out + [n // 2]


def order_table(n):
    ring = ring_order(n)
    place = {device: i for i, device in enumerate(ring)}
    return np.array(
        [[ring[(place[me] + d) % n] for d in distances(n)] for me in range(n)], np.int32
    )


def onward(values, n):
    ring = ring_order(n)
    return lax.ppermute(values, "narrow", [(ring[i], ring[(i + 1) % n]) for i in range(n)])


def backward(values, n):
    ring = ring_order(n)
    return lax.ppermute(values, "narrow", [(ring[(i + 1) % n], ring[i]) for i in range(n)])


def barrier(*values):
    return lax.optimization_barrier(values)


def add16(a, b):
    return (a.astype(F32) + b.astype(F32)).astype(BF16)


class Gather:
    def __init__(self, own, n):
        self.n, self.left_steps = n, n // 2
        self.left = self.right = own
        self.pieces = [own]

    def outgoing(self):
        if self.left_steps == 1:
            half = self.left.shape[0] // 2
            return self.left[:half], self.right[half:]
        return self.left, self.right

    def incoming(self, left, right):
        self.left_steps -= 1
        self.left, self.right = left, right
        self.pieces += [left, right]

    def step(self, count=1):
        for _ in range(count):
            left, right = self.outgoing()
            self.incoming(onward(left, self.n), backward(right, self.n))
        return self

    def finish(self):
        return self.step(self.left_steps).pieces


class Gather2:
    def __init__(self, halves, n):
        self.n, self.left_steps = n, n // 2
        self.left, self.right = list(halves), list(halves)
        self.pieces = [list(halves)]

    def step(self, count=1):
        for _ in range(count):
            self.left_steps -= 1
            if self.left_steps == 0:
                self.pieces.append([onward(self.left[0], self.n), backward(self.right[1], self.n)])
                return self
            for i in range(2):
                self.left[i] = onward(self.left[i], self.n)
                self.right[i] = backward(self.right[i], self.n)
            self.pieces += [list(self.left), list(self.right)]
        return self

    def finish(self):
        return self.step(self.left_steps).pieces


def merge_kernel(layout, *refs):
    outs, refs = refs[-2:], list(refs[:-2])
    at = 0
    for rows, half, offset in layout:
        if offset is None:
            for out in outs:
                out[at : at + rows] = refs.pop(0)[...]
        else:
            nears, parts, refs = refs[:2], refs[2:4], refs[4:]
            for i in range(2):
                low = half * i if half < rows else 0
                outs[i][at : at + rows] = nears[i][...]
                outs[i][at + low : at + low + half] = add16(
                    nears[i][low : low + half], parts[i][offset : offset + half]
                )
        at += rows


def join_one(low, near, part, out):
    rows = part.shape[0]
    out[...] = near[...]
    out[low : low + rows] = add16(near[low : low + rows], part[...])


class Scatter:
    def __init__(self, parts, n):
        self.n, self.left_steps = n, n // 2
        self.near = {d: parts[i] for i, d in enumerate(distances(n)[:-1])}
        self.left, self.right = parts[-2], parts[-1]
        self.received = None

    def operands(self):
        if self.received is None:
            return [self.left, self.right], (self.left.shape[0], 0, None)
        left, right, offset, half = self.received
        near = [self.near[self.left_steps], self.near[-self.left_steps]]
        return near + [left, right], (near[0].shape[0], half, offset)

    def take(self, left, right, offset, rows):
        self.left_steps -= 1
        if self.left_steps == 0:
            at = slice(offset, offset + rows)
            self.result = self.near[0].astype(F32) + left[at].astype(F32) + right[at].astype(F32)
        self.received = (left, right, offset, rows)

    def step(self, count=1):
        for _ in range(count):
            self.left_steps -= 1
            left, right = onward(self.left, self.n), backward(self.right, self.n)
            k = self.left_steps
            shape = self.near[k].shape
            if k == 0:
                self.result = (self.near[0], left, right)
            elif shape == left.shape:
                self.left, self.right = add16(self.near[k], left), add16(self.near[-k], right)
            else:
                half = shape[0] // 2
                self.left, self.right = [
                    call(
                        functools.partial(join_one, low),
                        [(shape, BF16)],
                        [VMEM] * 2,
                        shape[0] * shape[1],
                        14 * MIB,
                    )(near, part)[0]
                    for low, near, part in ((0, self.near[k], left), (half, self.near[-k], right))
                ]
        return self

    def finish(self):
        return self.step(self.left_steps).result


class Together:
    def __init__(self, *scatters):
        self.scatters, self.n = scatters, scatters[0].n

    def outgoing(self):
        operands, self.layout = [], []
        for s in self.scatters:
            values, layout = s.operands()
            operands += values
            self.layout.append(layout)
        if len(self.layout) == 1 and self.layout[0][2] is None:
            return operands
        rows = sum(entry[0] for entry in self.layout)
        return call(
            functools.partial(merge_kernel, tuple(self.layout)),
            [((rows, D), BF16)] * 2,
            [VMEM] * len(operands),
            2 * rows * D,
            14 * MIB,
        )(*operands)

    def incoming(self, left, right):
        offset = 0
        for s, (rows, _, _) in zip(self.scatters, self.layout):
            s.take(left, right, offset, rows)
            offset += rows


def region(streams=(), swaps=(), work=None, inputs=()):
    out = [v for s in streams for v in s.outgoing()]
    count = len(out)
    values, inputs = lax.optimization_barrier((out + [s[0] for s in swaps], list(inputs)))
    moved = [
        onward(v, streams[0].n) if i % 2 == 0 else backward(v, streams[0].n)
        for i, v in enumerate(values[:count])
    ]
    moved += [swap(v, s[1], s[2]) for v, s in zip(values[count:], swaps)]
    results = work(*inputs) if work else ()
    moved, results = lax.optimization_barrier((moved, results))
    for i, s in enumerate(streams):
        s.incoming(*moved[2 * i : 2 * i + 2])
    return moved[count:], results


def meet(*streams):
    values = barrier(*[v for s in streams for v in (s.left, s.right)])
    for i, s in enumerate(streams):
        s.left, s.right = values[2 * i : 2 * i + 2]


def swap(values, axis, bit):
    size = lax.axis_size(axis)
    return lax.ppermute(values, axis, [(i, i ^ bit) for i in range(size)])


class Butterfly:
    def __init__(self, values, axis):
        self.left, self.right, self.axis, self.bit = values, jnp.zeros((1, 128), F32), axis, 1

    def step(self):
        if self.bit < lax.axis_size(self.axis):
            self.left = self.left + swap(self.left, self.axis, self.bit)
            self.bit *= 2
        return self

    def finish(self):
        while self.bit < lax.axis_size(self.axis):
            self.step()
        return self.left


def ladder(values, bit=4):
    while bit < lax.axis_size("wide"):
        values = add16(values, swap(values, "wide", bit))
        bit *= 2
    return values


def own_half(core):
    return pl.ds(pl.multiple_of(core[0] * (D // 2), D // 2), D // 2)


def columns_kernel(cuts, lefts, rights, core, *refs):
    sources, outs, refs = refs[:4], refs[4 : 4 + len(cuts)], refs[4 + len(cuts) :]
    left, left_other, right, right_other, semaphores = refs
    width = outs[0].shape[0]
    columns = right.shape[1]
    copies = Copies(semaphores)
    coming = [
        copies.start(sources[1].at[:, pl.ds(lefts[1], left.shape[1])], left_other),
        copies.start(sources[3].at[:, pl.ds(rights[1], columns)], right_other),
        copies.start(sources[0].at[:, pl.ds(lefts[0], left.shape[1])], left),
    ]
    if rights[0] is None:
        coming.append(copies.start(sources[2].at[:, own_half(core)], right))
    else:
        coming.append(copies.start(sources[2].at[:, pl.ds(rights[0], columns)], right))
    coming[0].wait()
    coming[1].wait()
    part = dot(left_other[:, :width], right_other[...], TN)
    coming[2].wait()
    coming[3].wait()
    part += dot(left[:, :width], right[...], TN)
    for out, (low, high) in zip(outs, cuts):
        out[...] = part[:, low:high].astype(BF16)


def own_columns(core, cuts, width, left, left_other, right, right_other, lefts=(0, 0), low=0):
    total = left.shape[0]
    padded = -(-width // 128) * 128
    return call(
        functools.partial(columns_kernel, cuts, lefts, (None, low)),
        [((width, high - low), BF16) for low, high in cuts],
        [SMEM] + [ANY] * 4,
        2 * total * D * width,
        50 * MIB,
        [pltpu.VMEM((total, padded), BF16)] * 2
        + [pltpu.VMEM((total, D // 2), BF16)] * 2
        + [pltpu.SemaphoreType.DMA((4,))],
    )(core.reshape(1), left, left_other, right, right_other)


def rows_kernel(first, core, *refs):
    sources, refs = refs[:4], refs[4:]
    outs, (normed, normed_other, grads, grads_other, semaphores) = refs[:-5], refs[-5:]
    width = outs[0].shape[1]
    columns = pl.ds(first * width, len(outs) * width)
    copies = Copies(semaphores)
    coming = [
        copies.start(sources[1], normed_other),
        copies.start(sources[3].at[:, columns], grads_other),
        copies.start(sources[0].at[:, own_half(core)], normed),
        copies.start(sources[2].at[:, columns], grads),
    ]
    coming[0].wait()
    coming[1].wait()
    part = dot(normed_other[...], grads_other[...], TN)
    coming[2].wait()
    coming[3].wait()
    part += dot(normed[...], grads[...], TN)
    for i, out in enumerate(outs):
        out[...] = part[:, i * width : (i + 1) * width].astype(BF16)


def own_rows(core, first, count, width, normed, normed_other, bundle, bundle_other):
    total = normed.shape[0]
    return call(
        functools.partial(rows_kernel, first),
        [((D // 2, width), BF16)] * count,
        [SMEM] + [ANY] * 4,
        2 * total * D * width * count,
        50 * MIB,
        [pltpu.VMEM((total, D // 2), BF16)] * 2
        + [pltpu.VMEM((total, count * width), BF16)] * 2
        + [pltpu.SemaphoreType.DMA((4,))],
    )(core.reshape(1), normed, normed_other, bundle, bundle_other)


def add_kernel(keep, crossed, out):
    out[...] = (keep[...] + crossed[...].astype(F32)).astype(BF16)


def sum_kernel(*refs):
    out, low = refs[-1], 0
    for i in range(len(refs) // 2):
        width = refs[2 * i].shape[1]
        out[:, low : low + width] = add16(refs[2 * i][...], refs[2 * i + 1][...])
        low += width


def summed(*values):
    rows = values[0].shape[0]
    columns = sum(v.shape[1] for v in values[::2])
    return ladder(
        call(
            sum_kernel,
            [((rows, columns), BF16)],
            [VMEM] * len(values),
            rows * columns,
            14 * MIB,
        )(*values)[0]
    )


def place(core, own, other, row_halves):
    rows, columns = own.shape
    return call(
        functools.partial(place_kernel, row_halves),
        [((2 * rows, columns) if row_halves else (rows, 2 * columns), F32)],
        [SMEM] + [VMEM] * 2,
        rows * columns,
        14 * MIB,
    )(core.reshape(1), own, other)[0]


def place_two(core, own, other):
    rows, columns = own.shape
    return call(
        place_two_kernel,
        [((2 * rows, columns // 2), F32)] * 2,
        [SMEM] + [VMEM] * 2,
        rows * columns,
        14 * MIB,
    )(core.reshape(1), own, other)


def place_two_kernel(core, own, other, *outs):
    rows, columns = own.shape[0], outs[0].shape[1]
    for where, ref in ((core[0], own), (1 - core[0], other)):
        here = pl.ds(pl.multiple_of(where * rows, 128), rows)
        for i, out in enumerate(outs):
            out[here, :] = ref[:, i * columns : (i + 1) * columns].astype(F32)


def place_kernel(row_halves, core, own, other, out):
    rows, columns = own.shape
    for where, ref in ((core[0], own), (1 - core[0], other)):
        if row_halves:
            out[pl.ds(pl.multiple_of(where * rows, 128), rows), :] = ref[...].astype(F32)
        else:
            out[:, pl.ds(pl.multiple_of(where * columns, 128), columns)] = ref[...].astype(F32)


def call(kernel, outs, in_specs, flops, limit, scratch=(), out_specs=None, aliases=None):
    return pl.pallas_call(
        kernel,
        out_shape=[jax.ShapeDtypeStruct(s, d) for s, d in outs],
        in_specs=in_specs,
        out_specs=out_specs or [VMEM] * len(outs),
        scratch_shapes=list(scratch),
        input_output_aliases=aliases or {},
        compiler_params=pltpu.CompilerParams(vmem_limit_bytes=limit),
        cost_estimate=pl.CostEstimate(
            flops=flops, bytes_accessed=2 * flops // 1000, transcendentals=0
        ),
    )


def part_shapes(n, rows):
    return [((rows, D), BF16)] * (n - 1) + [((rows // 2, D), BF16)] * 2


class Copies:
    def __init__(self, semaphores):
        self.semaphores, self.count, self.out = semaphores, 0, []

    def start(self, source, target):
        copy = pltpu.make_async_copy(source, target, self.semaphores.at[self.count])
        self.count += 1
        copy.start()
        return copy

    def write(self, source, target):
        self.out.append(self.start(source, target))

    def drain(self):
        for copy in self.out:
            copy.wait()


def other_half(core):
    return pl.ds(pl.multiple_of((1 - core[0]) * (D // 2), D // 2), D // 2)


def fetch_halves(copies, pieces, target, start_of):
    half = pieces[0].shape[0]
    out = []
    for r, piece in enumerate(pieces):
        at = start_of(r // 2) + r % 2 * half
        out.append(copies.start(piece, target.at[pl.ds(at, half), :]))
    return out


def fetch_pieces(copies, pieces, target, start_of, halved=True):
    rows = pieces[0].shape[0]
    out = []
    for r, piece in enumerate(pieces):
        if halved and r == len(pieces) - 1:
            at = start_of(r - 1) + rows // 2
        else:
            at = start_of(r)
        out.append(copies.start(piece, target.at[pl.ds(at, piece.shape[0]), :]))
    return out


def write_part(copies, buffer, parts, r, halved=True):
    n = len(parts) - halved
    rows = parts[0].shape[0]
    start = r * rows
    if halved and r == n - 1:
        half = rows // 2
        copies.write(buffer.at[pl.ds(start, half), :], parts[n - 1])
        copies.write(buffer.at[pl.ds(start + half, half), :], parts[n])
    else:
        copies.write(buffer.at[pl.ds(start, rows), :], parts[r])


def store_part(parts, r, values):
    n = len(parts) - 1
    if r < n - 1:
        parts[r][...] = values
    else:
        half = values.shape[0] // 2
        parts[n - 1][...] = values[:half]
        parts[n][...] = values[half:]


def assemble(pieces, target, start_of):
    n = len(pieces) - 1
    rows = pieces[0].shape[0]
    half = rows // 2
    for r in range(n - 1):
        target[pl.ds(start_of(r), rows), :] = pieces[r][...]
    start = start_of(n - 1)
    target[pl.ds(start, half), :] = pieces[n - 1][...]
    target[pl.ds(start + half, half), :] = pieces[n][...]


def segment_of(positions, ends):
    return sum((positions >= e).astype(jnp.int32) for e in ends)


def row_ends(lengths):
    first = lengths[0, 0]
    second = first + lengths[0, 1]
    return (first, second, second + lengths[0, 2])


class Block:
    def __init__(self, b, ends):
        start = b * BLOCK
        rows = lax.broadcasted_iota(jnp.int32, (BLOCK, BLOCK), 0)
        columns = lax.broadcasted_iota(jnp.int32, (BLOCK, BLOCK), 1)
        seg_rows = segment_of(rows + start, ends)
        seg_columns = segment_of(columns + start, ends)
        same = seg_rows == seg_columns
        self.mask = jnp.logical_and(same, rows >= columns)
        self.mask_t = jnp.logical_and(same, columns >= rows)
        self.last = segment_of(start + BLOCK - 1, ends)
        self.earlier = segment_of(start - 1, ends) if b > 0 else -1
        wide_rows = lax.broadcasted_iota(jnp.int32, (BLOCK, HEAD_DIM), 0)
        segments = segment_of(wide_rows + start, ends)
        self.from_state = segments == self.earlier
        self.to_state = segments == self.last

    def decay(self, full):
        return jnp.where(self.mask, full, 0.0)

    def keeping(self, rate):
        factor = jnp.exp(jnp.full((HEAD_DIM, HEAD_DIM), -rate * BLOCK, F32))
        return jnp.where(self.last == self.earlier, factor, 0.0)


def full_decay(rate, turned=False):
    rows = lax.broadcasted_iota(jnp.int32, (BLOCK, BLOCK), int(turned))
    columns = lax.broadcasted_iota(jnp.int32, (BLOCK, BLOCK), 1 - int(turned))
    return jnp.exp(-rate * jnp.maximum(rows - columns, 0).astype(F32))


def edge_factors(rate):
    rows = lax.broadcasted_iota(jnp.int32, (BLOCK, HEAD_DIM), 0).astype(F32)
    return jnp.exp(-rate * (rows + 1.0)), jnp.exp(-rate * (BLOCK - 1.0 - rows))


def silu16(values):
    return (values * jax.nn.sigmoid(values)).astype(BF16)


def silu_grad(before):
    sigmoid = jax.nn.sigmoid(before)
    return sigmoid * (1.0 + before * (1.0 - sigmoid))


def entry_kernel(n, heads, order, core, lengths, rates, *refs):
    pieces, refs = refs[: 2 * n], refs[2 * n :]
    weights, mixer, refs = refs[:4], refs[4], refs[5:]
    normed_out, normed_send, proj_out, mixed_out, squares, states_out, refs = *refs[:6], refs[6:]
    parts, refs = refs[: n + 1], refs[n + 1 :]
    normed, weight_in, mixer_in, proj, mixed, pre, states, buffer, semaphores = refs
    copies = Copies(semaphores)
    rows = 2 * pieces[0].shape[0]
    total = n * rows
    width = heads * HEAD_DIM
    coming = fetch_halves(
        copies, pieces, normed, lambda r: pl.multiple_of(order[0, r] * rows, rows)
    )
    for copy in coming:
        copy.wait()
    fetched = [copies.start(w, weight_in.at[i]) for i, w in enumerate(weights)]
    mixer_copy = copies.start(mixer, mixer_in)
    copies.write(normed, normed_out)
    copies.write(normed.at[:, other_half(core)], normed_send)
    for i in range(4):
        fetched[i].wait()
        for b in range(total // BLOCK):
            here = pl.ds(b * BLOCK, BLOCK)
            proj[here, i * width : (i + 1) * width] = dot(normed[here, :], weight_in[i])
    copies.write(proj, proj_out)
    ends = row_ends(lengths)
    fulls = [full_decay(rates[h]) for h in range(heads)]
    edges = [edge_factors(rates[h]) for h in range(heads)]
    state = [jnp.zeros((HEAD_DIM, HEAD_DIM), F32) for _ in range(heads)]
    ones = jnp.ones((8, HEAD_DIM), BF16)
    for b in range(total // BLOCK):
        here = pl.ds(b * BLOCK, BLOCK)
        block = Block(b, ends)
        square = jnp.zeros((8, BLOCK), F32)
        for h in range(heads):
            at = [slice(i * width + h * HEAD_DIM, i * width + (h + 1) * HEAD_DIM) for i in range(4)]
            query, key = silu16(proj[here, at[0]]), silu16(proj[here, at[1]])
            value = proj[here, at[2]].astype(BF16)
            inner, carried = edges[h]
            inner = jnp.where(block.from_state, inner, 0.0)
            carried = jnp.where(block.to_state, carried, 0.0)
            states[b, h] = state[h]
            weight = (dot(query, key, NT) * block.decay(fulls[h])).astype(BF16)
            high, low = split(state[h])
            out = dot(weight, value) + inner * (dot(query, high) + dot(query, low))
            state[h] = block.keeping(rates[h]) * state[h] + dot(
                (key.astype(F32) * carried).astype(BF16), value, TN
            )
            mixed[here, at[0]] = out
            pre[here, at[0]] = (out * proj[here, at[3]]).astype(BF16)
            high, low = split(out * out)
            square += dot(ones, high, NT) + dot(ones, low, NT)
        squares[:, here] = square[0:1]
    copies.write(mixed, mixed_out)
    copies.write(states, states_out)
    mixer_copy.wait()
    for r in reversed(range(0, n, 2)):
        both = jnp.concatenate(
            [pre[pl.ds(pl.multiple_of(order[0, q] * rows, rows), rows), :] for q in (r, r + 1)], 0
        )
        buffer[r * rows : (r + 2) * rows, :] = dot(both, mixer_in[...]).astype(BF16)
        write_part(copies, buffer, parts, r + 1)
        write_part(copies, buffer, parts, r)
    copies.drain()


def column(row):
    return jnp.transpose(jnp.broadcast_to(row, (HEAD_DIM, row.shape[1])))


def exit_kernel(n, heads, order, core, lengths, rates, *refs):
    pieces, refs = refs[: n + 1], refs[n + 1 :]
    weights, mixer_hbm, refs = refs[:4], refs[4], refs[5:]
    proj_hbm, mixed_hbm, states_hbm, inverses, refs = *refs[:4], refs[4:]
    entry_out, send_out, keep_out, refs = *refs[:3], refs[3:]
    parts, refs = refs[:3], refs[3:]
    resid, weight_in, mixer, proj, mixed, states, scaled, entry_g, scaled_g, buffer, send, keep, sems = refs
    copies = Copies(sems)
    rows = pieces[0].shape[0]
    total = n * rows
    width = heads * HEAD_DIM
    mixer_copy = copies.start(mixer_hbm, mixer)
    coming = fetch_pieces(
        copies, pieces, resid, lambda r: pl.multiple_of(order[0, r] * rows, rows)
    )
    mixer_copy.wait()
    for copy in coming:
        copy.wait()
    saved = [
        copies.start(a, b)
        for a, b in ((proj_hbm, proj), (mixed_hbm, mixed), (states_hbm, states))
    ]
    fetched = [
        copies.start(w, weight_in.at[:, i * width : (i + 1) * width]) for i, w in enumerate(weights)
    ]
    for b in range(total // BLOCK):
        here = pl.ds(b * BLOCK, BLOCK)
        scaled_g[here, :] = dot(resid[here, :D], mixer[...], NT)
    for copy in saved:
        copy.wait()
    ends = row_ends(lengths)
    fulls = [full_decay(rates[h]) for h in range(heads)]
    turned = [full_decay(rates[h], True) for h in range(heads)]
    edges = [edge_factors(rates[h]) for h in range(heads)]
    later = [jnp.zeros((HEAD_DIM, HEAD_DIM), F32) for _ in range(heads)]
    for b in reversed(range(total // BLOCK)):
        here = pl.ds(b * BLOCK, BLOCK)
        block = Block(b, ends)
        inverse = column(inverses[:, here])
        coded = resid[here, D : D + 128].astype(F32)
        mean = (coded[:, 0:1] + coded[:, 1:2] + coded[:, 2:3]) * (1.0 / D)
        for h in range(heads):
            at = [slice(i * width + h * HEAD_DIM, i * width + (h + 1) * HEAD_DIM) for i in range(4)]
            query_pre, key_pre = proj[here, at[0]], proj[here, at[1]]
            query, key = silu16(query_pre), silu16(key_pre)
            value = proj[here, at[2]].astype(BF16)
            gate = proj[here, at[3]]
            grad_s = scaled_g[here, at[0]]
            unit = mixed[here, at[0]] * inverse
            scaled[here, at[0]] = (unit * gate).astype(BF16)
            entry_g[here, at[3]] = (grad_s * unit).astype(BF16)
            grad = (inverse * (grad_s * gate - unit * mean)).astype(BF16)
            inner, carried = edges[h]
            inner = jnp.where(block.from_state, inner, 0.0)
            carried = jnp.where(block.to_state, carried, 0.0)
            decay = block.decay(fulls[h])
            decay_t = jnp.where(block.mask_t, turned[h], 0.0)
            weight_t = (dot(key, query, NT) * decay_t).astype(BF16)
            score = (dot(grad, value, NT) * decay).astype(BF16)
            score_t = (dot(value, grad, NT) * decay_t).astype(BF16)
            high, low = split(states[b, h])
            query_g = dot(score, key) + inner * (dot(grad, high, NT) + dot(grad, low, NT))
            high, low = split(later[h])
            key_g = dot(score_t, query) + carried * (dot(value, high, NT) + dot(value, low, NT))
            value_g = dot(weight_t, grad) + carried * (dot(key, high) + dot(key, low))
            later[h] = (
                dot((query.astype(F32) * inner).astype(BF16), grad, TN)
                + block.keeping(rates[h]) * later[h]
            )
            entry_g[here, at[0]] = (query_g * silu_grad(query_pre)).astype(BF16)
            entry_g[here, at[1]] = (key_g * silu_grad(key_pre)).astype(BF16)
            entry_g[here, at[2]] = value_g.astype(BF16)
    copies.write(entry_g, entry_out)
    send[...] = dot(scaled[...], resid[:, other_half(core)], TN).astype(BF16)
    copies.write(send, send_out)
    keep[...] = dot(scaled[...], resid[:, own_half(core)], TN)
    copies.write(keep, keep_out)
    for copy in fetched:
        copy.wait()
    both = jnp.concatenate(
        [
            entry_g[pl.ds(pl.multiple_of(order[0, q] * rows, rows), rows), :]
            for q in (n - 2, n - 1)
        ],
        0,
    )
    buffer[...] = dot(both, weight_in[...], NT).astype(BF16)
    half = rows // 2
    for part, (low, high) in zip(parts, ((0, rows), (rows, rows + half), (rows + half, 2 * rows))):
        copies.write(buffer.at[pl.ds(low, high - low), :], part)
    copies.drain()


def project_kernel(n, order, *refs):
    entry_hbm, weights, refs = refs[0], refs[1:5], refs[5:]
    parts, refs = refs[: n - 2], refs[n - 2 :]
    entry_g, weight_in, buffer, sems = refs
    copies = Copies(sems)
    rows = parts[0].shape[0]
    width = weights[0].shape[1]
    coming = [
        copies.start(w, weight_in.at[:, i * width : (i + 1) * width]) for i, w in enumerate(weights)
    ] + [copies.start(entry_hbm, entry_g)]
    for copy in coming:
        copy.wait()
    for r in reversed(range(0, n - 2, 2)):
        both = jnp.concatenate(
            [entry_g[pl.ds(pl.multiple_of(order[0, q] * rows, rows), rows), :] for q in (r, r + 1)],
            0,
        )
        buffer[r * rows : (r + 2) * rows, :] = dot(both, weight_in[...], NT).astype(BF16)
        for q in (r + 1, r):
            copies.write(buffer.at[pl.ds(q * rows, rows), :], parts[q])
    copies.drain()


def cotangent_kernel(n, core, *refs):
    pieces, down, grad, grad_send, *products = refs[: n + 1], *refs[n + 1 :]
    rows = pieces[0].shape[0]
    assemble(pieces, grad, lambda r: r * rows)
    grad_send[...] = grad[:, other_half(core)]
    for r, out in enumerate(products):
        out[...] = dot(grad[pl.ds(2 * r * rows, 2 * rows), :], down[...], NT)


def hidden_kernel(index, halved, core, *refs):
    count = 2 + halved
    pieces, refs = refs[:count], refs[count:]
    first, second, product_g, refs = *refs[:3], refs[3:]
    refs = refs if index == 0 else refs[4:]
    (normed_out, product_out, second_out, bundle), refs = refs[:4], refs[4:]
    parts, refs = refs[:count], refs[count:]
    normed, product, first_g, second_g, sems = refs
    copies = Copies(sems)
    low = 0
    for piece in pieces:
        normed[low : low + piece.shape[0], :] = piece[...]
        low += piece.shape[0]
    units, padded = first.shape[0], product.shape[1]
    if padded > units:
        for ref in (product, first_g, second_g):
            ref[:, units:] = jnp.zeros((low, padded - units), BF16)
    here = pl.ds(index * low, low)
    copies.write(normed, normed_out.at[here, :])
    copies.write(normed.at[:, other_half(core)], bundle.at[here, pl.ds(padded, D // 2)])
    tokens = normed[...]
    first_act, second_act = dot(tokens, first[...], NT), dot(tokens, second[...], NT)
    product[:, :units] = (first_act * second_act).astype(BF16)
    copies.write(product, product_out.at[here, :])
    grad = product_g[...]
    one, two = (grad * second_act).astype(BF16), (grad * first_act).astype(BF16)
    first_g[:, :units] = one
    copies.write(first_g, bundle.at[here, pl.ds(0, padded)])
    second_g[:, :units] = two
    copies.write(second_g, second_out.at[here, :])
    result = (dot(one, first[...]) + dot(two, second[...])).astype(BF16)
    low = 0
    for part in parts:
        part[...] = result[low : low + part.shape[0]]
        low += part.shape[0]
    copies.drain()


def down_kernel(n, product, down, *parts):
    rows, units = parts[0].shape[0], down.shape[0]
    for r in range(0, n, 2):
        result = dot(product[pl.ds(r * rows, 2 * rows), :units], down[...]).astype(BF16)
        store_part(parts, r, result[:rows])
        store_part(parts, r + 1, result[rows:])


def norm_kernel(tokens, *halves):
    out = normalize(tokens[...].astype(F32)).astype(BF16)
    half = halves[0].shape[0]
    halves[0][...] = out[:half]
    halves[1][...] = out[half:]


def middle_kernel(tokens, near, left, right, inverse, attn, hidden, normed):
    whole = near[...].astype(F32) + left[...].astype(F32) + right[...].astype(F32)
    whole = whole * inverse[...]
    attn[...] = whole
    whole = tokens[...].astype(F32) + whole
    hidden[...] = whole
    normed[...] = normalize(whole).astype(BF16)


def resid_kernel(low, grad, hidden, near, left, right, attn, hidden_g, coded):
    rows = grad.shape[0]
    here = slice(low, low + rows)
    normed_g = near[...].astype(F32) + left[here, :].astype(F32) + right[here, :].astype(F32)
    whole = grad[...].astype(F32) + norm_grad(hidden[...], normed_g)
    hidden_g[...] = whole
    resid = whole.astype(BF16)
    coded[:, :D] = resid
    inner = jnp.sum(resid.astype(F32) * attn[...], axis=1, keepdims=True)
    lane = lax.broadcasted_iota(jnp.int32, (1, 128), 1)
    out = jnp.zeros((rows, 128), F32)
    for i in range(3):
        high = inner.astype(BF16).astype(F32)
        out += jnp.where(lane == i, high, 0.0)
        inner -= high
    coded[:, D:] = out.astype(BF16)


def output_kernel(tokens, attn, ffn, valid_rows, output, sums):
    rows = tokens.shape[0]
    valid = lax.broadcasted_iota(jnp.int32, (rows, 1), 0) < valid_rows[0]
    tokens_wide = tokens[...].astype(F32)
    output[...] = (tokens_wide + attn[...] + ffn[...]).astype(BF16)
    lane = lax.broadcasted_iota(jnp.int32, (1, 128), 1)
    out = jnp.zeros((1, 128), F32)
    for i, values in enumerate((tokens_wide, attn[...], ffn[...])):
        per_row = jnp.sum(values * values, axis=1, keepdims=True)
        whole = jnp.sum(jnp.where(valid, per_row, 0.0), axis=0, keepdims=True)
        out += jnp.where(lane == i, whole, 0.0)
    counted = jnp.clip(valid_rows[0], 0, rows).astype(F32)
    sums[...] = out + jnp.where(lane == 3, counted, 0.0)


def local(
    tokens_in,
    query_weight,
    key_weight,
    value_weight,
    gate_weight,
    mixer_weight,
    first_weight,
    second_weight,
    down_weight,
    doc_lengths,
    head_decay,
    out_grad,
):
    n = lax.axis_size("narrow")
    rows = tokens_in.shape[0]
    total = rows * n
    heads = head_decay.shape[0]
    width = heads * HEAD_DIM
    units = first_weight.shape[1]
    me = lax.axis_index("narrow")
    core = lax.axis_index("wide") % 2
    start_row = me * rows
    order = lax.dynamic_slice(jnp.asarray(order_table(n)), (me, 0), (1, n))
    where = core.reshape(1)
    entry_weights = (query_weight, key_weight, value_weight, gate_weight)
    tokens_wide = tokens_in.astype(F32)
    rates = head_decay

    half_rows = total // 2
    blocks = total // BLOCK
    first_t, second_t = first_weight.T, second_weight.T
    valid_rows = (jnp.sum(doc_lengths[0, : NDOC - 1]) - start_row).reshape(1)

    half_shapes = [((rows // 2, D), BF16)] * 2
    halves = call(norm_kernel, half_shapes, [VMEM], 6 * rows * D, 14 * MIB)(tokens_in)
    pieces = [v for pair in Gather2(halves, n).finish() for v in pair]
    shapes = [
        ((total, D), BF16),
        ((total, D // 2), BF16),
        ((total, 4 * width), F32),
        ((total, width), F32),
        ((1, total), F32),
        ((blocks, heads, HEAD_DIM, HEAD_DIM), F32),
    ] + part_shapes(n, rows)
    *pieces, grad_own = barrier(*pieces, out_grad)
    cotangent = Gather(grad_own, n).step()
    normed, normed_send, proj, mixed, squares, states, *parts = call(
        functools.partial(entry_kernel, n, heads),
        shapes,
        [SMEM] * 4 + [ANY] * (2 * n + 5),
        12 * total * D * width,
        54 * MIB,
        [
            pltpu.VMEM((total, D), BF16),
            pltpu.VMEM((4, D, width), BF16),
            pltpu.VMEM((width, D), BF16),
            pltpu.VMEM((total, 4 * width), F32),
            pltpu.VMEM((total, width), F32),
            pltpu.VMEM((total, width), BF16),
            pltpu.VMEM((blocks, heads, HEAD_DIM, HEAD_DIM), F32),
            pltpu.VMEM((total, D), BF16),
            pltpu.SemaphoreType.DMA((3 * n + 13,)),
        ],
        [VMEM if i == 4 else ANY for i in range(len(shapes))],
    )(order, where, doc_lengths, rates, *pieces, *entry_weights, mixer_weight)
    squares, cotangent.left, cotangent.right, *parts = barrier(
        squares, cotangent.left, cotangent.right, *parts
    )
    scatter = Scatter(parts, n)
    hop = Butterfly(squares, "narrow")
    while cotangent.left_steps:
        scatter.step()
        cotangent.step()
        hop.step()
        meet(scatter, cotangent, hop)
    squares = hop.finish()
    grad_pieces = cotangent.pieces
    inverses = lax.rsqrt(squares / D + EPS)
    inverse_own = lax.dynamic_slice(inverses, (0, start_row), (1, rows)).reshape(rows, 1)
    near, left, right = scatter.finish()
    attn_own, hidden_own, normed_own = call(
        middle_kernel,
        [((rows, D), F32)] * 2 + [((rows, D), BF16)],
        [VMEM] * 5,
        12 * rows * D,
        14 * MIB,
    )(tokens_in, near, left, right, inverse_own)

    padded = -(-units // 128) * 128

    def hidden(index, pieces):
        halved = index == n // 2 - 1
        half_row = rows // 2
        part_rows = [rows, half_row, half_row] if halved else [rows, rows]
        count = len(part_rows)
        outs = call(
            functools.partial(hidden_kernel, index, halved),
            [((total, D), BF16)]
            + [((total, padded), BF16)] * 2
            + [((total, padded + D // 2), BF16)]
            + [((p, D), BF16) for p in part_rows],
            [SMEM] + [VMEM] * (count + 3) + [ANY] * len(whole),
            16 * rows * D * units,
            40 * MIB,
            [pltpu.VMEM((2 * rows, D), BF16)]
            + [pltpu.VMEM((2 * rows, padded), BF16)] * 3
            + [pltpu.SemaphoreType.DMA((5,))],
            [ANY] * 4 + [VMEM] * count,
            {count + 4 + i: i for i in range(len(whole))},
        )(where, *pieces, first_t, second_t, product_g[index], *whole)
        return outs[:4], list(outs[4:])

    normed_own, grad_pieces = lax.optimization_barrier((normed_own, grad_pieces))
    gather = Gather(normed_own, n).step()
    grad_all, grad_send, *product_g = call(
        functools.partial(cotangent_kernel, n),
        [((total, D), BF16), ((total, D // 2), BF16)] + [((2 * rows, units), F32)] * (n // 2),
        [SMEM] + [VMEM] * (n + 2),
        2 * total * D * units,
        22 * MIB,
    )(where, *grad_pieces, down_weight)
    gather.left, gather.right, grad_send, normed_send, product_g = lax.optimization_barrier(
        (gather.left, gather.right, grad_send, normed_send, product_g)
    )
    whole, parts = [], []
    for i in range(n // 2 - 1):
        pieces = gather.pieces[2 * i : 2 * i + 2]
        gather.step()
        whole, new_parts = hidden(i, pieces)
        if i == 0:
            normed_other = swap(normed_send, "wide", 1)
            gather.left, gather.right, normed_other, new_parts = lax.optimization_barrier(
                (gather.left, gather.right, normed_other, new_parts)
            )
        parts += new_parts
    grad_other = swap(grad_send, "wide", 1)
    *pieces, grad_other = barrier(*gather.pieces[n - 2 :], grad_other)
    whole, new_parts = hidden(n // 2 - 1, pieces)
    parts += new_parts
    normed2, product, second_g, bundle = whole

    scatter = Scatter(parts, n)
    stream = Together(scatter)
    half = D // 2
    cut_at = [(0, 384, 896, half), (0, half), (0, 512, half)]
    cuts = [tuple(zip(at[:-1], at[1:])) for at in cut_at]

    (product_other, bundle_other), _ = region(
        [stream], [(product, "wide", 1), (bundle, "wide", 1)]
    )
    (second_other_g,), down_own = region(
        [stream],
        [(second_g, "wide", 1)],
        lambda *v: own_columns(core, cuts[0], units, *v),
        [product, product_other, grad_all, grad_other],
    )
    down_in, first_in, second_in = [], [], []
    (received,), first_own = region(
        [stream],
        [(down_own[0], "wide", 2)],
        lambda *v: own_columns(core, cuts[1], units, *v, v[1], low=padded),
        [bundle, bundle_other, normed2],
    )
    down_in.append(received)
    (received,), second_own = region(
        [stream],
        [(down_own[1], "wide", 2)],
        lambda *v: own_columns(core, cuts[2], units, *v, low=padded),
        [second_g, second_other_g, normed2, bundle_other],
    )
    down_in.append(received)
    while scatter.left_steps:
        region([stream])
    left, right, low, _ = scatter.received
    hidden_g, resid_own = call(
        functools.partial(resid_kernel, low),
        [((rows, D), F32), ((rows, D + 128), BF16)],
        [VMEM] * 6,
        20 * rows * D,
        14 * MIB,
    )(out_grad, hidden_own, scatter.near[0], left, right, attn_own)

    gather = Gather(resid_own, n)

    def mixed_pairs(owns, ins):
        return [v for pair in zip(owns, ins) for v in pair]

    def output_parts(product):
        return call(
            functools.partial(down_kernel, n),
            part_shapes(n, rows),
            [VMEM] * 2,
            2 * total * D * units,
            14 * MIB,
        )(product, down_weight)

    down_own, first_own = list(down_own), list(first_own)
    resid_own, product, down_own[2], first_own[0] = barrier(
        resid_own, product, down_own[2], first_own[0]
    )
    gather = Gather(resid_own, n).step(n // 2 - 1)
    parts = output_parts(product)
    down_in.append(swap(down_own[2], "wide", 2))
    first_in = swap(first_own[0], "wide", 2)
    gather.left, gather.right, parts, down_in[2], first_in = lax.optimization_barrier(
        (gather.left, gather.right, parts, down_in[2], first_in)
    )
    scatter2 = Scatter(parts, n)
    stream2 = Together(scatter2)
    (received,), (first_total, down_total) = region(
        [gather, stream2],
        [(second_own[0], "wide", 2)],
        lambda own, other, *v: (summed(own, other), summed(*v)),
        [first_own[0], first_in, *mixed_pairs(down_own, down_in)],
    )
    second_in.append(received)

    shapes = [
        ((total, 4 * width), BF16),
        ((width, D // 2), BF16),
        ((width, D // 2), F32),
        ((rows, D), BF16),
        ((rows // 2, D), BF16),
        ((rows // 2, D), BF16),
    ]
    leave = call(
        functools.partial(exit_kernel, n, heads),
        shapes,
        [SMEM] * 4 + [ANY] * (n + 9) + [VMEM],
        12 * total * D * width,
        60 * MIB,
        [
            pltpu.VMEM((total, D + 128), BF16),
            pltpu.VMEM((D, 4 * width), BF16),
            pltpu.VMEM((width, D), BF16),
            pltpu.VMEM((total, 4 * width), F32),
            pltpu.VMEM((total, width), F32),
            pltpu.VMEM((blocks, heads, HEAD_DIM, HEAD_DIM), F32),
            pltpu.VMEM((total, width), BF16),
            pltpu.VMEM((total, 4 * width), BF16),
            pltpu.VMEM((total, width), F32),
            pltpu.VMEM((2 * rows, D), BF16),
            pltpu.VMEM((width, D // 2), BF16),
            pltpu.VMEM((width, D // 2), F32),
            pltpu.SemaphoreType.DMA((2 * n + 15,)),
        ],
        [ANY] * len(shapes),
    )
    (received, first_other, down_other), (entry_g, mixer_send, mixer_keep, *parts) = region(
        [stream2],
        [(second_own[1], "wide", 2), (first_total, "wide", 1), (down_total, "wide", 1)],
        lambda inverses, *pieces: leave(
            order,
            where,
            doc_lengths,
            rates,
            *pieces,
            *entry_weights,
            mixer_weight,
            proj,
            mixed,
            states,
            inverses,
        ),
        [inverses, *gather.pieces],
    )
    second_in.append(received)

    far = parts
    scatter = Scatter(part_shapes(n, rows)[: n - 2] + far, n)
    stream = Together(scatter2, scatter)

    def mixer_work(keep, crossed_send, entry_g, normed, normed_other):
        (mixer_own,) = call(
            add_kernel, [(keep.shape, BF16)], [VMEM] * 2, keep.size, 14 * MIB
        )(keep, swap(crossed_send, "wide", 1))
        mixer_in = swap(mixer_own, "wide", 2)
        entry_other = swap(entry_g, "wide", 1)
        parts = call(
            functools.partial(project_kernel, n),
            part_shapes(n, rows)[: n - 2],
            [SMEM] + [ANY] * 5,
            6 * total * D * width,
            48 * MIB,
            [
                pltpu.VMEM((total, 4 * width), BF16),
                pltpu.VMEM((D, 4 * width), BF16),
                pltpu.VMEM((total - 2 * rows, D), BF16),
                pltpu.SemaphoreType.DMA((n + 4,)),
            ],
            [ANY] * (n - 2),
        )(order, entry_g, *entry_weights)
        owns = own_rows(core, 2, 2, width, normed, normed_other, entry_g, entry_other)
        return mixer_own, mixer_in, owns, entry_other, parts

    _, (mixer_own, mixer_in, (value_own, gate_own), entry_other, parts) = region(
        [stream],
        [],
        mixer_work,
        [mixer_keep, mixer_send, entry_g, normed, normed_other],
    )
    scatter.near.update({d: parts[i] for i, d in enumerate(distances(n)[:-2])})

    def entry_work(normed, normed_other, entry_g, entry_other, *values):
        mixer_total = summed(*values[:2])
        mixer_other = swap(mixer_total, "wide", 1)
        owns = own_rows(core, 0, 2, width, normed, normed_other, entry_g, entry_other)
        first_w = place(core, *values[2:4], False)
        down_w = place(core, *values[4:6], False)
        return owns, mixer_total, mixer_other, first_w, down_w, summed(*values[6:])

    (gate_in, value_in), work_out = region(
        [stream],
        [(gate_own, "wide", 2), (value_own, "wide", 2)],
        entry_work,
        [normed, normed_other, entry_g, entry_other, mixer_own, mixer_in]
        + [first_total, first_other, down_total, down_other]
        + mixed_pairs(second_own, second_in),
    )
    (query_own, key_own), mixer_total, mixer_other, first_w, down_w, second_total = work_out
    while scatter2.left_steps:
        region([stream])
    ffn_own = scatter2.result
    stream = Together(scatter)

    def output_work(tokens_in, attn_own, ffn_own, a, b, *pairs):
        output, stats = call(
            output_kernel,
            [((rows, D), BF16), ((1, 128), F32)],
            [VMEM] * 3 + [SMEM],
            6 * rows * D,
            14 * MIB,
        )(tokens_in, attn_own, ffn_own, valid_rows)
        stats = stats + swap(stats, "narrow", 1)
        return output, stats, place(core, a, b, False), summed(*pairs)

    (key_in, second_other), (output, stats, mixer_w, pair_total) = region(
        [stream],
        [(key_own, "wide", 2), (second_total, "wide", 1)],
        output_work,
        [tokens_in, attn_own, ffn_own, mixer_total, mixer_other]
        + [gate_own, gate_in, value_own, value_in],
    )
    (query_in, pair_other, hop), (second_w, key_total) = region(
        [stream],
        [(query_own, "wide", 2), (pair_total, "wide", 1), (stats, "narrow", 2)],
        lambda own, other, *v: (place(core, own, other, False), summed(*v)),
        [second_total, second_other, key_own, key_in],
    )
    stats = stats + hop
    while scatter.left_steps:
        region([stream])
    normed_g = scatter.result

    (key_other, hop), (query_total, (gate_w, value_w)) = region(
        [],
        [(key_total, "wide", 1), (stats, "narrow", 4)],
        lambda a, b, *v: (summed(a, b), place_two(core, *v)),
        [query_own, query_in, pair_total, pair_other],
    )
    stats = stats + hop
    query_other = swap(query_total, "wide", 1)
    for axis, bit in (("narrow", 8), ("wide", 1)):
        while bit < lax.axis_size(axis):
            stats = stats + swap(stats, axis, bit)
            bit *= 2
    input_grad = hidden_g + norm_grad(tokens_wide, normed_g)
    key_w = place(core, key_total, key_other, True)
    query_w = place(core, query_total, query_other, True)
    stream_rms = jnp.sqrt(stats[0, :3] / (stats[0, 3] * D))
    return (
        output,
        input_grad,
        query_w,
        key_w,
        value_w,
        gate_w,
        mixer_w,
        first_w.T,
        second_w.T,
        down_w,
        stream_rms,
    )


def solution(mesh):
    split_tokens = P(("wide", "narrow"), None)
    columns, rows = P(None, "narrow"), P("narrow", None)
    return jax.shard_map(
        local,
        mesh=mesh,
        in_specs=(split_tokens,)
        + (columns,) * 4
        + (rows, columns, columns, rows, P("wide", None), P("narrow"), split_tokens),
        out_specs=(split_tokens,) * 2 + (columns,) * 4 + (rows, columns, columns, rows, P()),
        check_vma=False,
    )
```
